32 devices in a mesh: groups: 2 (over x), box: 16 (over z, y, core).
Axes of the slice: x: 2, y: 2, z: 4, core: 2. Of those that a mesh axis runs over, the one named last changes fastest.
Arguments:
- source_weights: float32 [2, 81, 65536], P(None, None, ('groups', 'box')), parts along dimension 2, may hold values from -2 to 2
- wave_vectors: float32 [4, 2, 65536], P(None, None, ('groups', 'box')), parts along dimension 2, may hold values from -8 to 8
- source_centers: float32 [4, 2, 65536], P(None, None, ('groups', 'box')), parts along dimension 2, may hold values from -1 to 1
- phase_coef: float32 [4, 3], replicated, may hold values from 0.5 to 1.5
- phase_kind: int32 [65536], P(('groups', 'box')), parts along dimension 0, may hold values from 0 to 3
Outputs:
- target_coef: float32 [2, 81, 65536], P(None, None, ('groups', 'box')), parts along dimension 2
The draws below stay inside these ranges and needn't reach their ends.
There are 2 independent parts, one for each index of `groups`. The reference program is written for one: setup_inputs(seed, part) draws one part's arguments, and reference() takes and returns one part's arrays. A program takes and returns all parts, laid end to end along the dimension named above; an argument that names none is the same for every part. Nothing has to cross between parts.
All inputs are finite; a program needn't handle non-finite values.
Results may differ from the reference program's by a relative error of at most 0.0003.
Values sent between devices are 32-bit elements; how exact they have to be, the bound alone decides.
No kernel may reach another device: no remote copies, remote signals or barrier semaphores. Data moves between devices by JAX's collectives and lax.ppermute only.
A program may use at most 64 MiB of HBM per device.

```python
import math
import jax
import jax.numpy as jnp
from jax import lax

CHEB = 9
KINDS = 4
LEVELS = 4
BOX_DEV = 2048
BOXES = 32768
N_BOX = 16


def with_ends(values, key, smallest, high):
    longest = values.shape.index(max(values.shape))
    spots = []
    for shift in (0, 1):
        where = [jax.random.randint(jax.random.fold_in(key, axis), (), 0, length) for axis, length in enumerate(values.shape)]
        where[longest] = (where[longest] + shift) % values.shape[longest]
        spots.append(tuple(where))
    return values.at[spots[0]].set(smallest).at[spots[1]].set(high)


def shard_levels(own_key, dims, cuts, smallest, largest):
    level = 1.0
    for axis_at, blocks in cuts:
        steps = jax.random.uniform(jax.random.fold_in(jax.random.fold_in(own_key, 6), axis_at), (blocks,), jnp.float32, smallest / len(cuts), largest / len(cuts))
        level = level * jnp.repeat(jnp.exp(steps), dims[axis_at] // blocks).reshape((-1,) + (1,) * (len(dims) - 1 - axis_at))
    return level


def scatter_about(key, shape, scale, bound, cuts=(), held_as=jnp.bfloat16):
    array = scale * jax.random.normal(key, shape, jnp.float32)
    if cuts:
        array = array * shard_levels(key, shape, cuts, -0.22, 0.18)
    return jnp.clip(array, -bound, bound).astype(held_as)


def setup_inputs(seed: int = 0, part: int = 0) -> dict:
    splits = jax.random.split(jax.random.key(seed), 6)
    own_keys = jax.random.split(jax.random.fold_in(splits[5], part), 6)
    return {
        "source_weights": scatter_about(own_keys[0], (2, CHEB * CHEB, BOXES), 0.25, 2.0, ((2, 16),), jnp.float32),
        "wave_vectors": jnp.clip(jax.random.uniform(own_keys[1], (LEVELS, 2, BOXES), jnp.float32, -8.0, 8.0) * shard_levels(own_keys[1], (LEVELS, 2, BOXES), ((2, 16),), -0.4, 0.0), -8.0, 8.0),
        "source_centers": jnp.clip(jax.random.uniform(own_keys[2], (LEVELS, 2, BOXES), jnp.float32, -1.0, 1.0) * shard_levels(own_keys[2], (LEVELS, 2, BOXES), ((2, 16),), -0.4, 0.0), -1.0, 1.0),
        "phase_coef": jnp.clip(jax.random.uniform(splits[3], (KINDS, 3), jnp.float32, 0.5, 1.5), 0.5, 1.5),
        "phase_kind": with_ends(jax.random.randint(own_keys[4], (BOXES,), 0, KINDS), jax.random.fold_in(own_keys[4], 1), 0, KINDS - 1).astype(jnp.int32),
    }


def chebyshev_nodes():
    return jnp.cos(math.pi * (2.0 * jnp.arange(CHEB, dtype=jnp.float32) + 1.0) / (2.0 * CHEB))

def lagrange_matrix(targets):
    node_values = chebyshev_nodes()
    row_list = []
    for t_index in range(CHEB):
        factor_product = jnp.ones_like(targets)
        for other_node in range(CHEB):
            if other_node != t_index:
                factor_product = factor_product * (targets - node_values[other_node]) / (node_values[t_index] - node_values[other_node])
        row_list.append(factor_product)
    return jnp.stack(row_list)

def child_matrix(which_child, along_first):
    node_values = chebyshev_nodes()
    one_dim = lagrange_matrix((node_values + 2.0 * which_child - 1.0) / 2.0)
    identity = jnp.eye(CHEB, dtype=jnp.float32)
    if along_first:
        return jnp.kron(one_dim, identity)
    return jnp.kron(identity, one_dim)

def box_phase(first_coord, second_coord, wave_block, center_block, box_coefs, half_size):
    point_one = center_block[0][None, :] + half_size * first_coord[:, None]
    point_two = center_block[1][None, :] + half_size * second_coord[:, None]
    root_term = box_coefs[0] * jnp.sqrt((box_coefs[1] * wave_block[0]) ** 2 + wave_block[1] ** 2 + 1.0)
    return 2.0 * math.pi * (point_one * wave_block[0] + point_two * wave_block[1] + root_term * (1.0 + box_coefs[2] * point_one * point_one))

def combine(child_zero, child_one, wave_block, center_block, box_coefs, level_index):
    node_values = chebyshev_nodes()
    first_coord = jnp.repeat(node_values, CHEB)
    second_coord = jnp.tile(node_values, CHEB)
    half_size = 2.0 ** (level_index - LEVELS)
    along_first = level_index % 2 == 0
    summed = None
    for which_child, values in ((0, child_zero), (1, child_one)):
        shifted = (node_values + 2.0 * which_child - 1.0) / 2.0
        if along_first:
            coord_first = jnp.repeat(shifted, CHEB)
            coord_second = second_coord
        else:
            coord_first = first_coord
            coord_second = jnp.tile(shifted, CHEB)
        phases = box_phase(coord_first, coord_second, wave_block, center_block, box_coefs, half_size)
        cosine = jnp.cos(phases)
        sine_part = jnp.sin(phases)
        real_part = cosine * values[0] + sine_part * values[1]
        imag_part = cosine * values[1] - sine_part * values[0]
        interpolated = jnp.einsum('ts,rsb->rtb', child_matrix(which_child, along_first), jnp.stack([real_part, imag_part]), precision=lax.Precision.HIGHEST)
        summed = interpolated if summed is None else summed + interpolated
    phases = box_phase(first_coord, second_coord, wave_block, center_block, box_coefs, half_size)
    cosine = jnp.cos(phases)
    sine_part = jnp.sin(phases)
    return jnp.stack([cosine * summed[0] - sine_part * summed[1], cosine * summed[1] + sine_part * summed[0]])

def lookup_coefs(phase_kind, phase_coef):
    picked = jnp.zeros((3, phase_kind.shape[-1]), jnp.float32)
    for kind_index in range(KINDS):
        picked = picked + jnp.where(phase_kind == kind_index, 1.0, 0.0)[None, :] * phase_coef[kind_index][:, None]
    return picked

def reference(source_weights, wave_vectors, source_centers, phase_coef, phase_kind):
    box_coefs = lookup_coefs(phase_kind, phase_coef)
    points = CHEB * CHEB
    current = source_weights
    log_local = BOX_DEV.bit_length() - 1
    log_axis = N_BOX.bit_length() - 1
    for level_index in range(LEVELS):
        position = log_local + log_axis - 1 - level_index
        outer_count = BOXES >> position + 1
        inner_count = 1 << position
        split = current.reshape(2, points, outer_count, 2, inner_count)
        child_zero = jnp.broadcast_to(split[:, :, :, 0:1, :], split.shape).reshape(2, points, BOXES)
        child_one = jnp.broadcast_to(split[:, :, :, 1:2, :], split.shape).reshape(2, points, BOXES)
        current = combine(child_zero, child_one, wave_vectors[level_index], source_centers[level_index], box_coefs, level_index)
    group_size = BOX_DEV // N_BOX
    return current.reshape(2, points, N_BOX, N_BOX, group_size).transpose(0, 1, 3, 2, 4).reshape(2, points, BOXES)
```

```python
import math

import numpy as np

import jax
import jax.numpy as jnp
from jax import lax
from jax.experimental import pallas as pl
from jax.experimental.pallas import tpu as pltpu
from jax.sharding import PartitionSpec as P

CHEB = 9
POINTS = CHEB * CHEB
KINDS = 4
LEVELS = 4
SLOTS = 1 << LEVELS
LANES = 128
WEIGHT_ROWS = 2 * POINTS
PHASE_ROWS = 4 * LEVELS
USED_ROWS = WEIGHT_ROWS + PHASE_ROWS
ROWS = (USED_ROWS + 7) // 8 * 8

NODES = np.cos(math.pi * (2.0 * np.arange(CHEB) + 1.0) / (2.0 * CHEB))
NODES[CHEB // 2] = 0.0


def interpolation_halves():
    targets = (NODES - 1.0) / 2.0
    matrix = np.ones((CHEB, CHEB))
    for t in range(CHEB):
        for m in range(CHEB):
            if m != t:
                matrix[t] *= (targets - NODES[m]) / (NODES[t] - NODES[m])
    return (matrix + matrix[::-1]) / 2.0, (matrix - matrix[::-1]) / 2.0


EVEN_HALF, ODD_HALF = interpolation_halves()

SIN_COEFS = (3.1415926401839673, -5.167710090328242, 2.5500776596583643, -0.5982921590176602, 0.0776594073245765)
COS_COEFS = (0.999999953466542, -4.934792858659144, 4.05841191384421, -1.3318801591805476, 0.219696794464285)


def cos_sin_turns(turns):
    rest = turns - jnp.round(turns)
    square = rest * rest
    sine = jnp.float32(SIN_COEFS[-1])
    cosine = jnp.float32(COS_COEFS[-1])
    for s, c in zip(SIN_COEFS[-2::-1], COS_COEFS[-2::-1]):
        sine = sine * square + s
        cosine = cosine * square + c
    sine = sine * rest
    twice = sine + sine
    return 1.0 - twice * sine, twice * cosine


def phase_rows(wave, center, kind, coef_ref):
    a = b = e = jnp.zeros(kind.shape, jnp.float32)
    for index in range(KINDS):
        chosen = kind == index
        a = jnp.where(chosen, coef_ref[index, 0], a)
        b = jnp.where(chosen, coef_ref[index, 1], b)
        e = jnp.where(chosen, coef_ref[index, 2], e)
    k1, k2 = wave
    x1, x2 = center
    level = lax.broadcasted_iota(jnp.int32, k1.shape, 0)
    half = jnp.full(k1.shape, 2.0**-LEVELS, jnp.float32)
    for index in range(1, LEVELS):
        half = jnp.where(level == index, 2.0 ** (index - LEVELS), half)
    scaled = b * k1
    root = a * jnp.sqrt(scaled * scaled + k2 * k2 + 1.0)
    bent = root * e
    constant = x1 * k1 + x2 * k2 + root + bent * x1 * x1
    constant = constant - jnp.round(constant)
    return constant, half * (k1 + 2.0 * bent * x1), half * half * bent, half * k2


def pack_kernel(me_ref, coef_ref, weights_ref, wave_ref, center_ref, kind_ref, *refs):
    outs, phases_ref = refs[:-1], refs[-1]
    rows = phase_rows(
        (wave_ref[:, 0, :], wave_ref[:, 1, :]), (center_ref[:, 0, :], center_ref[:, 1, :]), kind_ref[...], coef_ref
    )
    for index, values in enumerate(rows):
        phases_ref[index * LEVELS : (index + 1) * LEVELS, :] = values
    width = outs[0].shape[-1]
    for step, out in enumerate(outs):
        columns = pl.ds(pl.multiple_of((me_ref[0] ^ step) * width, width), width)
        out[:POINTS, :] = weights_ref[0, :, columns]
        out[POINTS:WEIGHT_ROWS, :] = weights_ref[1, :, columns]
        out[WEIGHT_ROWS:USED_ROWS, :] = phases_ref[:, columns]
        out[USED_ROWS:, :] = jnp.zeros((ROWS - USED_ROWS, width), jnp.float32)


def pack(me, phase_coef, weights, wave, center, kind):
    block = jax.ShapeDtypeStruct((ROWS, LANES), jnp.float32)
    vmem = pl.BlockSpec(memory_space=pltpu.VMEM)
    smem = pl.BlockSpec(memory_space=pltpu.SMEM)
    return pl.pallas_call(
        pack_kernel,
        out_shape=[block] * SLOTS,
        in_specs=[smem, smem, vmem, vmem, vmem, vmem],
        out_specs=[vmem] * SLOTS,
        scratch_shapes=[pltpu.VMEM((PHASE_ROWS, weights.shape[-1]), jnp.float32)],
        compiler_params=pltpu.CompilerParams(vmem_limit_bytes=32 * 2**20),
        name="pack",
    )(me, phase_coef, weights, wave, center, kind)


def level_factors(level, tile, phase_of, parent_ref, child_ref, common_ref):
    constant, linear, quadratic, other = (phase_of(level, part, tile) for part in range(4))
    if level % 2 == 0:
        split = lambda x: constant + x * (linear + x * quadratic)
        common = lambda x: x * other
    else:
        split = lambda x: constant + x * other
        common = lambda x: x * (linear + x * quadratic)
    for t in range(CHEB):
        node = float(NODES[t])
        parent_ref[tile, t, 0], parent_ref[tile, t, 1] = cos_sin_turns(split(node))
        for child in range(2):
            shifted = (node + 2.0 * child - 1.0) / 2.0
            child_ref[tile, child, t, 0], child_ref[tile, child, t, 1] = cos_sin_turns(split(shifted))
        cosine, sine = cos_sin_turns(common(node))
        common_ref[tile, t] = cosine * cosine + sine * sine


def level_column(tile, column, children, parent_ref, child_ref, common_ref, store):
    scaled = []
    for child in range(2):
        line = []
        for s in range(CHEB):
            real, imag = children[child][s]
            cosine, sine = child_ref[tile, child, s, 0], child_ref[tile, child, s, 1]
            line.append((cosine * real + sine * imag, cosine * imag - sine * real))
        scaled.append(line)
    halves = []
    for part in range(2):
        plus = [scaled[0][s][part] + scaled[1][CHEB - 1 - s][part] for s in range(CHEB)]
        minus = [scaled[0][s][part] - scaled[1][CHEB - 1 - s][part] for s in range(CHEB)]
        halves.append((plus, minus))
    common = common_ref[tile, column]
    mid = CHEB // 2
    for t in range(mid + 1):
        sums = []
        for part in range(2):
            plus, minus = halves[part]
            even = plus[0] * float(EVEN_HALF[t, 0])
            for s in range(1, CHEB):
                even = even + plus[s] * float(EVEN_HALF[t, s])
            if t == mid:
                sums.append((even,))
                continue
            odd = minus[0] * float(ODD_HALF[t, 0])
            for s in range(1, CHEB):
                odd = odd + minus[s] * float(ODD_HALF[t, s])
            sums.append((even + odd, even - odd))
        for which, row in enumerate((t,) if t == mid else (t, CHEB - 1 - t)):
            real, imag = sums[0][which] * common, sums[1][which] * common
            cosine, sine = parent_ref[tile, row, 0], parent_ref[tile, row, 1]
            store(row, cosine * real - sine * imag, cosine * imag + sine * real)


def combine_kernel(me_ref, *refs):
    blocks = refs[:SLOTS]
    out_ref, held, work, parent_ref, child_ref, common_ref, sems = refs[SLOTS:]
    me = me_ref[0]
    copies = []
    for step in range(SLOTS):
        spot = pl.ds(pl.multiple_of((me ^ step) * ROWS, 8), ROWS)
        copies.append(pltpu.make_async_copy(blocks[step], held.at[spot, :], sems.at[step]))
        copies[-1].start()
    for copy in copies:
        copy.wait()

    def received(row, tile):
        return held[pl.ds(tile * 8 * ROWS + row, 8, stride=ROWS), :]

    def phase_of(level, part, tile):
        return received(WEIGHT_ROWS + part * LEVELS + level, tile)

    for level in range(LEVELS):
        for tile in range(2):
            level_factors(level, tile, phase_of, parent_ref, child_ref, common_ref)
        bit = 1 << (LEVELS - 1 - level)
        along_first = level % 2 == 0

        def row_of(split, column, part, along_first=along_first):
            return part * POINTS + (split * CHEB + column if along_first else column * CHEB + split)

        def column_step(column, _, level=level, bit=bit, row_of=row_of):
            if level == 0:
                children = [
                    [tuple(received(row_of(s, column, part), child) for part in range(2)) for s in range(CHEB)]
                    for child in range(2)
                ]
            for tile in range(2):
                if level > 0:
                    upper = (lax.broadcasted_iota(jnp.int32, (8, LANES), 0) & bit) != 0
                    children = [[], []]
                    for s in range(CHEB):
                        pairs = [[], []]
                        for part in range(2):
                            value = work[row_of(s, column, part), tile]
                            down = pltpu.roll(value, bit, 0)
                            up = down if bit == 4 else pltpu.roll(value, 8 - bit, 0)
                            pairs[0].append(jnp.where(upper, down, value))
                            pairs[1].append(jnp.where(upper, value, up))
                        children[0].append(tuple(pairs[0]))
                        children[1].append(tuple(pairs[1]))

                def store(row, real, imag, tile=tile):
                    work[row_of(row, column, 0), tile] = real
                    work[row_of(row, column, 1), tile] = imag

                level_column(tile, column, children, parent_ref, child_ref, common_ref, store)
            return 0

        lax.fori_loop(0, CHEB, column_step, 0)

    for box in range(SLOTS):
        for part in range(2):
            out_ref[part, :, box * LANES : (box + 1) * LANES] = work[
                part * POINTS : (part + 1) * POINTS, box // 8, box % 8, :
            ]


def combine(me, blocks):
    hbm = pl.BlockSpec(memory_space=pl.ANY)
    vmem = pl.BlockSpec(memory_space=pltpu.VMEM)
    smem = pl.BlockSpec(memory_space=pltpu.SMEM)
    return pl.pallas_call(
        combine_kernel,
        out_shape=jax.ShapeDtypeStruct((2, POINTS, SLOTS * LANES), jnp.float32),
        in_specs=[smem] + [hbm] * SLOTS,
        out_specs=vmem,
        scratch_shapes=[
            pltpu.VMEM((SLOTS * ROWS, LANES), jnp.float32),
            pltpu.VMEM((WEIGHT_ROWS, 2, 8, LANES), jnp.float32),
            pltpu.VMEM((2, CHEB, 2, 8, LANES), jnp.float32),
            pltpu.VMEM((2, 2, CHEB, 2, 8, LANES), jnp.float32),
            pltpu.VMEM((2, CHEB, 8, LANES), jnp.float32),
            pltpu.SemaphoreType.DMA((SLOTS,)),
        ],
        compiler_params=pltpu.CompilerParams(vmem_limit_bytes=32 * 2**20),
        name="combine",
    )(me, *blocks)


def on_device(source_weights, wave_vectors, source_centers, phase_coef, phase_kind):
    devices = lax.axis_size("box")
    me = lax.axis_index("box").astype(jnp.int32)[None]
    kind = phase_kind[None, :]
    if devices == SLOTS:
        blocks = pack(me, phase_coef, source_weights, wave_vectors, source_centers, kind)
        moved = [blocks[0]] + [None] * (SLOTS - 1)
        for step in range(SLOTS - 1, 0, -1):
            moved[step] = lax.ppermute(blocks[step], "box", [(s, s ^ step) for s in range(SLOTS)])
        return combine(me, moved)
    zero = jnp.zeros_like(me)
    blocks = pack(zero, phase_coef, source_weights, wave_vectors, source_centers, kind)
    whole = jnp.concatenate(blocks, axis=1)
    whole = lax.all_to_all(whole, "box", split_axis=1, concat_axis=1, tiled=True)
    return combine(zero, [whole[:, s * LANES : (s + 1) * LANES] for s in range(SLOTS)])


def solution(mesh):
    in_specs = (
        P(None, None, ("groups", "box")),
        P(None, None, ("groups", "box")),
        P(None, None, ("groups", "box")),
        P(),
        P(("groups", "box")),
    )
    out_specs = P(None, None, ("groups", "box"))
    return jax.shard_map(on_device, mesh=mesh, in_specs=in_specs, out_specs=out_specs, check_vma=False)
```

```python
import math

import numpy as np

import jax
import jax.numpy as jnp
from jax import lax
from jax.experimental import pallas as pl
from jax.experimental.pallas import tpu as pltpu
from jax.sharding import PartitionSpec as P

CHEB = 9
POINTS = CHEB * CHEB
KINDS = 4
LEVELS = 4
SLOTS = 1 << LEVELS
LANES = 128
WEIGHT_ROWS = 2 * POINTS
PHASE_ROWS = 4 * LEVELS
USED_ROWS = WEIGHT_ROWS + PHASE_ROWS
ROWS = (USED_ROWS + 7) // 8 * 8
ORDER = (8, 1, 9, 2, 10, 3, 11, 4, 12, 5, 13, 6, 14, 7, 15, 0)

NODES = np.cos(math.pi * (2.0 * np.arange(CHEB) + 1.0) / (2.0 * CHEB))
NODES[CHEB // 2] = 0.0


def interpolation_halves():
    targets = (NODES - 1.0) / 2.0
    matrix = np.ones((CHEB, CHEB))
    for t in range(CHEB):
        for m in range(CHEB):
            if m != t:
                matrix[t] *= (targets - NODES[m]) / (NODES[t] - NODES[m])
    return (matrix + matrix[::-1]) / 2.0, (matrix - matrix[::-1]) / 2.0


EVEN_HALF, ODD_HALF = interpolation_halves()

SIN_COEFS = (3.1415926401839673, -5.167710090328242, 2.5500776596583643, -0.5982921590176602, 0.0776594073245765)
COS_COEFS = (0.999999953466542, -4.934792858659144, 4.05841191384421, -1.3318801591805476, 0.219696794464285)


def cos_sin_turns(turns):
    rest = turns - jnp.round(turns)
    square = rest * rest
    sine = jnp.float32(SIN_COEFS[-1])
    cosine = jnp.float32(COS_COEFS[-1])
    for s, c in zip(SIN_COEFS[-2::-1], COS_COEFS[-2::-1]):
        sine = sine * square + s
        cosine = cosine * square + c
    sine = sine * rest
    twice = sine + sine
    return 1.0 - twice * sine, twice * cosine


def phase_rows(wave, center, kind, coef_ref):
    a = b = e = jnp.zeros(kind.shape, jnp.float32)
    for index in range(KINDS):
        chosen = kind == index
        a = jnp.where(chosen, coef_ref[index, 0], a)
        b = jnp.where(chosen, coef_ref[index, 1], b)
        e = jnp.where(chosen, coef_ref[index, 2], e)
    k1, k2 = wave
    x1, x2 = center
    level = lax.broadcasted_iota(jnp.int32, k1.shape, 0)
    half = jnp.full(k1.shape, 2.0**-LEVELS, jnp.float32)
    for index in range(1, LEVELS):
        half = jnp.where(level == index, 2.0 ** (index - LEVELS), half)
    scaled = b * k1
    root = a * jnp.sqrt(scaled * scaled + k2 * k2 + 1.0)
    bent = root * e
    constant = x1 * k1 + x2 * k2 + root + bent * x1 * x1
    constant = constant - jnp.round(constant)
    return constant, half * (k1 + 2.0 * bent * x1), half * half * bent, half * k2


def pack_kernel(me_ref, coef_ref, weights_ref, wave_ref, center_ref, kind_ref, *refs):
    outs, phases_ref = refs[:-1], refs[-1]
    rows = phase_rows(
        (wave_ref[:, 0, :], wave_ref[:, 1, :]), (center_ref[:, 0, :], center_ref[:, 1, :]), kind_ref[...], coef_ref
    )
    for index, values in enumerate(rows):
        phases_ref[index * LEVELS : (index + 1) * LEVELS, :] = values
    width = outs[0].shape[-1]
    for step, out in zip(ORDER, outs):
        slot = me_ref[0] ^ step
        columns = pl.ds(pl.multiple_of(slot * width, width), width)
        for part in range(2):
            out[part * POINTS : (part + 1) * POINTS, :] = weights_ref[
                pl.ds(2 * slot + part, POINTS, stride=2 * SLOTS), :
            ]
        out[WEIGHT_ROWS:USED_ROWS, :] = phases_ref[:, columns]
        out[USED_ROWS:, :] = jnp.zeros((ROWS - USED_ROWS, width), jnp.float32)


def pack(me, phase_coef, weights, wave, center, kind):
    block = jax.ShapeDtypeStruct((ROWS, LANES), jnp.float32)
    vmem = pl.BlockSpec(memory_space=pltpu.VMEM)
    smem = pl.BlockSpec(memory_space=pltpu.SMEM)
    return pl.pallas_call(
        pack_kernel,
        out_shape=[block] * SLOTS,
        in_specs=[smem, smem, vmem, vmem, vmem, vmem],
        out_specs=[vmem] * SLOTS,
        scratch_shapes=[pltpu.VMEM((PHASE_ROWS, kind.shape[-1]), jnp.float32)],
        compiler_params=pltpu.CompilerParams(vmem_limit_bytes=32 * 2**20),
        name="pack",
    )(me, phase_coef, weights, wave, center, kind)


def level_factors(level, tile, phase_of, parent_ref, child_ref, common_ref):
    constant, linear, quadratic, other = (phase_of(level, part, tile) for part in range(4))
    if level % 2 == 0:
        split = lambda x: constant + x * (linear + x * quadratic)
        common = lambda x: x * other
    else:
        split = lambda x: constant + x * other
        common = lambda x: x * (linear + x * quadratic)
    for t in range(CHEB):
        node = float(NODES[t])
        parent_ref[tile, t, 0], parent_ref[tile, t, 1] = cos_sin_turns(split(node))
        for child in range(2):
            shifted = (node + 2.0 * child - 1.0) / 2.0
            child_ref[tile, child, t, 0], child_ref[tile, child, t, 1] = cos_sin_turns(split(shifted))
        cosine, sine = cos_sin_turns(common(node))
        common_ref[tile, t] = cosine * cosine + sine * sine


def level_column(tile, column, children, parent_ref, child_ref, common_ref, store):
    scaled = []
    for child in range(2):
        line = []
        for s in range(CHEB):
            real, imag = children[child][s]
            cosine, sine = child_ref[tile, child, s, 0], child_ref[tile, child, s, 1]
            line.append((cosine * real + sine * imag, cosine * imag - sine * real))
        scaled.append(line)
    halves = []
    for part in range(2):
        plus = [scaled[0][s][part] + scaled[1][CHEB - 1 - s][part] for s in range(CHEB)]
        minus = [scaled[0][s][part] - scaled[1][CHEB - 1 - s][part] for s in range(CHEB)]
        halves.append((plus, minus))
    common = common_ref[tile, column]
    mid = CHEB // 2
    for t in range(mid + 1):
        sums = []
        for part in range(2):
            plus, minus = halves[part]
            even = plus[0] * float(EVEN_HALF[t, 0])
            for s in range(1, CHEB):
                even = even + plus[s] * float(EVEN_HALF[t, s])
            if t == mid:
                sums.append((even,))
                continue
            odd = minus[0] * float(ODD_HALF[t, 0])
            for s in range(1, CHEB):
                odd = odd + minus[s] * float(ODD_HALF[t, s])
            sums.append((even + odd, even - odd))
        for which, row in enumerate((t,) if t == mid else (t, CHEB - 1 - t)):
            real, imag = sums[0][which] * common, sums[1][which] * common
            cosine, sine = parent_ref[tile, row, 0], parent_ref[tile, row, 1]
            store(row, cosine * real - sine * imag, cosine * imag + sine * real)


def combine_kernel(me_ref, *refs):
    blocks = refs[:SLOTS]
    out_ref, held, work, parent_ref, child_ref, common_ref, sems = refs[SLOTS:]
    me = me_ref[0]
    copies = []
    for index, step in enumerate(ORDER):
        spot = pl.ds(pl.multiple_of((me ^ step) * ROWS, 8), ROWS)
        copies.append(pltpu.make_async_copy(blocks[index], held.at[spot, :], sems.at[index]))
        copies[-1].start()
    for copy in copies:
        copy.wait()

    def received(row, tile):
        return held[pl.ds(tile * 8 * ROWS + row, 8, stride=ROWS), :]

    def phase_of(level, part, tile):
        return received(WEIGHT_ROWS + part * LEVELS + level, tile)

    for level in range(LEVELS):
        for tile in range(2):
            level_factors(level, tile, phase_of, parent_ref, child_ref, common_ref)
        bit = 1 << (LEVELS - 1 - level)
        along_first = level % 2 == 0

        def row_of(split, column, part, along_first=along_first):
            return part * POINTS + (split * CHEB + column if along_first else column * CHEB + split)

        def column_step(column, _, level=level, bit=bit, row_of=row_of):
            if level == 0:
                children = [
                    [tuple(received(row_of(s, column, part), child) for part in range(2)) for s in range(CHEB)]
                    for child in range(2)
                ]
            for tile in range(2):
                if level > 0:
                    upper = (lax.broadcasted_iota(jnp.int32, (8, LANES), 0) & bit) != 0
                    children = [[], []]
                    for s in range(CHEB):
                        pairs = [[], []]
                        for part in range(2):
                            value = work[row_of(s, column, part), tile]
                            down = pltpu.roll(value, bit, 0)
                            up = down if bit == 4 else pltpu.roll(value, 8 - bit, 0)
                            pairs[0].append(jnp.where(upper, down, value))
                            pairs[1].append(jnp.where(upper, value, up))
                        children[0].append(tuple(pairs[0]))
                        children[1].append(tuple(pairs[1]))

                def store(row, real, imag, tile=tile):
                    for part, value in enumerate((real, imag)):
                        index = row_of(row, column, part)
                        if level < LEVELS - 1:
                            work[index, tile] = value
                        else:
                            start = (index - part * POINTS) * 2 * SLOTS + tile * 16 + part
                            out_ref[pl.ds(start, 8, stride=2), :] = value

                level_column(tile, column, children, parent_ref, child_ref, common_ref, store)
            return 0

        lax.fori_loop(0, CHEB, column_step, 0)


def combine(me, blocks):
    hbm = pl.BlockSpec(memory_space=pl.ANY)
    vmem = pl.BlockSpec(memory_space=pltpu.VMEM)
    smem = pl.BlockSpec(memory_space=pltpu.SMEM)
    return pl.pallas_call(
        combine_kernel,
        out_shape=jax.ShapeDtypeStruct((WEIGHT_ROWS * SLOTS, LANES), jnp.float32),
        in_specs=[smem] + [hbm] * SLOTS,
        out_specs=vmem,
        scratch_shapes=[
            pltpu.VMEM((SLOTS * ROWS, LANES), jnp.float32),
            pltpu.VMEM((WEIGHT_ROWS, 2, 8, LANES), jnp.float32),
            pltpu.VMEM((2, CHEB, 2, 8, LANES), jnp.float32),
            pltpu.VMEM((2, 2, CHEB, 2, 8, LANES), jnp.float32),
            pltpu.VMEM((2, CHEB, 8, LANES), jnp.float32),
            pltpu.SemaphoreType.DMA((SLOTS,)),
        ],
        compiler_params=pltpu.CompilerParams(vmem_limit_bytes=32 * 2**20),
        name="combine",
    )(me, *blocks)


def to_rows(weights):
    return weights.reshape(2, POINTS, SLOTS, LANES).transpose(1, 2, 0, 3).reshape(WEIGHT_ROWS * SLOTS, LANES)


def from_rows(rows):
    return rows.reshape(POINTS, SLOTS, 2, LANES).transpose(2, 0, 1, 3).reshape(2, POINTS, SLOTS * LANES)


def on_device(source_weights, wave_vectors, source_centers, phase_coef, phase_kind):
    devices = lax.axis_size("box")
    me = lax.axis_index("box").astype(jnp.int32)[None]
    direct = devices == SLOTS
    if not direct:
        me = jnp.zeros_like(me)
    blocks = pack(
        me, phase_coef, to_rows(source_weights), wave_vectors, source_centers, phase_kind[None, :]
    )
    if direct:
        blocks = [
            lax.ppermute(block, "box", [(s, s ^ step) for s in range(SLOTS)]) if step else block
            for step, block in zip(ORDER, blocks)
        ]
    else:
        whole = jnp.concatenate([blocks[ORDER.index(s)] for s in range(SLOTS)], axis=1)
        whole = lax.all_to_all(whole, "box", split_axis=1, concat_axis=1, tiled=True)
        blocks = [whole[:, s * LANES : (s + 1) * LANES] for s in ORDER]
    return from_rows(combine(me, blocks))


def solution(mesh):
    in_specs = (
        P(None, None, ("groups", "box")),
        P(None, None, ("groups", "box")),
        P(None, None, ("groups", "box")),
        P(),
        P(("groups", "box")),
    )
    out_specs = P(None, None, ("groups", "box"))
    return jax.shard_map(on_device, mesh=mesh, in_specs=in_specs, out_specs=out_specs, check_vma=False)
```

```python
import functools
import math

import numpy as np

import jax
import jax.numpy as jnp
from jax import lax
from jax.experimental import pallas as pl
from jax.experimental.pallas import tpu as pltpu
from jax.sharding import PartitionSpec as P

CHEB = 9
POINTS = CHEB * CHEB
KINDS = 4
LEVELS = 4
SLOTS = 1 << LEVELS
LANES = 128
WEIGHT_ROWS = 2 * POINTS
PHASE_ROWS = 4 * LEVELS
USED_ROWS = WEIGHT_ROWS + PHASE_ROWS
ROWS = (USED_ROWS + 7) // 8 * 8
OCT = SLOTS // 2
EVEN_ORDER = (8, 10, 2, 12, 4, 14, 6, 0)
ODD_ORDER = (9, 11, 3, 13, 5, 15, 7, 1)

NODES = np.cos(math.pi * (2.0 * np.arange(CHEB) + 1.0) / (2.0 * CHEB))
NODES[CHEB // 2] = 0.0


def interpolation_halves():
    targets = (NODES - 1.0) / 2.0
    matrix = np.ones((CHEB, CHEB))
    for t in range(CHEB):
        for m in range(CHEB):
            if m != t:
                matrix[t] *= (targets - NODES[m]) / (NODES[t] - NODES[m])
    return (matrix + matrix[::-1]) / 2.0, (matrix - matrix[::-1]) / 2.0


EVEN_HALF, ODD_HALF = interpolation_halves()

SIN_COEFS = (3.1415926401839673, -5.167710090328242, 2.5500776596583643, -0.5982921590176602, 0.0776594073245765)
COS_COEFS = (0.999999953466542, -4.934792858659144, 4.05841191384421, -1.3318801591805476, 0.219696794464285)


def cos_sin_turns(turns):
    rest = turns - jnp.round(turns)
    square = rest * rest
    sine = jnp.float32(SIN_COEFS[-1])
    cosine = jnp.float32(COS_COEFS[-1])
    for s, c in zip(SIN_COEFS[-2::-1], COS_COEFS[-2::-1]):
        sine = sine * square + s
        cosine = cosine * square + c
    sine = sine * rest
    twice = sine + sine
    return 1.0 - twice * sine, twice * cosine


def phase_rows(wave, center, kind, coef_ref):
    a = b = e = jnp.zeros(kind.shape, jnp.float32)
    for index in range(KINDS):
        chosen = kind == index
        a = jnp.where(chosen, coef_ref[index, 0], a)
        b = jnp.where(chosen, coef_ref[index, 1], b)
        e = jnp.where(chosen, coef_ref[index, 2], e)
    k1, k2 = wave
    x1, x2 = center
    level = lax.broadcasted_iota(jnp.int32, k1.shape, 0)
    half = jnp.full(k1.shape, 2.0**-LEVELS, jnp.float32)
    for index in range(1, LEVELS):
        half = jnp.where(level == index, 2.0 ** (index - LEVELS), half)
    scaled = b * k1
    root = a * jnp.sqrt(scaled * scaled + k2 * k2 + 1.0)
    bent = root * e
    constant = x1 * k1 + x2 * k2 + root + bent * x1 * x1
    constant = constant - jnp.round(constant)
    return constant, half * (k1 + 2.0 * bent * x1), half * half * bent, half * k2


def pack_kernel(far, me_ref, coef_hbm, weights_hbm, wave_hbm, center_hbm, kind_hbm, *refs):
    outs = refs[:OCT]
    coef_ref, wave_ref, center_ref, kind_ref, phases_ref, sems, block_sems = refs[OCT:]
    me = me_ref[0]
    first = ((me // OCT) ^ far) * OCT
    columns = pl.ds(pl.multiple_of(first * LANES, OCT * LANES), OCT * LANES)
    small = [
        pltpu.make_async_copy(coef_hbm, coef_ref, sems.at[0]),
        pltpu.make_async_copy(wave_hbm.at[:, :, columns], wave_ref, sems.at[1]),
        pltpu.make_async_copy(center_hbm.at[:, :, columns], center_ref, sems.at[2]),
        pltpu.make_async_copy(kind_hbm.at[:, columns], kind_ref, sems.at[3]),
    ]
    large = [
        pltpu.make_async_copy(
            weights_hbm.at[:, first + ((me % OCT) ^ step)], outs[step].at[pl.ds(0, POINTS)], block_sems.at[step]
        )
        for step in range(OCT)
    ]
    for copy in small + large:
        copy.start()
    for copy in small:
        copy.wait()
    rows = phase_rows(
        (wave_ref[:, 0, :], wave_ref[:, 1, :]), (center_ref[:, 0, :], center_ref[:, 1, :]), kind_ref[...], coef_ref
    )
    for index, values in enumerate(rows):
        for level in range(LEVELS):
            row = index * LEVELS + level
            phases_ref[row // 2, row % 2, :] = values[level]
    for step, out in enumerate(outs):
        mine = pl.ds(pl.multiple_of(((me % OCT) ^ step) * LANES, LANES), LANES)
        out[POINTS : USED_ROWS // 2] = phases_ref[:, :, mine]
        out[USED_ROWS // 2 :] = jnp.zeros(((ROWS - USED_ROWS) // 2, 2, LANES), jnp.float32)
    for copy in large:
        copy.wait()


def pack(far, me, phase_coef, weights, wave, center, kind):
    block = jax.ShapeDtypeStruct((ROWS // 2, 2, LANES), jnp.float32)
    vmem = pl.BlockSpec(memory_space=pltpu.VMEM)
    hbm = pl.BlockSpec(memory_space=pltpu.HBM)
    blocks = pl.pallas_call(
        functools.partial(pack_kernel, far),
        out_shape=[block] * OCT,
        in_specs=[pl.BlockSpec(memory_space=pltpu.SMEM)] + [hbm] * 5,
        out_specs=[vmem] * OCT,
        scratch_shapes=[
            pltpu.SMEM(phase_coef.shape, jnp.float32),
            pltpu.VMEM((LEVELS, 2, OCT * LANES), jnp.float32),
            pltpu.VMEM((LEVELS, 2, OCT * LANES), jnp.float32),
            pltpu.VMEM((1, OCT * LANES), jnp.int32),
            pltpu.VMEM((PHASE_ROWS // 2, 2, OCT * LANES), jnp.float32),
            pltpu.SemaphoreType.DMA((4,)),
            pltpu.SemaphoreType.DMA((OCT,)),
        ],
        compiler_params=pltpu.CompilerParams(vmem_limit_bytes=16 * 2**20),
        cost_estimate=pl.CostEstimate(flops=2**20, bytes_accessed=2 * 2**20, transcendentals=0),
        name="pack_far" if far else "pack_near",
    )(me, phase_coef, weights, wave, center, kind)
    return [block.reshape(ROWS, LANES) for block in blocks]


def level_factors(level, phases, parent_ref, child_ref, common_ref):
    constant, linear, quadratic, other = phases
    if level % 2 == 0:
        split = lambda x: constant + x * (linear + x * quadratic)
        common = lambda x: x * other
    else:
        split = lambda x: constant + x * other
        common = lambda x: x * (linear + x * quadratic)
    for t in range(CHEB):
        node = float(NODES[t])
        parent_ref[t, 0], parent_ref[t, 1] = cos_sin_turns(split(node))
        for child in range(2):
            shifted = (node + 2.0 * child - 1.0) / 2.0
            child_ref[child, t, 0], child_ref[child, t, 1] = cos_sin_turns(split(shifted))
        cosine, sine = cos_sin_turns(common(node))
        common_ref[t] = cosine * cosine + sine * sine


def level_column(column, children, parent_ref, child_ref, common_ref, store):
    scaled = []
    for child in range(2):
        line = []
        for s in range(CHEB):
            real, imag = children[child][s]
            cosine, sine = child_ref[child, s, 0], child_ref[child, s, 1]
            line.append((cosine * real + sine * imag, cosine * imag - sine * real))
        scaled.append(line)
    halves = []
    for part in range(2):
        plus = [scaled[0][s][part] + scaled[1][CHEB - 1 - s][part] for s in range(CHEB)]
        minus = [scaled[0][s][part] - scaled[1][CHEB - 1 - s][part] for s in range(CHEB)]
        halves.append((plus, minus))
    common = common_ref[column]
    mid = CHEB // 2
    for t in range(mid + 1):
        sums = []
        for part in range(2):
            plus, minus = halves[part]
            even = plus[0] * float(EVEN_HALF[t, 0])
            for s in range(1, CHEB):
                even = even + plus[s] * float(EVEN_HALF[t, s])
            if t == mid:
                sums.append((even,))
                continue
            odd = minus[0] * float(ODD_HALF[t, 0])
            for s in range(1, CHEB):
                odd = odd + minus[s] * float(ODD_HALF[t, s])
            sums.append((even + odd, even - odd))
        for which, row in enumerate((t,) if t == mid else (t, CHEB - 1 - t)):
            real, imag = sums[0][which] * common, sums[1][which] * common
            cosine, sine = parent_ref[row, 0], parent_ref[row, 1]
            store(row, cosine * real - sine * imag, cosine * imag + sine * real)


def row_of(level, split, column, part):
    return part + 2 * (split * CHEB + column if level % 2 == 0 else column * CHEB + split)


def join_chips(me, blocks, order, held, sems, work, last_phases, factors):
    copies = []
    for index, step in enumerate(order):
        spot = pl.ds(pl.multiple_of(((me ^ step) // 2) * ROWS, 8), ROWS)
        copies.append(pltpu.make_async_copy(blocks[index], held.at[spot, :], sems.at[index]))
        copies[-1].start()
    for copy in copies:
        copy.wait()

    def received(row):
        return held[pl.ds(row, OCT, stride=ROWS), :]

    for part in range(4):
        last_phases[part] = received(WEIGHT_ROWS + part * LEVELS + LEVELS - 1)
    for level in range(LEVELS - 1):
        level_factors(level, [received(WEIGHT_ROWS + part * LEVELS + level) for part in range(4)], *factors)
        bit = OCT >> (level + 1)

        def column_step(column, _, level=level, bit=bit):
            upper = (lax.broadcasted_iota(jnp.int32, (OCT, LANES), 0) & bit) != 0
            children = [[], []]
            for s in range(CHEB):
                pairs = [[], []]
                for part in range(2):
                    row = row_of(level, s, column, part)
                    value = received(row) if level == 0 else work[row]
                    down = pltpu.roll(value, bit, 0)
                    up = down if 2 * bit == OCT else pltpu.roll(value, OCT - bit, 0)
                    pairs[0].append(jnp.where(upper, down, value))
                    pairs[1].append(jnp.where(upper, value, up))
                children[0].append(tuple(pairs[0]))
                children[1].append(tuple(pairs[1]))

            def store(row, real, imag):
                work[row_of(level, row, column, 0)] = real
                work[row_of(level, row, column, 1)] = imag

            level_column(column, children, *factors, store)
            return 0

        lax.fori_loop(0, CHEB, column_step, 0)


def even_kernel(me_ref, *refs):
    blocks = refs[:OCT]
    work, last_phases, held, parent_ref, child_ref, common_ref, sems = refs[OCT:]
    factors = (parent_ref, child_ref, common_ref)
    join_chips(me_ref[0], blocks, EVEN_ORDER, held, sems, work, last_phases, factors)


def odd_kernel(me_ref, even_work, even_phases, *refs):
    blocks = refs[:OCT]
    out_hbm, work, last_phases, held, out_ref, parent_ref, child_ref, common_ref, sems, out_sems = refs[OCT:]
    me = me_ref[0]
    own = me % 2
    early = [
        pltpu.make_async_copy(even_work, work.at[own], out_sems.at[0]),
        pltpu.make_async_copy(even_phases, last_phases.at[own], out_sems.at[1]),
    ]
    for copy in early:
        copy.start()
    factors = [ref.at[0] for ref in (parent_ref, child_ref, common_ref)]
    join_chips(me, blocks, ODD_ORDER, held, sems, work.at[1 - own], last_phases.at[1 - own], factors)
    for copy in early:
        copy.wait()

    level = LEVELS - 1
    for parity in range(2):
        level_factors(
            level,
            [last_phases[parity, part] for part in range(4)],
            parent_ref.at[parity],
            child_ref.at[parity],
            common_ref.at[parity],
        )
    chunk = out_ref.shape[0] // CHEB

    def leave(column):
        rows = pl.ds(pl.multiple_of(column * chunk, 8), chunk)
        return pltpu.make_async_copy(out_ref.at[rows, :], out_hbm.at[rows, :], out_sems.at[column])

    def column_step(column, _):
        children = [
            [tuple(work[child, row_of(level, s, column, part)] for part in range(2)) for s in range(CHEB)]
            for child in range(2)
        ]
        for parity in range(2):

            def store(row, real, imag, parity=parity):
                start = row_of(level, row, column, 0) * SLOTS + 2 * parity
                out_ref[pl.ds(start, OCT, stride=4), :] = real
                out_ref[pl.ds(start + 1, OCT, stride=4), :] = imag

            level_column(
                column, children, parent_ref.at[parity], child_ref.at[parity], common_ref.at[parity], store
            )
        leave(column).start()
        return 0

    lax.fori_loop(0, CHEB, column_step, 0)
    for column in range(CHEB):
        leave(column).wait()


def factor_scratch(count):
    return [
        pltpu.VMEM(count + (CHEB, 2, OCT, LANES), jnp.float32),
        pltpu.VMEM(count + (2, CHEB, 2, OCT, LANES), jnp.float32),
        pltpu.VMEM(count + (CHEB, OCT, LANES), jnp.float32),
    ]


def combine_even(me, blocks):
    vmem = pl.BlockSpec(memory_space=pltpu.VMEM)
    return pl.pallas_call(
        even_kernel,
        out_shape=[
            jax.ShapeDtypeStruct((WEIGHT_ROWS, OCT, LANES), jnp.float32),
            jax.ShapeDtypeStruct((4, OCT, LANES), jnp.float32),
        ],
        in_specs=[pl.BlockSpec(memory_space=pltpu.SMEM)] + [pl.BlockSpec(memory_space=pl.ANY)] * OCT,
        out_specs=[vmem, vmem],
        scratch_shapes=[
            pltpu.VMEM((OCT * ROWS, LANES), jnp.float32),
            *factor_scratch(()),
            pltpu.SemaphoreType.DMA((OCT,)),
        ],
        compiler_params=pltpu.CompilerParams(vmem_limit_bytes=16 * 2**20),
        cost_estimate=pl.CostEstimate(flops=40 * 2**20, bytes_accessed=12 * 2**20, transcendentals=0),
        name="combine_even",
    )(me, *blocks)


def combine_odd(me, even, blocks):
    hbm = pl.BlockSpec(memory_space=pltpu.HBM)
    anywhere = pl.BlockSpec(memory_space=pl.ANY)
    return pl.pallas_call(
        odd_kernel,
        out_shape=jax.ShapeDtypeStruct((WEIGHT_ROWS * SLOTS, LANES), jnp.float32),
        in_specs=[pl.BlockSpec(memory_space=pltpu.SMEM)] + [anywhere] * (2 + OCT),
        out_specs=hbm,
        scratch_shapes=[
            pltpu.VMEM((2, WEIGHT_ROWS, OCT, LANES), jnp.float32),
            pltpu.VMEM((2, 4, OCT, LANES), jnp.float32),
            pltpu.VMEM((OCT * ROWS, LANES), jnp.float32),
            pltpu.VMEM((WEIGHT_ROWS * SLOTS, LANES), jnp.float32),
            *factor_scratch((2,)),
            pltpu.SemaphoreType.DMA((OCT,)),
            pltpu.SemaphoreType.DMA((CHEB,)),
        ],
        compiler_params=pltpu.CompilerParams(vmem_limit_bytes=16 * 2**20),
        cost_estimate=pl.CostEstimate(flops=80 * 2**20, bytes_accessed=20 * 2**20, transcendentals=0),
        name="combine_odd",
    )(me, *even, *blocks)


def on_device(source_weights, wave_vectors, source_centers, phase_coef, phase_kind):
    devices = lax.axis_size("box")
    me = lax.axis_index("box").astype(jnp.int32)[None]
    direct = devices == SLOTS
    if not direct:
        me = jnp.zeros_like(me)
    weights = source_weights.reshape(2, POINTS, SLOTS, LANES).transpose(1, 2, 0, 3)
    operands = [phase_coef, weights, wave_vectors, source_centers, phase_kind[None, :]]
    operands = [me] + [pltpu.with_memory_space_constraint(operand, pltpu.HBM) for operand in operands]
    far_blocks = pack(1, *operands)
    operands[0], far_blocks[0] = lax.optimization_barrier((me, far_blocks[0]))
    near_blocks = pack(0, *operands)
    blocks = near_blocks + far_blocks
    if direct:
        for step in EVEN_ORDER + ODD_ORDER:
            if step:
                blocks[step] = lax.ppermute(blocks[step], "box", [(s, s ^ step) for s in range(SLOTS)])
    else:
        whole = jnp.concatenate(blocks, axis=1)
        whole = lax.all_to_all(whole, "box", split_axis=1, concat_axis=1, tiled=True)
        blocks = [whole[:, s * LANES : (s + 1) * LANES] for s in range(SLOTS)]
    even = combine_even(me, [blocks[step] for step in EVEN_ORDER])
    rows = combine_odd(me, even, [blocks[step] for step in ODD_ORDER])
    return rows.reshape(POINTS, SLOTS, 2, LANES).transpose(2, 0, 1, 3).reshape(2, POINTS, SLOTS * LANES)


def solution(mesh):
    in_specs = (
        P(None, None, ("groups", "box")),
        P(None, None, ("groups", "box")),
        P(None, None, ("groups", "box")),
        P(),
        P(("groups", "box")),
    )
    out_specs = P(None, None, ("groups", "box"))
    return jax.shard_map(on_device, mesh=mesh, in_specs=in_specs, out_specs=out_specs, check_vma=False)
```

```python
import functools
import math

import numpy as np

import jax
import jax.numpy as jnp
from jax import lax
from jax.experimental import pallas as pl
from jax.experimental.pallas import tpu as pltpu
from jax.sharding import PartitionSpec as P

CHEB = 9
POINTS = CHEB * CHEB
KINDS = 4
LEVELS = 4
SLOTS = 1 << LEVELS
LANES = 128
WEIGHT_ROWS = 2 * POINTS
PHASE_ROWS = 4 * LEVELS
USED_ROWS = WEIGHT_ROWS + PHASE_ROWS
ROWS = (USED_ROWS + 7) // 8 * 8
OCT = SLOTS // 2
FAR = ((8, 9), (10, 11), (12,), (14,), (13,), (15,))
NEAR = ((2, 3), (4, 5), (6, 7), (1,), (0,))
SENDS = ((8, None), (10, None), (2, None), (4, None), (6, None), (12, 2), (14, 4), (13, 12), (15, 14))

NODES = np.cos(math.pi * (2.0 * np.arange(CHEB) + 1.0) / (2.0 * CHEB))
NODES[CHEB // 2] = 0.0


def interpolation_halves():
    targets = (NODES - 1.0) / 2.0
    matrix = np.ones((CHEB, CHEB))
    for t in range(CHEB):
        for m in range(CHEB):
            if m != t:
                matrix[t] *= (targets - NODES[m]) / (NODES[t] - NODES[m])
    return (matrix + matrix[::-1]) / 2.0, (matrix - matrix[::-1]) / 2.0


EVEN_HALF, ODD_HALF = interpolation_halves()

SIN_COEFS = (3.1415926401839673, -5.167710090328242, 2.5500776596583643, -0.5982921590176602, 0.0776594073245765)
COS_COEFS = (0.999999953466542, -4.934792858659144, 4.05841191384421, -1.3318801591805476, 0.219696794464285)


def cos_sin_turns(turns):
    rest = turns - jnp.round(turns)
    square = rest * rest
    sine = jnp.float32(SIN_COEFS[-1])
    cosine = jnp.float32(COS_COEFS[-1])
    for s, c in zip(SIN_COEFS[-2::-1], COS_COEFS[-2::-1]):
        sine = sine * square + s
        cosine = cosine * square + c
    sine = sine * rest
    twice = sine + sine
    return 1.0 - twice * sine, twice * cosine


def phase_rows(wave, center, kind, coef_ref):
    a = b = e = jnp.zeros(kind.shape, jnp.float32)
    for index in range(KINDS):
        chosen = kind == index
        a = jnp.where(chosen, coef_ref[index, 0], a)
        b = jnp.where(chosen, coef_ref[index, 1], b)
        e = jnp.where(chosen, coef_ref[index, 2], e)
    k1, k2 = wave
    x1, x2 = center
    level = lax.broadcasted_iota(jnp.int32, k1.shape, 0)
    half = jnp.full(k1.shape, 2.0**-LEVELS, jnp.float32)
    for index in range(1, LEVELS):
        half = jnp.where(level == index, 2.0 ** (index - LEVELS), half)
    scaled = b * k1
    root = a * jnp.sqrt(scaled * scaled + k2 * k2 + 1.0)
    bent = root * e
    constant = x1 * k1 + x2 * k2 + root + bent * x1 * x1
    constant = constant - jnp.round(constant)
    return constant, half * (k1 + 2.0 * bent * x1), half * half * bent, half * k2


def pack_kernel(far, messages, me_ref, coef_hbm, weights_hbm, wave_hbm, center_hbm, kind_hbm, *refs):
    coef_ref, wave_ref, center_ref, kind_ref, phases_ref, sems, block_sems = refs[len(messages) :]
    outs = [None] * OCT
    for message, ref in zip(messages, refs):
        for index, step in enumerate(message):
            outs[step % OCT] = ref.at[pl.ds(index * (ROWS // 2), ROWS // 2)]
    me = me_ref[0]
    first = ((me // OCT) ^ far) * OCT
    columns = pl.ds(pl.multiple_of(first * LANES, OCT * LANES), OCT * LANES)
    small = [
        pltpu.make_async_copy(coef_hbm, coef_ref, sems.at[0]),
        pltpu.make_async_copy(wave_hbm.at[:, :, columns], wave_ref, sems.at[1]),
        pltpu.make_async_copy(center_hbm.at[:, :, columns], center_ref, sems.at[2]),
        pltpu.make_async_copy(kind_hbm.at[:, columns], kind_ref, sems.at[3]),
    ]
    large = [
        pltpu.make_async_copy(
            weights_hbm.at[:, first + ((me % OCT) ^ step)], outs[step].at[pl.ds(0, POINTS)], block_sems.at[step]
        )
        for step in range(OCT)
    ]
    for copy in small + large:
        copy.start()
    for copy in small:
        copy.wait()
    rows = phase_rows(
        (wave_ref[:, 0, :], wave_ref[:, 1, :]), (center_ref[:, 0, :], center_ref[:, 1, :]), kind_ref[...], coef_ref
    )
    for index, values in enumerate(rows):
        for level in range(LEVELS):
            row = index * LEVELS + level
            phases_ref[row // 2, row % 2, :] = values[level]
    for step, out in enumerate(outs):
        mine = pl.ds(pl.multiple_of(((me % OCT) ^ step) * LANES, LANES), LANES)
        out[POINTS : USED_ROWS // 2] = phases_ref[:, :, mine]
        out[USED_ROWS // 2 :] = jnp.zeros(((ROWS - USED_ROWS) // 2, 2, LANES), jnp.float32)
    for copy in large:
        copy.wait()


def pack(far, me, phase_coef, weights, wave, center, kind):
    messages = FAR if far else NEAR
    vmem = pl.BlockSpec(memory_space=pltpu.VMEM)
    hbm = pl.BlockSpec(memory_space=pltpu.HBM)
    arrays = pl.pallas_call(
        functools.partial(pack_kernel, far, messages),
        out_shape=[jax.ShapeDtypeStruct((len(m) * ROWS // 2, 2, LANES), jnp.float32) for m in messages],
        in_specs=[pl.BlockSpec(memory_space=pltpu.SMEM)] + [hbm] * 5,
        out_specs=[vmem] * len(messages),
        scratch_shapes=[
            pltpu.SMEM(phase_coef.shape, jnp.float32),
            pltpu.VMEM((LEVELS, 2, OCT * LANES), jnp.float32),
            pltpu.VMEM((LEVELS, 2, OCT * LANES), jnp.float32),
            pltpu.VMEM((1, OCT * LANES), jnp.int32),
            pltpu.VMEM((PHASE_ROWS // 2, 2, OCT * LANES), jnp.float32),
            pltpu.SemaphoreType.DMA((4,)),
            pltpu.SemaphoreType.DMA((OCT,)),
        ],
        compiler_params=pltpu.CompilerParams(vmem_limit_bytes=16 * 2**20),
        cost_estimate=pl.CostEstimate(flops=2**20, bytes_accessed=2 * 2**20, transcendentals=0),
        name="pack_far" if far else "pack_near",
    )(me, phase_coef, weights, wave, center, kind)
    return {m[0]: array.reshape(-1, LANES) for m, array in zip(messages, arrays)}


def level_factors(level, phases, parent_ref, child_ref, common_ref):
    constant, linear, quadratic, other = phases
    if level % 2 == 0:
        split = lambda x: constant + x * (linear + x * quadratic)
        common = lambda x: x * other
    else:
        split = lambda x: constant + x * other
        common = lambda x: x * (linear + x * quadratic)
    for t in range(CHEB):
        node = float(NODES[t])
        parent_ref[t, 0], parent_ref[t, 1] = cos_sin_turns(split(node))
        for child in range(2):
            shifted = (node + 2.0 * child - 1.0) / 2.0
            child_ref[child, t, 0], child_ref[child, t, 1] = cos_sin_turns(split(shifted))
        cosine, sine = cos_sin_turns(common(node))
        common_ref[t] = cosine * cosine + sine * sine


def level_column(column, children, parent_ref, child_ref, common_ref, store):
    scaled = []
    for child in range(2):
        line = []
        for s in range(CHEB):
            real, imag = children[child][s]
            cosine, sine = child_ref[child, s, 0], child_ref[child, s, 1]
            line.append((cosine * real + sine * imag, cosine * imag - sine * real))
        scaled.append(line)
    halves = []
    for part in range(2):
        plus = [scaled[0][s][part] + scaled[1][CHEB - 1 - s][part] for s in range(CHEB)]
        minus = [scaled[0][s][part] - scaled[1][CHEB - 1 - s][part] for s in range(CHEB)]
        halves.append((plus, minus))
    common = common_ref[column]
    mid = CHEB // 2
    for t in range(mid + 1):
        sums = []
        for part in range(2):
            plus, minus = halves[part]
            even = plus[0] * float(EVEN_HALF[t, 0])
            for s in range(1, CHEB):
                even = even + plus[s] * float(EVEN_HALF[t, s])
            if t == mid:
                sums.append((even,))
                continue
            odd = minus[0] * float(ODD_HALF[t, 0])
            for s in range(1, CHEB):
                odd = odd + minus[s] * float(ODD_HALF[t, s])
            sums.append((even + odd, even - odd))
        for which, row in enumerate((t,) if t == mid else (t, CHEB - 1 - t)):
            real, imag = sums[0][which] * common, sums[1][which] * common
            cosine, sine = parent_ref[row, 0], parent_ref[row, 1]
            store(row, cosine * real - sine * imag, cosine * imag + sine * real)


def row_of(level, split, column, part):
    return part + 2 * (split * CHEB + column if level % 2 == 0 else column * CHEB + split)


def join_chips(me, arrays, pieces, held, sems, work, last_phases, factors):
    copies = []
    for step, index, block in pieces:
        spot = pl.ds(pl.multiple_of(((me ^ step) // 2) * ROWS, 8), ROWS)
        source = arrays[index].at[pl.ds(block * ROWS, ROWS), :]
        copies.append(pltpu.make_async_copy(source, held.at[spot, :], sems.at[step // 2]))
        copies[-1].start()
    for copy in copies:
        copy.wait()

    def received(row):
        return held[pl.ds(row, OCT, stride=ROWS), :]

    for part in range(4):
        last_phases[part] = received(WEIGHT_ROWS + part * LEVELS + LEVELS - 1)
    for level in range(LEVELS - 1):
        level_factors(level, [received(WEIGHT_ROWS + part * LEVELS + level) for part in range(4)], *factors)
        bit = OCT >> (level + 1)

        def column_step(column, _, level=level, bit=bit):
            upper = (lax.broadcasted_iota(jnp.int32, (OCT, LANES), 0) & bit) != 0
            children = [[], []]
            for s in range(CHEB):
                pairs = [[], []]
                for part in range(2):
                    row = row_of(level, s, column, part)
                    value = received(row) if level == 0 else work[row]
                    down = pltpu.roll(value, bit, 0)
                    up = down if 2 * bit == OCT else pltpu.roll(value, OCT - bit, 0)
                    pairs[0].append(jnp.where(upper, down, value))
                    pairs[1].append(jnp.where(upper, value, up))
                children[0].append(tuple(pairs[0]))
                children[1].append(tuple(pairs[1]))

            def store(row, real, imag):
                work[row_of(level, row, column, 0)] = real
                work[row_of(level, row, column, 1)] = imag

            level_column(column, children, *factors, store)
            return 0

        lax.fori_loop(0, CHEB, column_step, 0)


def even_kernel(pieces, count, me_ref, *refs):
    work, last_phases, held, parent_ref, child_ref, common_ref, sems = refs[count:]
    factors = (parent_ref, child_ref, common_ref)
    join_chips(me_ref[0], refs, pieces, held, sems, work, last_phases, factors)


def odd_kernel(pieces, count, me_ref, even_work, even_phases, *refs):
    out_hbm, work, last_phases, held, out_ref, parent_ref, child_ref, common_ref, sems, out_sems = refs[count:]
    me = me_ref[0]
    own = me % 2
    early = [
        pltpu.make_async_copy(even_work, work.at[own], out_sems.at[0]),
        pltpu.make_async_copy(even_phases, last_phases.at[own], out_sems.at[1]),
    ]
    for copy in early:
        copy.start()
    factors = [ref.at[0] for ref in (parent_ref, child_ref, common_ref)]
    join_chips(me, refs, pieces, held, sems, work.at[1 - own], last_phases.at[1 - own], factors)
    for copy in early:
        copy.wait()

    level = LEVELS - 1
    for parity in range(2):
        level_factors(
            level,
            [last_phases[parity, part] for part in range(4)],
            parent_ref.at[parity],
            child_ref.at[parity],
            common_ref.at[parity],
        )
    chunk = out_ref.shape[0] // CHEB

    def leave(column):
        rows = pl.ds(pl.multiple_of(column * chunk, 8), chunk)
        return pltpu.make_async_copy(out_ref.at[rows, :], out_hbm.at[rows, :], out_sems.at[column])

    def column_step(column, _):
        children = [
            [tuple(work[child, row_of(level, s, column, part)] for part in range(2)) for s in range(CHEB)]
            for child in range(2)
        ]
        for parity in range(2):

            def store(row, real, imag, parity=parity):
                start = row_of(level, row, column, 0) * SLOTS + 2 * parity
                out_ref[pl.ds(start, OCT, stride=4), :] = real
                out_ref[pl.ds(start + 1, OCT, stride=4), :] = imag

            level_column(
                column, children, parent_ref.at[parity], child_ref.at[parity], common_ref.at[parity], store
            )
        leave(column).start()
        return 0

    lax.fori_loop(0, CHEB, column_step, 0)
    for column in range(CHEB):
        leave(column).wait()


def factor_scratch(count):
    return [
        pltpu.VMEM(count + (CHEB, 2, OCT, LANES), jnp.float32),
        pltpu.VMEM(count + (2, CHEB, 2, OCT, LANES), jnp.float32),
        pltpu.VMEM(count + (CHEB, OCT, LANES), jnp.float32),
    ]


def combine_even(me, arrays, pieces):
    vmem = pl.BlockSpec(memory_space=pltpu.VMEM)
    return pl.pallas_call(
        functools.partial(even_kernel, pieces, len(arrays)),
        out_shape=[
            jax.ShapeDtypeStruct((WEIGHT_ROWS, OCT, LANES), jnp.float32),
            jax.ShapeDtypeStruct((4, OCT, LANES), jnp.float32),
        ],
        in_specs=[pl.BlockSpec(memory_space=pltpu.SMEM)] + [pl.BlockSpec(memory_space=pl.ANY)] * len(arrays),
        out_specs=[vmem, vmem],
        scratch_shapes=[
            pltpu.VMEM((OCT * ROWS, LANES), jnp.float32),
            *factor_scratch(()),
            pltpu.SemaphoreType.DMA((OCT,)),
        ],
        compiler_params=pltpu.CompilerParams(vmem_limit_bytes=16 * 2**20),
        cost_estimate=pl.CostEstimate(flops=40 * 2**20, bytes_accessed=12 * 2**20, transcendentals=0),
        name="combine_even",
    )(me, *arrays)


def combine_odd(me, even, arrays, pieces):
    hbm = pl.BlockSpec(memory_space=pltpu.HBM)
    anywhere = pl.BlockSpec(memory_space=pl.ANY)
    return pl.pallas_call(
        functools.partial(odd_kernel, pieces, len(arrays)),
        out_shape=jax.ShapeDtypeStruct((WEIGHT_ROWS * SLOTS, LANES), jnp.float32),
        in_specs=[pl.BlockSpec(memory_space=pltpu.SMEM)] + [anywhere] * (2 + len(arrays)),
        out_specs=hbm,
        scratch_shapes=[
            pltpu.VMEM((2, WEIGHT_ROWS, OCT, LANES), jnp.float32),
            pltpu.VMEM((2, 4, OCT, LANES), jnp.float32),
            pltpu.VMEM((OCT * ROWS, LANES), jnp.float32),
            pltpu.VMEM((WEIGHT_ROWS * SLOTS, LANES), jnp.float32),
            *factor_scratch((2,)),
            pltpu.SemaphoreType.DMA((OCT,)),
            pltpu.SemaphoreType.DMA((CHEB,)),
        ],
        compiler_params=pltpu.CompilerParams(vmem_limit_bytes=16 * 2**20),
        cost_estimate=pl.CostEstimate(flops=80 * 2**20, bytes_accessed=20 * 2**20, transcendentals=0),
        name="combine_odd",
    )(me, *even, *arrays)


def on_device(source_weights, wave_vectors, source_centers, phase_coef, phase_kind):
    devices = lax.axis_size("box")
    me = lax.axis_index("box").astype(jnp.int32)[None]
    direct = devices == SLOTS
    if not direct:
        me = jnp.zeros_like(me)
    weights = source_weights.reshape(2, POINTS, SLOTS, LANES).transpose(1, 2, 0, 3)
    operands = [phase_coef, weights, wave_vectors, source_centers, phase_kind[None, :]]
    operands = [me] + [pltpu.with_memory_space_constraint(operand, pltpu.HBM) for operand in operands]
    sent = pack(1, *operands)
    sent.update(pack(0, *operands))
    if direct:

        def exchange(array, step):
            return lax.ppermute(array, "box", [(s, s ^ step) for s in range(SLOTS)])

        for step, earlier in SENDS:
            if earlier is not None:
                sent[step], sent[earlier] = lax.optimization_barrier((sent[step], sent[earlier]))
            sent[step] = exchange(sent[step], step)
        far_swap = exchange(jnp.concatenate([sent[8][ROWS:], sent[10][ROWS:]]), 1)
        near_swap = exchange(jnp.concatenate([sent[1], sent[2][ROWS:], sent[4][ROWS:], sent[6][ROWS:]]), 1)
        even_arrays = [sent[step] for step in range(0, SLOTS, 2)]
        even_pieces = [(step, step // 2, 0) for step in range(0, SLOTS, 2)]
        odd_arrays = [near_swap, far_swap, sent[13], sent[15]]
        odd_pieces = [(1, 0, 0), (3, 0, 1), (5, 0, 2), (7, 0, 3), (9, 1, 0), (11, 1, 1), (13, 2, 0), (15, 3, 0)]
    else:
        blocks = [None] * SLOTS
        for message in FAR + NEAR:
            for index, step in enumerate(message):
                blocks[step] = sent[message[0]][index * ROWS : (index + 1) * ROWS]
        whole = jnp.concatenate(blocks, axis=1)
        whole = lax.all_to_all(whole, "box", split_axis=1, concat_axis=1, tiled=True)
        blocks = [whole[:, s * LANES : (s + 1) * LANES] for s in range(SLOTS)]
        even_arrays, odd_arrays = blocks[0::2], blocks[1::2]
        even_pieces = [(2 * index, index, 0) for index in range(OCT)]
        odd_pieces = [(2 * index + 1, index, 0) for index in range(OCT)]
    even = combine_even(me, even_arrays, even_pieces)
    rows = combine_odd(me, even, odd_arrays, odd_pieces)
    return rows.reshape(POINTS, SLOTS, 2, LANES).transpose(2, 0, 1, 3).reshape(2, POINTS, SLOTS * LANES)


def solution(mesh):
    in_specs = (
        P(None, None, ("groups", "box")),
        P(None, None, ("groups", "box")),
        P(None, None, ("groups", "box")),
        P(),
        P(("groups", "box")),
    )
    out_specs = P(None, None, ("groups", "box"))
    return jax.shard_map(on_device, mesh=mesh, in_specs=in_specs, out_specs=out_specs, check_vma=False)
```

```python
import functools
import math

import numpy as np

import jax
import jax.numpy as jnp
from jax import lax
from jax.experimental import pallas as pl
from jax.experimental.pallas import tpu as pltpu
from jax.sharding import PartitionSpec as P

CHEB = 9
POINTS = CHEB * CHEB
KINDS = 4
LEVELS = 4
SLOTS = 1 << LEVELS
LANES = 128
WEIGHT_ROWS = 2 * POINTS
PHASE_ROWS = 4 * LEVELS
USED_ROWS = WEIGHT_ROWS + PHASE_ROWS
ROWS = (USED_ROWS + 7) // 8 * 8
OCT = SLOTS // 2
PACKS = ((8, 10, 12), (2, 4, 6), (14, 9, 11, 13, 15), (3, 5, 7, 1, 0))
EVEN_ORDER = (8, 10, 12, 2, 4, 6, 14, 0)
ODD_ORDER = (9, 11, 13, 15, 3, 5, 7, 1)

NODES = np.cos(math.pi * (2.0 * np.arange(CHEB) + 1.0) / (2.0 * CHEB))
NODES[CHEB // 2] = 0.0


def interpolation_halves():
    targets = (NODES - 1.0) / 2.0
    matrix = np.ones((CHEB, CHEB))
    for t in range(CHEB):
        for m in range(CHEB):
            if m != t:
                matrix[t] *= (targets - NODES[m]) / (NODES[t] - NODES[m])
    return (matrix + matrix[::-1]) / 2.0, (matrix - matrix[::-1]) / 2.0


EVEN_HALF, ODD_HALF = interpolation_halves()

SIN_COEFS = (3.1415926401839673, -5.167710090328242, 2.5500776596583643, -0.5982921590176602, 0.0776594073245765)
COS_COEFS = (0.999999953466542, -4.934792858659144, 4.05841191384421, -1.3318801591805476, 0.219696794464285)


def cos_sin_turns(turns):
    rest = turns - jnp.round(turns)
    square = rest * rest
    sine = jnp.float32(SIN_COEFS[-1])
    cosine = jnp.float32(COS_COEFS[-1])
    for s, c in zip(SIN_COEFS[-2::-1], COS_COEFS[-2::-1]):
        sine = sine * square + s
        cosine = cosine * square + c
    sine = sine * rest
    twice = sine + sine
    return 1.0 - twice * sine, twice * cosine


def phase_rows(wave, center, kind, coef_ref):
    a = b = e = jnp.zeros(kind.shape, jnp.float32)
    for index in range(KINDS):
        chosen = kind == index
        a = jnp.where(chosen, coef_ref[index, 0], a)
        b = jnp.where(chosen, coef_ref[index, 1], b)
        e = jnp.where(chosen, coef_ref[index, 2], e)
    k1, k2 = wave
    x1, x2 = center
    level = lax.broadcasted_iota(jnp.int32, k1.shape, 0)
    half = jnp.full(k1.shape, 2.0**-LEVELS, jnp.float32)
    for index in range(1, LEVELS):
        half = jnp.where(level == index, 2.0 ** (index - LEVELS), half)
    scaled = b * k1
    root = a * jnp.sqrt(scaled * scaled + k2 * k2 + 1.0)
    bent = root * e
    constant = x1 * k1 + x2 * k2 + root + bent * x1 * x1
    constant = constant - jnp.round(constant)
    return constant, half * (k1 + 2.0 * bent * x1), half * half * bent, half * k2


def phase_kernel(coef_hbm, wave_hbm, center_hbm, kind_hbm, phases_ref, coef_ref, wave_ref, center_ref, kind_ref, sems):
    copies = [
        pltpu.make_async_copy(source, target, sems.at[index])
        for index, (source, target) in enumerate(
            ((coef_hbm, coef_ref), (wave_hbm, wave_ref), (center_hbm, center_ref), (kind_hbm, kind_ref))
        )
    ]
    for copy in copies:
        copy.start()
    for copy in copies:
        copy.wait()
    rows = phase_rows(
        (wave_ref[:, 0, :], wave_ref[:, 1, :]), (center_ref[:, 0, :], center_ref[:, 1, :]), kind_ref[...], coef_ref
    )
    for index, values in enumerate(rows):
        for level in range(LEVELS):
            row = index * LEVELS + level
            phases_ref[row // 2, row % 2, :] = values[level]


def pack_kernel(steps, first, me_ref, weights_hbm, *refs):
    if first:
        small, refs = refs[:4], refs[4:]
        outs, refs = refs[: len(steps)], refs[len(steps) :]
        phases_ref, block_sems, scratch = refs[0], refs[1], refs[2:]
    else:
        phases_ref, outs, block_sems = refs[0], refs[1 : 1 + len(steps)], refs[1 + len(steps)]
    slots = [me_ref[0] ^ step for step in steps]
    copies = [
        pltpu.make_async_copy(weights_hbm.at[:, slot], out.at[pl.ds(0, POINTS)], block_sems.at[index])
        for index, (slot, out) in enumerate(zip(slots, outs))
    ]
    for copy in copies:
        copy.start()
    if first:
        phase_kernel(*small, phases_ref, *scratch)
    for slot, out in zip(slots, outs):
        out[POINTS : USED_ROWS // 2] = phases_ref[:, :, pl.ds(pl.multiple_of(slot * LANES, LANES), LANES)]
        out[USED_ROWS // 2 :] = jnp.zeros(((ROWS - USED_ROWS) // 2, 2, LANES), jnp.float32)
    for copy in copies:
        copy.wait()


def pack(steps, me, weights, phases, sources):
    first = phases is None
    vmem = pl.BlockSpec(memory_space=pltpu.VMEM)
    hbm = pl.BlockSpec(memory_space=pltpu.HBM)
    out_shape = [jax.ShapeDtypeStruct((ROWS // 2, 2, LANES), jnp.float32) for _ in steps]
    scratch = [pltpu.SemaphoreType.DMA((len(steps),))]
    if first:
        boxes = sources[-1].shape[-1]
        out_shape.append(jax.ShapeDtypeStruct((PHASE_ROWS // 2, 2, boxes), jnp.float32))
        scratch += [pltpu.SMEM(sources[0].shape, jnp.float32)]
        scratch += [pltpu.VMEM(source.shape, source.dtype) for source in sources[1:]]
        scratch += [pltpu.SemaphoreType.DMA((len(sources),))]
    operands = sources if first else [phases]
    *arrays, last = pl.pallas_call(
        functools.partial(pack_kernel, steps, first),
        out_shape=out_shape,
        in_specs=[pl.BlockSpec(memory_space=pltpu.SMEM), hbm] + ([hbm] * len(sources) if first else [vmem]),
        out_specs=[vmem] * len(out_shape),
        scratch_shapes=scratch,
        compiler_params=pltpu.CompilerParams(vmem_limit_bytes=16 * 2**20),
        cost_estimate=pl.CostEstimate(flops=2**20, bytes_accessed=2**20, transcendentals=0),
        name="pack",
    )(me, weights, *operands)
    if first:
        phases = last
    else:
        arrays.append(last)
    return dict(zip(steps, arrays)), phases


def level_factors(level, phases, parent_ref, child_ref, common_ref):
    constant, linear, quadratic, other = phases
    if level % 2 == 0:
        split = lambda x: constant + x * (linear + x * quadratic)
        common = lambda x: x * other
    else:
        split = lambda x: constant + x * other
        common = lambda x: x * (linear + x * quadratic)
    for t in range(CHEB):
        node = float(NODES[t])
        parent_ref[t, 0], parent_ref[t, 1] = cos_sin_turns(split(node))
        for child in range(2):
            shifted = (node + 2.0 * child - 1.0) / 2.0
            child_ref[child, t, 0], child_ref[child, t, 1] = cos_sin_turns(split(shifted))
        cosine, sine = cos_sin_turns(common(node))
        common_ref[t] = cosine * cosine + sine * sine


def level_column(column, children, parent_ref, child_ref, common_ref, store):
    scaled = []
    for child in range(2):
        line = []
        for s in range(CHEB):
            real, imag = children[child][s]
            cosine, sine = child_ref[child, s, 0], child_ref[child, s, 1]
            line.append((cosine * real + sine * imag, cosine * imag - sine * real))
        scaled.append(line)
    halves = []
    for part in range(2):
        plus = [scaled[0][s][part] + scaled[1][CHEB - 1 - s][part] for s in range(CHEB)]
        minus = [scaled[0][s][part] - scaled[1][CHEB - 1 - s][part] for s in range(CHEB)]
        halves.append((plus, minus))
    common = common_ref[column]
    mid = CHEB // 2
    for t in range(mid + 1):
        sums = []
        for part in range(2):
            plus, minus = halves[part]
            even = plus[0] * float(EVEN_HALF[t, 0])
            for s in range(1, CHEB):
                even = even + plus[s] * float(EVEN_HALF[t, s])
            if t == mid:
                sums.append((even,))
                continue
            odd = minus[0] * float(ODD_HALF[t, 0])
            for s in range(1, CHEB):
                odd = odd + minus[s] * float(ODD_HALF[t, s])
            sums.append((even + odd, even - odd))
        for which, row in enumerate((t,) if t == mid else (t, CHEB - 1 - t)):
            real, imag = sums[0][which] * common, sums[1][which] * common
            cosine, sine = parent_ref[row, 0], parent_ref[row, 1]
            store(row, cosine * real - sine * imag, cosine * imag + sine * real)


def row_of(level, split, column, part):
    return part + 2 * (split * CHEB + column if level % 2 == 0 else column * CHEB + split)


def join_chips(me, arrays, pieces, held, sems, work, last_phases, factors):
    copies = []
    for step, index, block in pieces:
        spot = pl.ds(pl.multiple_of(((me ^ step) // 2) * ROWS, 8), ROWS)
        source = arrays[index].at[pl.ds(block * ROWS, ROWS), :]
        copies.append(pltpu.make_async_copy(source, held.at[spot, :], sems.at[step // 2]))
        copies[-1].start()
    for copy in copies:
        copy.wait()

    def received(row):
        return held[pl.ds(row, OCT, stride=ROWS), :]

    for part in range(4):
        last_phases[part] = received(WEIGHT_ROWS + part * LEVELS + LEVELS - 1)
    for level in range(LEVELS - 1):
        level_factors(level, [received(WEIGHT_ROWS + part * LEVELS + level) for part in range(4)], *factors)
        bit = OCT >> (level + 1)

        def column_step(column, _, level=level, bit=bit):
            upper = (lax.broadcasted_iota(jnp.int32, (OCT, LANES), 0) & bit) != 0
            children = [[], []]
            for s in range(CHEB):
                pairs = [[], []]
                for part in range(2):
                    row = row_of(level, s, column, part)
                    value = received(row) if level == 0 else work[row]
                    down = pltpu.roll(value, bit, 0)
                    up = down if 2 * bit == OCT else pltpu.roll(value, OCT - bit, 0)
                    pairs[0].append(jnp.where(upper, down, value))
                    pairs[1].append(jnp.where(upper, value, up))
                children[0].append(tuple(pairs[0]))
                children[1].append(tuple(pairs[1]))

            def store(row, real, imag):
                work[row_of(level, row, column, 0)] = real
                work[row_of(level, row, column, 1)] = imag

            level_column(column, children, *factors, store)
            return 0

        lax.fori_loop(0, CHEB, column_step, 0)


def even_kernel(pieces, count, me_ref, *refs):
    work, last_phases, held, parent_ref, child_ref, common_ref, sems = refs[count:]
    factors = (parent_ref, child_ref, common_ref)
    join_chips(me_ref[0], refs, pieces, held, sems, work, last_phases, factors)


def odd_kernel(pieces, count, me_ref, even_work, even_phases, *refs):
    out_hbm, work, last_phases, held, out_ref, parent_ref, child_ref, common_ref, sems, out_sems = refs[count:]
    me = me_ref[0]
    own = me % 2
    early = [
        pltpu.make_async_copy(even_work, work.at[own], out_sems.at[0]),
        pltpu.make_async_copy(even_phases, last_phases.at[own], out_sems.at[1]),
    ]
    for copy in early:
        copy.start()
    factors = [ref.at[0] for ref in (parent_ref, child_ref, common_ref)]
    join_chips(me, refs, pieces, held, sems, work.at[1 - own], last_phases.at[1 - own], factors)
    for copy in early:
        copy.wait()

    level = LEVELS - 1
    for parity in range(2):
        level_factors(
            level,
            [last_phases[parity, part] for part in range(4)],
            parent_ref.at[parity],
            child_ref.at[parity],
            common_ref.at[parity],
        )
    chunk = out_ref.shape[0] // CHEB

    def leave(column):
        rows = pl.ds(pl.multiple_of(column * chunk, 8), chunk)
        return pltpu.make_async_copy(out_ref.at[rows, :], out_hbm.at[rows, :], out_sems.at[column])

    def column_step(column, _):
        children = [
            [tuple(work[child, row_of(level, s, column, part)] for part in range(2)) for s in range(CHEB)]
            for child in range(2)
        ]
        for parity in range(2):

            def store(row, real, imag, parity=parity):
                start = row_of(level, row, column, 0) * SLOTS + 2 * parity
                out_ref[pl.ds(start, OCT, stride=4), :] = real
                out_ref[pl.ds(start + 1, OCT, stride=4), :] = imag

            level_column(
                column, children, parent_ref.at[parity], child_ref.at[parity], common_ref.at[parity], store
            )
        leave(column).start()
        return 0

    lax.fori_loop(0, CHEB, column_step, 0)
    for column in range(CHEB):
        leave(column).wait()


def factor_scratch(count):
    return [
        pltpu.VMEM(count + (CHEB, 2, OCT, LANES), jnp.float32),
        pltpu.VMEM(count + (2, CHEB, 2, OCT, LANES), jnp.float32),
        pltpu.VMEM(count + (CHEB, OCT, LANES), jnp.float32),
    ]


def combine_even(me, arrays, pieces):
    vmem = pl.BlockSpec(memory_space=pltpu.VMEM)
    return pl.pallas_call(
        functools.partial(even_kernel, pieces, len(arrays)),
        out_shape=[
            jax.ShapeDtypeStruct((WEIGHT_ROWS, OCT, LANES), jnp.float32),
            jax.ShapeDtypeStruct((4, OCT, LANES), jnp.float32),
        ],
        in_specs=[pl.BlockSpec(memory_space=pltpu.SMEM)] + [pl.BlockSpec(memory_space=pl.ANY)] * len(arrays),
        out_specs=[vmem, vmem],
        scratch_shapes=[
            pltpu.VMEM((OCT * ROWS, LANES), jnp.float32),
            *factor_scratch(()),
            pltpu.SemaphoreType.DMA((OCT,)),
        ],
        compiler_params=pltpu.CompilerParams(vmem_limit_bytes=16 * 2**20),
        cost_estimate=pl.CostEstimate(flops=40 * 2**20, bytes_accessed=12 * 2**20, transcendentals=0),
        name="combine_even",
    )(me, *arrays)


def combine_odd(me, even, arrays, pieces):
    hbm = pl.BlockSpec(memory_space=pltpu.HBM)
    anywhere = pl.BlockSpec(memory_space=pl.ANY)
    return pl.pallas_call(
        functools.partial(odd_kernel, pieces, len(arrays)),
        out_shape=jax.ShapeDtypeStruct((WEIGHT_ROWS * SLOTS, LANES), jnp.float32),
        in_specs=[pl.BlockSpec(memory_space=pltpu.SMEM)] + [anywhere] * (2 + len(arrays)),
        out_specs=hbm,
        scratch_shapes=[
            pltpu.VMEM((2, WEIGHT_ROWS, OCT, LANES), jnp.float32),
            pltpu.VMEM((2, 4, OCT, LANES), jnp.float32),
            pltpu.VMEM((OCT * ROWS, LANES), jnp.float32),
            pltpu.VMEM((WEIGHT_ROWS * SLOTS, LANES), jnp.float32),
            *factor_scratch((2,)),
            pltpu.SemaphoreType.DMA((OCT,)),
            pltpu.SemaphoreType.DMA((CHEB,)),
        ],
        compiler_params=pltpu.CompilerParams(vmem_limit_bytes=16 * 2**20),
        cost_estimate=pl.CostEstimate(flops=80 * 2**20, bytes_accessed=20 * 2**20, transcendentals=0),
        name="combine_odd",
    )(me, *even, *arrays)


def on_device(source_weights, wave_vectors, source_centers, phase_coef, phase_kind):
    devices = lax.axis_size("box")
    me = lax.axis_index("box").astype(jnp.int32)[None]
    direct = devices == SLOTS
    if not direct:
        me = jnp.zeros_like(me)
    weights = source_weights.reshape(2, POINTS, SLOTS, LANES).transpose(1, 2, 0, 3)
    weights, *sources = [
        pltpu.with_memory_space_constraint(operand, pltpu.HBM)
        for operand in (weights, phase_coef, wave_vectors, source_centers, phase_kind[None, :])
    ]
    blocks, phases = {}, None
    for steps in PACKS:
        if blocks:
            last = next(reversed(blocks))
            phases, blocks[last] = lax.optimization_barrier((phases, blocks[last]))
        packed, phases = pack(steps, me, weights, phases, sources)
        blocks.update(packed)
    blocks = {step: block.reshape(ROWS, LANES) for step, block in blocks.items()}
    if direct:
        for step in EVEN_ORDER + ODD_ORDER:
            if step:
                blocks[step] = lax.ppermute(blocks[step], "box", [(s, s ^ step) for s in range(SLOTS)])
    else:
        whole = jnp.concatenate([blocks[step] for step in range(SLOTS)], axis=1)
        whole = lax.all_to_all(whole, "box", split_axis=1, concat_axis=1, tiled=True)
        blocks = [whole[:, s * LANES : (s + 1) * LANES] for s in range(SLOTS)]
    even_arrays, odd_arrays = ([blocks[step] for step in order] for order in (EVEN_ORDER, ODD_ORDER))
    even_pieces, odd_pieces = ([(step, index, 0) for index, step in enumerate(o)] for o in (EVEN_ORDER, ODD_ORDER))
    even = combine_even(me, even_arrays, even_pieces)
    rows = combine_odd(me, even, odd_arrays, odd_pieces)
    return rows.reshape(POINTS, SLOTS, 2, LANES).transpose(2, 0, 1, 3).reshape(2, POINTS, SLOTS * LANES)


def solution(mesh):
    in_specs = (
        P(None, None, ("groups", "box")),
        P(None, None, ("groups", "box")),
        P(None, None, ("groups", "box")),
        P(),
        P(("groups", "box")),
    )
    out_specs = P(None, None, ("groups", "box"))
    return jax.shard_map(on_device, mesh=mesh, in_specs=in_specs, out_specs=out_specs, check_vma=False)
```

```python
import functools
import math

import numpy as np

import jax
import jax.numpy as jnp
from jax import lax
from jax.experimental import pallas as pl
from jax.experimental.pallas import tpu as pltpu
from jax.sharding import PartitionSpec as P

CHEB = 9
POINTS = CHEB * CHEB
KINDS = 4
LEVELS = 4
SLOTS = 1 << LEVELS
LANES = 128
WEIGHT_ROWS = 2 * POINTS
PHASE_ROWS = 4 * LEVELS
USED_ROWS = WEIGHT_ROWS + PHASE_ROWS
ROWS = (USED_ROWS + 7) // 8 * 8
OCT = SLOTS // 2
PACKS = ((8, 10, 12), (2, 4, 6), (14, 9, 11, 13, 15), (3, 5, 7, 1, 0))
EVEN_ORDER = (8, 10, 12, 2, 4, 6, 14, 0)
ODD_ORDER = (9, 11, 13, 15, 3, 5, 7, 1)
LATE = (7, 1)

NODES = np.cos(math.pi * (2.0 * np.arange(CHEB) + 1.0) / (2.0 * CHEB))
NODES[CHEB // 2] = 0.0


def interpolation_halves():
    targets = (NODES - 1.0) / 2.0
    matrix = np.ones((CHEB, CHEB))
    for t in range(CHEB):
        for m in range(CHEB):
            if m != t:
                matrix[t] *= (targets - NODES[m]) / (NODES[t] - NODES[m])
    return (matrix + matrix[::-1]) / 2.0, (matrix - matrix[::-1]) / 2.0


EVEN_HALF, ODD_HALF = interpolation_halves()

SIN_COEFS = (3.1415926401839673, -5.167710090328242, 2.5500776596583643, -0.5982921590176602, 0.0776594073245765)
COS_COEFS = (0.999999953466542, -4.934792858659144, 4.05841191384421, -1.3318801591805476, 0.219696794464285)


def cos_sin_turns(turns):
    rest = turns - jnp.round(turns)
    square = rest * rest
    sine = jnp.float32(SIN_COEFS[-1])
    cosine = jnp.float32(COS_COEFS[-1])
    for s, c in zip(SIN_COEFS[-2::-1], COS_COEFS[-2::-1]):
        sine = sine * square + s
        cosine = cosine * square + c
    sine = sine * rest
    twice = sine + sine
    return 1.0 - twice * sine, twice * cosine


def phase_rows(wave, center, kind, coef_ref):
    a = b = e = jnp.zeros(kind.shape, jnp.float32)
    for index in range(KINDS):
        chosen = kind == index
        a = jnp.where(chosen, coef_ref[index, 0], a)
        b = jnp.where(chosen, coef_ref[index, 1], b)
        e = jnp.where(chosen, coef_ref[index, 2], e)
    k1, k2 = wave
    x1, x2 = center
    level = lax.broadcasted_iota(jnp.int32, k1.shape, 0)
    half = jnp.full(k1.shape, 2.0**-LEVELS, jnp.float32)
    for index in range(1, LEVELS):
        half = jnp.where(level == index, 2.0 ** (index - LEVELS), half)
    scaled = b * k1
    root = a * jnp.sqrt(scaled * scaled + k2 * k2 + 1.0)
    bent = root * e
    constant = x1 * k1 + x2 * k2 + root + bent * x1 * x1
    constant = constant - jnp.round(constant)
    return constant, half * (k1 + 2.0 * bent * x1), half * half * bent, half * k2


def phase_kernel(coef_hbm, wave_hbm, center_hbm, kind_hbm, phases_ref, coef_ref, wave_ref, center_ref, kind_ref, sems):
    copies = [
        pltpu.make_async_copy(source, target, sems.at[index])
        for index, (source, target) in enumerate(
            ((coef_hbm, coef_ref), (wave_hbm, wave_ref), (center_hbm, center_ref), (kind_hbm, kind_ref))
        )
    ]
    for copy in copies:
        copy.start()
    for copy in copies:
        copy.wait()
    rows = phase_rows(
        (wave_ref[:, 0, :], wave_ref[:, 1, :]), (center_ref[:, 0, :], center_ref[:, 1, :]), kind_ref[...], coef_ref
    )
    for index, values in enumerate(rows):
        for level in range(LEVELS):
            row = index * LEVELS + level
            phases_ref[row // 2, row % 2, :] = values[level]


def pack_kernel(steps, first, me_ref, weights_hbm, *refs):
    if first:
        small, refs = refs[:4], refs[4:]
        outs, refs = refs[: len(steps)], refs[len(steps) :]
        phases_ref, block_sems, scratch = refs[0], refs[1], refs[2:]
    else:
        phases_ref, outs, block_sems = refs[0], refs[1 : 1 + len(steps)], refs[1 + len(steps)]
    slots = [me_ref[0] ^ step for step in steps]
    copies = [
        pltpu.make_async_copy(weights_hbm.at[:, slot], out.at[pl.ds(0, POINTS)], block_sems.at[index])
        for index, (slot, out) in enumerate(zip(slots, outs))
    ]
    for copy in copies:
        copy.start()
    if first:
        phase_kernel(*small, phases_ref, *scratch)
    for slot, out in zip(slots, outs):
        out[POINTS : USED_ROWS // 2] = phases_ref[:, :, pl.ds(pl.multiple_of(slot * LANES, LANES), LANES)]
        out[USED_ROWS // 2 :] = jnp.zeros(((ROWS - USED_ROWS) // 2, 2, LANES), jnp.float32)
    for copy in copies:
        copy.wait()


def pack(steps, me, weights, phases, sources):
    first = phases is None
    vmem = pl.BlockSpec(memory_space=pltpu.VMEM)
    hbm = pl.BlockSpec(memory_space=pltpu.HBM)
    out_shape = [jax.ShapeDtypeStruct((ROWS // 2, 2, LANES), jnp.float32) for _ in steps]
    scratch = [pltpu.SemaphoreType.DMA((len(steps),))]
    if first:
        boxes = sources[-1].shape[-1]
        out_shape.append(jax.ShapeDtypeStruct((PHASE_ROWS // 2, 2, boxes), jnp.float32))
        scratch += [pltpu.SMEM(sources[0].shape, jnp.float32)]
        scratch += [pltpu.VMEM(source.shape, source.dtype) for source in sources[1:]]
        scratch += [pltpu.SemaphoreType.DMA((len(sources),))]
    operands = sources if first else [phases]
    *arrays, last = pl.pallas_call(
        functools.partial(pack_kernel, steps, first),
        out_shape=out_shape,
        in_specs=[pl.BlockSpec(memory_space=pltpu.SMEM), hbm] + ([hbm] * len(sources) if first else [vmem]),
        out_specs=[vmem] * len(out_shape),
        scratch_shapes=scratch,
        compiler_params=pltpu.CompilerParams(vmem_limit_bytes=16 * 2**20),
        cost_estimate=pl.CostEstimate(flops=2**20, bytes_accessed=2**20, transcendentals=0),
        name="pack",
    )(me, weights, *operands)
    if first:
        phases = last
    else:
        arrays.append(last)
    return dict(zip(steps, arrays)), phases


def level_factors(level, phases, parent_ref, child_ref, common_ref):
    constant, linear, quadratic, other = phases
    if level % 2 == 0:
        split = lambda x: constant + x * (linear + x * quadratic)
        common = lambda x: x * other
    else:
        split = lambda x: constant + x * other
        common = lambda x: x * (linear + x * quadratic)
    for t in range(CHEB):
        node = float(NODES[t])
        parent_ref[t, 0], parent_ref[t, 1] = cos_sin_turns(split(node))
        for child in range(2):
            shifted = (node + 2.0 * child - 1.0) / 2.0
            child_ref[child, t, 0], child_ref[child, t, 1] = cos_sin_turns(split(shifted))
        cosine, sine = cos_sin_turns(common(node))
        common_ref[t] = cosine * cosine + sine * sine


def level_column(column, children, parent_ref, child_ref, common_ref, store):
    scaled = []
    for child in range(2):
        line = []
        for s in range(CHEB):
            real, imag = children[child][s]
            cosine, sine = child_ref[child, s, 0], child_ref[child, s, 1]
            line.append((cosine * real + sine * imag, cosine * imag - sine * real))
        scaled.append(line)
    halves = []
    for part in range(2):
        plus = [scaled[0][s][part] + scaled[1][CHEB - 1 - s][part] for s in range(CHEB)]
        minus = [scaled[0][s][part] - scaled[1][CHEB - 1 - s][part] for s in range(CHEB)]
        halves.append((plus, minus))
    common = common_ref[column]
    mid = CHEB // 2
    for t in range(mid + 1):
        sums = []
        for part in range(2):
            plus, minus = halves[part]
            even = plus[0] * float(EVEN_HALF[t, 0])
            for s in range(1, CHEB):
                even = even + plus[s] * float(EVEN_HALF[t, s])
            if t == mid:
                sums.append((even,))
                continue
            odd = minus[0] * float(ODD_HALF[t, 0])
            for s in range(1, CHEB):
                odd = odd + minus[s] * float(ODD_HALF[t, s])
            sums.append((even + odd, even - odd))
        for which, row in enumerate((t,) if t == mid else (t, CHEB - 1 - t)):
            real, imag = sums[0][which] * common, sums[1][which] * common
            cosine, sine = parent_ref[row, 0], parent_ref[row, 1]
            store(row, cosine * real - sine * imag, cosine * imag + sine * real)


def row_of(level, split, column, part):
    return part + 2 * (split * CHEB + column if level % 2 == 0 else column * CHEB + split)


def join_chips(me, blocks, order, held, sems, work, last_phases, factors):
    copies = []
    for index, step in enumerate(order):
        spot = pl.ds(pl.multiple_of(((me ^ step) // 2) * ROWS, 8), ROWS)
        copies.append(pltpu.make_async_copy(blocks[index], held.at[spot, :], sems.at[index]))
        copies[-1].start()
    for copy in copies:
        copy.wait()

    def received(row):
        return held[pl.ds(row, OCT, stride=ROWS), :]

    for part in range(4):
        last_phases[part] = received(WEIGHT_ROWS + part * LEVELS + LEVELS - 1)
    for level in range(LEVELS - 1):
        level_factors(level, [received(WEIGHT_ROWS + part * LEVELS + level) for part in range(4)], *factors)
        bit = OCT >> (level + 1)

        def column_step(column, _, level=level, bit=bit):
            upper = (lax.broadcasted_iota(jnp.int32, (OCT, LANES), 0) & bit) != 0
            children = [[], []]
            for s in range(CHEB):
                pairs = [[], []]
                for part in range(2):
                    row = row_of(level, s, column, part)
                    value = received(row) if level == 0 else work[row]
                    down = pltpu.roll(value, bit, 0)
                    up = down if 2 * bit == OCT else pltpu.roll(value, OCT - bit, 0)
                    pairs[0].append(jnp.where(upper, down, value))
                    pairs[1].append(jnp.where(upper, value, up))
                children[0].append(tuple(pairs[0]))
                children[1].append(tuple(pairs[1]))

            def store(row, real, imag):
                work[row_of(level, row, column, 0)] = real
                work[row_of(level, row, column, 1)] = imag

            level_column(column, children, *factors, store)
            return 0

        lax.fori_loop(0, CHEB, column_step, 0, unroll=3)


def even_kernel(me_ref, *refs):
    work, last_phases, held, parent_ref, child_ref, common_ref, sems = refs[OCT:]
    factors = (parent_ref, child_ref, common_ref)
    join_chips(me_ref[0], refs, EVEN_ORDER, held, sems, work, last_phases, factors)


def odd_kernel(me_ref, even_work, even_phases, *refs):
    out_hbm, work, last_phases, held, out_ref, parent_ref, child_ref, common_ref, sems, out_sems = refs[OCT:]
    me = me_ref[0]
    own = me % 2
    early = [
        pltpu.make_async_copy(even_work, work.at[own], out_sems.at[0]),
        pltpu.make_async_copy(even_phases, last_phases.at[own], out_sems.at[1]),
    ]
    for copy in early:
        copy.start()
    factors = [ref.at[0] for ref in (parent_ref, child_ref, common_ref)]
    join_chips(me, refs, ODD_ORDER, held, sems, work.at[1 - own], last_phases.at[1 - own], factors)
    for copy in early:
        copy.wait()

    level = LEVELS - 1
    for parity in range(2):
        level_factors(
            level,
            [last_phases[parity, part] for part in range(4)],
            parent_ref.at[parity],
            child_ref.at[parity],
            common_ref.at[parity],
        )
    chunk = out_ref.shape[0] // CHEB

    def leave(column):
        rows = pl.ds(pl.multiple_of(column * chunk, 8), chunk)
        return pltpu.make_async_copy(out_ref.at[rows, :], out_hbm.at[rows, :], out_sems.at[column])

    def column_step(column, _):
        children = [
            [tuple(work[child, row_of(level, s, column, part)] for part in range(2)) for s in range(CHEB)]
            for child in range(2)
        ]
        for parity in range(2):

            def store(row, real, imag, parity=parity):
                start = row_of(level, row, column, 0) * SLOTS + 2 * parity
                out_ref[pl.ds(start, OCT, stride=4), :] = real
                out_ref[pl.ds(start + 1, OCT, stride=4), :] = imag

            level_column(
                column, children, parent_ref.at[parity], child_ref.at[parity], common_ref.at[parity], store
            )
        leave(column).start()
        return 0

    lax.fori_loop(0, CHEB, column_step, 0, unroll=3)
    for column in range(CHEB):
        leave(column).wait()


def factor_scratch(count):
    return [
        pltpu.VMEM(count + (CHEB, 2, OCT, LANES), jnp.float32),
        pltpu.VMEM(count + (2, CHEB, 2, OCT, LANES), jnp.float32),
        pltpu.VMEM(count + (CHEB, OCT, LANES), jnp.float32),
    ]


def combine_even(me, blocks):
    vmem = pl.BlockSpec(memory_space=pltpu.VMEM)
    return pl.pallas_call(
        even_kernel,
        out_shape=[
            jax.ShapeDtypeStruct((WEIGHT_ROWS, OCT, LANES), jnp.float32),
            jax.ShapeDtypeStruct((4, OCT, LANES), jnp.float32),
        ],
        in_specs=[pl.BlockSpec(memory_space=pltpu.SMEM)] + [pl.BlockSpec(memory_space=pl.ANY)] * OCT,
        out_specs=[vmem, vmem],
        scratch_shapes=[
            pltpu.VMEM((OCT * ROWS, LANES), jnp.float32),
            *factor_scratch(()),
            pltpu.SemaphoreType.DMA((OCT,)),
        ],
        compiler_params=pltpu.CompilerParams(vmem_limit_bytes=16 * 2**20),
        cost_estimate=pl.CostEstimate(flops=40 * 2**20, bytes_accessed=12 * 2**20, transcendentals=0),
        name="combine_even",
    )(me, *blocks)


def combine_odd(me, even, blocks):
    hbm = pl.BlockSpec(memory_space=pltpu.HBM)
    anywhere = pl.BlockSpec(memory_space=pl.ANY)
    return pl.pallas_call(
        odd_kernel,
        out_shape=jax.ShapeDtypeStruct((WEIGHT_ROWS * SLOTS, LANES), jnp.float32),
        in_specs=[pl.BlockSpec(memory_space=pltpu.SMEM)] + [anywhere] * (2 + OCT),
        out_specs=hbm,
        scratch_shapes=[
            pltpu.VMEM((2, WEIGHT_ROWS, OCT, LANES), jnp.float32),
            pltpu.VMEM((2, 4, OCT, LANES), jnp.float32),
            pltpu.VMEM((OCT * ROWS, LANES), jnp.float32),
            pltpu.VMEM((WEIGHT_ROWS * SLOTS, LANES), jnp.float32),
            *factor_scratch((2,)),
            pltpu.SemaphoreType.DMA((OCT,)),
            pltpu.SemaphoreType.DMA((CHEB,)),
        ],
        compiler_params=pltpu.CompilerParams(vmem_limit_bytes=16 * 2**20),
        cost_estimate=pl.CostEstimate(flops=80 * 2**20, bytes_accessed=20 * 2**20, transcendentals=0),
        name="combine_odd",
    )(me, *even, *blocks)


def on_device(source_weights, wave_vectors, source_centers, phase_coef, phase_kind):
    devices = lax.axis_size("box")
    me = lax.axis_index("box").astype(jnp.int32)[None]
    direct = devices == SLOTS
    if not direct:
        me = jnp.zeros_like(me)
    weights = source_weights.reshape(2, POINTS, SLOTS, LANES).transpose(1, 2, 0, 3)
    weights, *sources = [
        pltpu.with_memory_space_constraint(operand, pltpu.HBM)
        for operand in (weights, phase_coef, wave_vectors, source_centers, phase_kind[None, :])
    ]
    blocks, phases = {}, None
    for steps in PACKS:
        if blocks:
            last = next(reversed(blocks))
            phases, blocks[last] = lax.optimization_barrier((phases, blocks[last]))
        packed, phases = pack(steps, me, weights, phases, sources)
        blocks.update(packed)
    blocks = {step: block.reshape(ROWS, LANES) for step, block in blocks.items()}
    if direct:

        def send(step):
            return lax.ppermute(blocks[step], "box", [(s, s ^ step) for s in range(SLOTS)])

        for step in EVEN_ORDER + ODD_ORDER:
            if step and step not in LATE:
                blocks[step] = send(step)
    else:
        whole = jnp.concatenate([blocks[step] for step in range(SLOTS)], axis=1)
        whole = lax.all_to_all(whole, "box", split_axis=1, concat_axis=1, tiled=True)
        blocks = [whole[:, s * LANES : (s + 1) * LANES] for s in range(SLOTS)]
    even = list(combine_even(me, [blocks[step] for step in EVEN_ORDER]))
    if direct:
        for step in LATE:
            even[1], blocks[step] = lax.optimization_barrier((even[1], blocks[step]))
            blocks[step] = send(step)
    rows = combine_odd(me, even, [blocks[step] for step in ODD_ORDER])
    return rows.reshape(POINTS, SLOTS, 2, LANES).transpose(2, 0, 1, 3).reshape(2, POINTS, SLOTS * LANES)


def solution(mesh):
    in_specs = (
        P(None, None, ("groups", "box")),
        P(None, None, ("groups", "box")),
        P(None, None, ("groups", "box")),
        P(),
        P(("groups", "box")),
    )
    out_specs = P(None, None, ("groups", "box"))
    return jax.shard_map(on_device, mesh=mesh, in_specs=in_specs, out_specs=out_specs, check_vma=False)
```

```python
import functools
import math

import numpy as np

import jax
import jax.numpy as jnp
from jax import lax
from jax.experimental import pallas as pl
from jax.experimental.pallas import tpu as pltpu
from jax.sharding import PartitionSpec as P

CHEB = 9
POINTS = CHEB * CHEB
KINDS = 4
LEVELS = 4
SLOTS = 1 << LEVELS
LANES = 128
WEIGHT_ROWS = 2 * POINTS
PHASE_ROWS = 4 * LEVELS
USED_ROWS = WEIGHT_ROWS + PHASE_ROWS
ROWS = (USED_ROWS + 7) // 8 * 8
OCT = SLOTS // 2
PACKS = ((8, 10, 12), (2, 4, 6), (14, 9, 15, 3, 5, 7), (11, 13, 1, 0))
EVEN_ORDER = (8, 10, 12, 2, 4, 6, 14, 0)
ODD_ORDER = (9, 15, 3, 5, 7, 11, 13, 1)
LATE = (13, 1)

NODES = np.cos(math.pi * (2.0 * np.arange(CHEB) + 1.0) / (2.0 * CHEB))
NODES[CHEB // 2] = 0.0


def interpolation_halves():
    targets = (NODES - 1.0) / 2.0
    matrix = np.ones((CHEB, CHEB))
    for t in range(CHEB):
        for m in range(CHEB):
            if m != t:
                matrix[t] *= (targets - NODES[m]) / (NODES[t] - NODES[m])
    return (matrix + matrix[::-1]) / 2.0, (matrix - matrix[::-1]) / 2.0


EVEN_HALF, ODD_HALF = interpolation_halves()

SIN_COEFS = (3.1415926401839673, -5.167710090328242, 2.5500776596583643, -0.5982921590176602, 0.0776594073245765)
COS_COEFS = (0.999999953466542, -4.934792858659144, 4.05841191384421, -1.3318801591805476, 0.219696794464285)


def cos_sin_turns(turns):
    rest = turns - jnp.round(turns)
    square = rest * rest
    sine = jnp.float32(SIN_COEFS[-1])
    cosine = jnp.float32(COS_COEFS[-1])
    for s, c in zip(SIN_COEFS[-2::-1], COS_COEFS[-2::-1]):
        sine = sine * square + s
        cosine = cosine * square + c
    sine = sine * rest
    twice = sine + sine
    return 1.0 - twice * sine, twice * cosine


def phase_rows(wave, center, kind, coef_ref):
    a = b = e = jnp.zeros(kind.shape, jnp.float32)
    for index in range(KINDS):
        chosen = kind == index
        a = jnp.where(chosen, coef_ref[index, 0], a)
        b = jnp.where(chosen, coef_ref[index, 1], b)
        e = jnp.where(chosen, coef_ref[index, 2], e)
    k1, k2 = wave
    x1, x2 = center
    level = lax.broadcasted_iota(jnp.int32, k1.shape, 0)
    half = jnp.full(k1.shape, 2.0**-LEVELS, jnp.float32)
    for index in range(1, LEVELS):
        half = jnp.where(level == index, 2.0 ** (index - LEVELS), half)
    scaled = b * k1
    root = a * jnp.sqrt(scaled * scaled + k2 * k2 + 1.0)
    bent = root * e
    constant = x1 * k1 + x2 * k2 + root + bent * x1 * x1
    constant = constant - jnp.round(constant)
    return constant, half * (k1 + 2.0 * bent * x1), half * half * bent, half * k2


def phase_kernel(coef_hbm, wave_hbm, center_hbm, kind_hbm, phases_ref, coef_ref, wave_ref, center_ref, kind_ref, sems):
    copies = [
        pltpu.make_async_copy(source, target, sems.at[index])
        for index, (source, target) in enumerate(
            ((coef_hbm, coef_ref), (wave_hbm, wave_ref), (center_hbm, center_ref), (kind_hbm, kind_ref))
        )
    ]
    for copy in copies:
        copy.start()
    for copy in copies:
        copy.wait()
    rows = phase_rows(
        (wave_ref[:, 0, :], wave_ref[:, 1, :]), (center_ref[:, 0, :], center_ref[:, 1, :]), kind_ref[...], coef_ref
    )
    for index, values in enumerate(rows):
        for level in range(LEVELS):
            row = index * LEVELS + level
            phases_ref[row // 2, row % 2, :] = values[level]


def pack_kernel(steps, first, me_ref, weights_hbm, *refs):
    if first:
        small, refs = refs[:4], refs[4:]
        outs, refs = refs[: len(steps)], refs[len(steps) :]
        phases_ref, block_sems, scratch = refs[0], refs[1], refs[2:]
    else:
        phases_ref, outs, block_sems = refs[0], refs[1 : 1 + len(steps)], refs[1 + len(steps)]
    slots = [me_ref[0] ^ step for step in steps]
    copies = [
        pltpu.make_async_copy(weights_hbm.at[:, slot], out.at[pl.ds(0, POINTS)], block_sems.at[index])
        for index, (slot, out) in enumerate(zip(slots, outs))
    ]
    for copy in copies:
        copy.start()
    if first:
        phase_kernel(*small, phases_ref, *scratch)
    for slot, out in zip(slots, outs):
        out[POINTS : USED_ROWS // 2] = phases_ref[:, :, pl.ds(pl.multiple_of(slot * LANES, LANES), LANES)]
        out[USED_ROWS // 2 :] = jnp.zeros(((ROWS - USED_ROWS) // 2, 2, LANES), jnp.float32)
    for copy in copies:
        copy.wait()


def pack(steps, me, weights, phases, sources):
    first = phases is None
    vmem = pl.BlockSpec(memory_space=pltpu.VMEM)
    hbm = pl.BlockSpec(memory_space=pltpu.HBM)
    out_shape = [jax.ShapeDtypeStruct((ROWS // 2, 2, LANES), jnp.float32) for _ in steps]
    scratch = [pltpu.SemaphoreType.DMA((len(steps),))]
    if first:
        boxes = sources[-1].shape[-1]
        out_shape.append(jax.ShapeDtypeStruct((PHASE_ROWS // 2, 2, boxes), jnp.float32))
        scratch += [pltpu.SMEM(sources[0].shape, jnp.float32)]
        scratch += [pltpu.VMEM(source.shape, source.dtype) for source in sources[1:]]
        scratch += [pltpu.SemaphoreType.DMA((len(sources),))]
    operands = sources if first else [phases]
    *arrays, last = pl.pallas_call(
        functools.partial(pack_kernel, steps, first),
        out_shape=out_shape,
        in_specs=[pl.BlockSpec(memory_space=pltpu.SMEM), hbm] + ([hbm] * len(sources) if first else [vmem]),
        out_specs=[vmem] * len(out_shape),
        scratch_shapes=scratch,
        compiler_params=pltpu.CompilerParams(vmem_limit_bytes=16 * 2**20),
        cost_estimate=pl.CostEstimate(flops=2**20, bytes_accessed=2**20, transcendentals=0),
        name="pack",
    )(me, weights, *operands)
    if first:
        phases = last
    else:
        arrays.append(last)
    return dict(zip(steps, arrays)), phases


def level_factors(level, phases, parent_ref, child_ref, common_ref):
    constant, linear, quadratic, other = phases
    if level % 2 == 0:
        split = lambda x: constant + x * (linear + x * quadratic)
        common = lambda x: x * other
    else:
        split = lambda x: constant + x * other
        common = lambda x: x * (linear + x * quadratic)
    for t in range(CHEB):
        node = float(NODES[t])
        parent_ref[t, 0], parent_ref[t, 1] = cos_sin_turns(split(node))
        for child in range(2):
            shifted = (node + 2.0 * child - 1.0) / 2.0
            child_ref[child, t, 0], child_ref[child, t, 1] = cos_sin_turns(split(shifted))
        cosine, sine = cos_sin_turns(common(node))
        common_ref[t] = cosine * cosine + sine * sine


def level_column(column, children, parent_ref, child_ref, common_ref, store):
    scaled = []
    for child in range(2):
        line = []
        for s in range(CHEB):
            real, imag = children[child][s]
            cosine, sine = child_ref[child, s, 0], child_ref[child, s, 1]
            line.append((cosine * real + sine * imag, cosine * imag - sine * real))
        scaled.append(line)
    halves = []
    for part in range(2):
        plus = [scaled[0][s][part] + scaled[1][CHEB - 1 - s][part] for s in range(CHEB)]
        minus = [scaled[0][s][part] - scaled[1][CHEB - 1 - s][part] for s in range(CHEB)]
        halves.append((plus, minus))
    common = common_ref[column]
    mid = CHEB // 2
    for t in range(mid + 1):
        sums = []
        for part in range(2):
            plus, minus = halves[part]
            even = plus[0] * float(EVEN_HALF[t, 0])
            for s in range(1, CHEB):
                even = even + plus[s] * float(EVEN_HALF[t, s])
            if t == mid:
                sums.append((even,))
                continue
            odd = minus[0] * float(ODD_HALF[t, 0])
            for s in range(1, CHEB):
                odd = odd + minus[s] * float(ODD_HALF[t, s])
            sums.append((even + odd, even - odd))
        for which, row in enumerate((t,) if t == mid else (t, CHEB - 1 - t)):
            real, imag = sums[0][which] * common, sums[1][which] * common
            cosine, sine = parent_ref[row, 0], parent_ref[row, 1]
            store(row, cosine * real - sine * imag, cosine * imag + sine * real)


def row_of(level, split, column, part):
    return part + 2 * (split * CHEB + column if level % 2 == 0 else column * CHEB + split)


def join_chips(me, blocks, order, held, sems, work, last_phases, factors):
    copies = []
    for index, step in enumerate(order):
        spot = pl.ds(pl.multiple_of(((me ^ step) // 2) * ROWS, 8), ROWS)
        copies.append(pltpu.make_async_copy(blocks[index], held.at[spot, :], sems.at[index]))
        copies[-1].start()
    for copy in copies:
        copy.wait()

    def received(row):
        return held[pl.ds(row, OCT, stride=ROWS), :]

    for part in range(4):
        last_phases[part] = received(WEIGHT_ROWS + part * LEVELS + LEVELS - 1)
    for level in range(LEVELS - 1):
        level_factors(level, [received(WEIGHT_ROWS + part * LEVELS + level) for part in range(4)], *factors)
        bit = OCT >> (level + 1)

        def column_step(column, _, level=level, bit=bit):
            upper = (lax.broadcasted_iota(jnp.int32, (OCT, LANES), 0) & bit) != 0
            children = [[], []]
            for s in range(CHEB):
                pairs = [[], []]
                for part in range(2):
                    row = row_of(level, s, column, part)
                    value = received(row) if level == 0 else work[row]
                    down = pltpu.roll(value, bit, 0)
                    up = down if 2 * bit == OCT else pltpu.roll(value, OCT - bit, 0)
                    pairs[0].append(jnp.where(upper, down, value))
                    pairs[1].append(jnp.where(upper, value, up))
                children[0].append(tuple(pairs[0]))
                children[1].append(tuple(pairs[1]))

            def store(row, real, imag):
                work[row_of(level, row, column, 0)] = real
                work[row_of(level, row, column, 1)] = imag

            level_column(column, children, *factors, store)
            return 0

        lax.fori_loop(0, CHEB, column_step, 0, unroll=3)


def even_kernel(me_ref, *refs):
    work, last_phases, held, parent_ref, child_ref, common_ref, sems = refs[OCT:]
    factors = (parent_ref, child_ref, common_ref)
    join_chips(me_ref[0], refs, EVEN_ORDER, held, sems, work, last_phases, factors)


def odd_kernel(me_ref, even_work, even_phases, *refs):
    out_hbm, work, last_phases, held, out_ref, parent_ref, child_ref, common_ref, sems, out_sems = refs[OCT:]
    me = me_ref[0]
    own = me % 2
    early = [
        pltpu.make_async_copy(even_work, work.at[own], out_sems.at[0]),
        pltpu.make_async_copy(even_phases, last_phases.at[own], out_sems.at[1]),
    ]
    for copy in early:
        copy.start()
    factors = [ref.at[0] for ref in (parent_ref, child_ref, common_ref)]
    join_chips(me, refs, ODD_ORDER, held, sems, work.at[1 - own], last_phases.at[1 - own], factors)
    for copy in early:
        copy.wait()

    level = LEVELS - 1
    for parity in range(2):
        level_factors(
            level,
            [last_phases[parity, part] for part in range(4)],
            parent_ref.at[parity],
            child_ref.at[parity],
            common_ref.at[parity],
        )
    chunk = out_ref.shape[0] // CHEB

    def leave(column):
        rows = pl.ds(pl.multiple_of(column * chunk, 8), chunk)
        return pltpu.make_async_copy(out_ref.at[rows, :], out_hbm.at[rows, :], out_sems.at[column])

    def column_step(column, _):
        children = [
            [tuple(work[child, row_of(level, s, column, part)] for part in range(2)) for s in range(CHEB)]
            for child in range(2)
        ]
        for parity in range(2):

            def store(row, real, imag, parity=parity):
                start = row_of(level, row, column, 0) * SLOTS + 2 * parity
                out_ref[pl.ds(start, OCT, stride=4), :] = real
                out_ref[pl.ds(start + 1, OCT, stride=4), :] = imag

            level_column(
                column, children, parent_ref.at[parity], child_ref.at[parity], common_ref.at[parity], store
            )
        leave(column).start()
        return 0

    lax.fori_loop(0, CHEB, column_step, 0, unroll=3)
    for column in range(CHEB):
        leave(column).wait()


def factor_scratch(count):
    return [
        pltpu.VMEM(count + (CHEB, 2, OCT, LANES), jnp.float32),
        pltpu.VMEM(count + (2, CHEB, 2, OCT, LANES), jnp.float32),
        pltpu.VMEM(count + (CHEB, OCT, LANES), jnp.float32),
    ]


def combine_even(me, blocks):
    vmem = pl.BlockSpec(memory_space=pltpu.VMEM)
    return pl.pallas_call(
        even_kernel,
        out_shape=[
            jax.ShapeDtypeStruct((WEIGHT_ROWS, OCT, LANES), jnp.float32),
            jax.ShapeDtypeStruct((4, OCT, LANES), jnp.float32),
        ],
        in_specs=[pl.BlockSpec(memory_space=pltpu.SMEM)] + [pl.BlockSpec(memory_space=pl.ANY)] * OCT,
        out_specs=[vmem, vmem],
        scratch_shapes=[
            pltpu.VMEM((OCT * ROWS, LANES), jnp.float32),
            *factor_scratch(()),
            pltpu.SemaphoreType.DMA((OCT,)),
        ],
        compiler_params=pltpu.CompilerParams(vmem_limit_bytes=16 * 2**20),
        cost_estimate=pl.CostEstimate(flops=40 * 2**20, bytes_accessed=12 * 2**20, transcendentals=0),
        name="combine_even",
    )(me, *blocks)


def combine_odd(me, even, blocks):
    hbm = pl.BlockSpec(memory_space=pltpu.HBM)
    anywhere = pl.BlockSpec(memory_space=pl.ANY)
    return pl.pallas_call(
        odd_kernel,
        out_shape=jax.ShapeDtypeStruct((WEIGHT_ROWS * SLOTS, LANES), jnp.float32),
        in_specs=[pl.BlockSpec(memory_space=pltpu.SMEM)] + [anywhere] * (2 + OCT),
        out_specs=hbm,
        scratch_shapes=[
            pltpu.VMEM((2, WEIGHT_ROWS, OCT, LANES), jnp.float32),
            pltpu.VMEM((2, 4, OCT, LANES), jnp.float32),
            pltpu.VMEM((OCT * ROWS, LANES), jnp.float32),
            pltpu.VMEM((WEIGHT_ROWS * SLOTS, LANES), jnp.float32),
            *factor_scratch((2,)),
            pltpu.SemaphoreType.DMA((OCT,)),
            pltpu.SemaphoreType.DMA((CHEB,)),
        ],
        compiler_params=pltpu.CompilerParams(vmem_limit_bytes=16 * 2**20),
        cost_estimate=pl.CostEstimate(flops=80 * 2**20, bytes_accessed=20 * 2**20, transcendentals=0),
        name="combine_odd",
    )(me, *even, *blocks)


def on_device(source_weights, wave_vectors, source_centers, phase_coef, phase_kind):
    devices = lax.axis_size("box")
    me = lax.axis_index("box").astype(jnp.int32)[None]
    direct = devices == SLOTS
    if not direct:
        me = jnp.zeros_like(me)
    weights = source_weights.reshape(2, POINTS, SLOTS, LANES).transpose(1, 2, 0, 3)
    weights, *sources = [
        pltpu.with_memory_space_constraint(operand, pltpu.HBM)
        for operand in (weights, phase_coef, wave_vectors, source_centers, phase_kind[None, :])
    ]
    blocks, phases = {}, None
    for steps in PACKS:
        if blocks:
            last = next(reversed(blocks))
            phases, blocks[last] = lax.optimization_barrier((phases, blocks[last]))
        packed, phases = pack(steps, me, weights, phases, sources)
        blocks.update(packed)
    blocks = {step: block.reshape(ROWS, LANES) for step, block in blocks.items()}
    if direct:

        def send(step):
            return lax.ppermute(blocks[step], "box", [(s, s ^ step) for s in range(SLOTS)])

        for step in EVEN_ORDER + ODD_ORDER:
            if step and step not in LATE:
                blocks[step] = send(step)
    else:
        whole = jnp.concatenate([blocks[step] for step in range(SLOTS)], axis=1)
        whole = lax.all_to_all(whole, "box", split_axis=1, concat_axis=1, tiled=True)
        blocks = [whole[:, s * LANES : (s + 1) * LANES] for s in range(SLOTS)]
    even = list(combine_even(me, [blocks[step] for step in EVEN_ORDER]))
    if direct:
        for step in LATE:
            even[1], blocks[step] = lax.optimization_barrier((even[1], blocks[step]))
            blocks[step] = send(step)
    rows = combine_odd(me, even, [blocks[step] for step in ODD_ORDER])
    return rows.reshape(POINTS, SLOTS, 2, LANES).transpose(2, 0, 1, 3).reshape(2, POINTS, SLOTS * LANES)


def solution(mesh):
    in_specs = (
        P(None, None, ("groups", "box")),
        P(None, None, ("groups", "box")),
        P(None, None, ("groups", "box")),
        P(),
        P(("groups", "box")),
    )
    out_specs = P(None, None, ("groups", "box"))
    return jax.shard_map(on_device, mesh=mesh, in_specs=in_specs, out_specs=out_specs, check_vma=False)
```

```python
import functools
import math

import numpy as np

import jax
import jax.numpy as jnp
from jax import lax
from jax.experimental import pallas as pl
from jax.experimental.pallas import tpu as pltpu
from jax.sharding import PartitionSpec as P

CHEB = 9
POINTS = CHEB * CHEB
KINDS = 4
LEVELS = 4
SLOTS = 1 << LEVELS
LANES = 128
WEIGHT_ROWS = 2 * POINTS
PHASE_ROWS = 4 * LEVELS
USED_ROWS = WEIGHT_ROWS + PHASE_ROWS
ROWS = (USED_ROWS + 7) // 8 * 8
OCT = SLOTS // 2
PACKS = ((12, 4, 6, 10), (2, 14, 9, 15, 3, 11, 8, 7, 13, 5, 1, 0))
SENDS = (8, 12, 4, 6, 2, 14, 15, 3, 11, 7, 13, 5, 1, 10, 9)
WAITS = {9: 4, 1: 11}
EVEN_ORDER = (8, 4, 2, 12, 10, 6, 14, 0)
ODD_ORDER = (1, 3, 5, 11, 9, 15, 13, 7)

NODES = np.cos(math.pi * (2.0 * np.arange(CHEB) + 1.0) / (2.0 * CHEB))
NODES[CHEB // 2] = 0.0


def interpolation_halves():
    targets = (NODES - 1.0) / 2.0
    matrix = np.ones((CHEB, CHEB))
    for t in range(CHEB):
        for m in range(CHEB):
            if m != t:
                matrix[t] *= (targets - NODES[m]) / (NODES[t] - NODES[m])
    return (matrix + matrix[::-1]) / 2.0, (matrix - matrix[::-1]) / 2.0


EVEN_HALF, ODD_HALF = interpolation_halves()

SIN_COEFS = (3.1415926401839673, -5.167710090328242, 2.5500776596583643, -0.5982921590176602, 0.0776594073245765)
COS_COEFS = (0.999999953466542, -4.934792858659144, 4.05841191384421, -1.3318801591805476, 0.219696794464285)


def cos_sin_turns(turns):
    rest = turns - jnp.round(turns)
    square = rest * rest
    sine = jnp.float32(SIN_COEFS[-1])
    cosine = jnp.float32(COS_COEFS[-1])
    for s, c in zip(SIN_COEFS[-2::-1], COS_COEFS[-2::-1]):
        sine = sine * square + s
        cosine = cosine * square + c
    sine = sine * rest
    twice = sine + sine
    return 1.0 - twice * sine, twice * cosine


def phase_rows(wave, center, kind, coef_ref):
    a = b = e = jnp.zeros(kind.shape, jnp.float32)
    for index in range(KINDS):
        chosen = kind == index
        a = jnp.where(chosen, coef_ref[index, 0], a)
        b = jnp.where(chosen, coef_ref[index, 1], b)
        e = jnp.where(chosen, coef_ref[index, 2], e)
    k1, k2 = wave
    x1, x2 = center
    level = lax.broadcasted_iota(jnp.int32, k1.shape, 0)
    half = jnp.full(k1.shape, 2.0**-LEVELS, jnp.float32)
    for index in range(1, LEVELS):
        half = jnp.where(level == index, 2.0 ** (index - LEVELS), half)
    scaled = b * k1
    root = a * jnp.sqrt(scaled * scaled + k2 * k2 + 1.0)
    bent = root * e
    constant = x1 * k1 + x2 * k2 + root + bent * x1 * x1
    constant = constant - jnp.round(constant)
    return constant, half * (k1 + 2.0 * bent * x1), half * half * bent, half * k2


def phase_kernel(coef_hbm, wave_hbm, center_hbm, kind_hbm, phases_ref, coef_ref, wave_ref, center_ref, kind_ref, sems):
    copies = [
        pltpu.make_async_copy(source, target, sems.at[index])
        for index, (source, target) in enumerate(
            ((coef_hbm, coef_ref), (wave_hbm, wave_ref), (center_hbm, center_ref), (kind_hbm, kind_ref))
        )
    ]
    for copy in copies:
        copy.start()
    for copy in copies:
        copy.wait()
    rows = phase_rows(
        (wave_ref[:, 0, :], wave_ref[:, 1, :]), (center_ref[:, 0, :], center_ref[:, 1, :]), kind_ref[...], coef_ref
    )
    for index, values in enumerate(rows):
        for level in range(LEVELS):
            row = index * LEVELS + level
            phases_ref[row // 2, row % 2, :] = values[level]


def pack_kernel(steps, first, me_ref, weights_hbm, *refs):
    if first:
        small, refs = refs[:4], refs[4:]
        outs, refs = refs[: len(steps)], refs[len(steps) :]
        phases_ref, block_sems, scratch = refs[0], refs[1], refs[2:]
    else:
        phases_ref, outs, block_sems = refs[0], refs[1 : 1 + len(steps)], refs[1 + len(steps)]
    slots = [me_ref[0] ^ step for step in steps]
    copies = [
        pltpu.make_async_copy(weights_hbm.at[:, slot], out.at[pl.ds(0, POINTS)], block_sems.at[index])
        for index, (slot, out) in enumerate(zip(slots, outs))
    ]
    for copy in copies:
        copy.start()
    if first:
        phase_kernel(*small, phases_ref, *scratch)
    for slot, out in zip(slots, outs):
        out[POINTS : USED_ROWS // 2] = phases_ref[:, :, pl.ds(pl.multiple_of(slot * LANES, LANES), LANES)]
        out[USED_ROWS // 2 :] = jnp.zeros(((ROWS - USED_ROWS) // 2, 2, LANES), jnp.float32)
    for copy in copies:
        copy.wait()


def pack(steps, me, weights, phases, sources):
    first = phases is None
    vmem = pl.BlockSpec(memory_space=pltpu.VMEM)
    hbm = pl.BlockSpec(memory_space=pltpu.HBM)
    out_shape = [jax.ShapeDtypeStruct((ROWS // 2, 2, LANES), jnp.float32) for _ in steps]
    scratch = [pltpu.SemaphoreType.DMA((len(steps),))]
    if first:
        boxes = sources[-1].shape[-1]
        out_shape.append(jax.ShapeDtypeStruct((PHASE_ROWS // 2, 2, boxes), jnp.float32))
        scratch += [pltpu.SMEM(sources[0].shape, jnp.float32)]
        scratch += [pltpu.VMEM(source.shape, source.dtype) for source in sources[1:]]
        scratch += [pltpu.SemaphoreType.DMA((len(sources),))]
    operands = sources if first else [phases]
    *arrays, last = pl.pallas_call(
        functools.partial(pack_kernel, steps, first),
        out_shape=out_shape,
        in_specs=[pl.BlockSpec(memory_space=pltpu.SMEM), hbm] + ([hbm] * len(sources) if first else [vmem]),
        out_specs=[vmem] * len(out_shape),
        scratch_shapes=scratch,
        compiler_params=pltpu.CompilerParams(vmem_limit_bytes=16 * 2**20),
        cost_estimate=pl.CostEstimate(flops=2**20, bytes_accessed=2**20, transcendentals=0),
        name="pack",
    )(me, weights, *operands)
    if first:
        phases = last
    else:
        arrays.append(last)
    return dict(zip(steps, arrays)), phases


def level_factors(level, phases, parent_ref, child_ref, common_ref):
    constant, linear, quadratic, other = phases
    if level % 2 == 0:
        split = lambda x: constant + x * (linear + x * quadratic)
        common = lambda x: x * other
    else:
        split = lambda x: constant + x * other
        common = lambda x: x * (linear + x * quadratic)
    for t in range(CHEB):
        node = float(NODES[t])
        parent_ref[t, 0], parent_ref[t, 1] = cos_sin_turns(split(node))
        for child in range(2):
            shifted = (node + 2.0 * child - 1.0) / 2.0
            child_ref[child, t, 0], child_ref[child, t, 1] = cos_sin_turns(split(shifted))
        cosine, sine = cos_sin_turns(common(node))
        common_ref[t] = cosine * cosine + sine * sine


def level_column(column, children, parent_ref, child_ref, common_ref, store):
    scaled = []
    for child in range(2):
        line = []
        for s in range(CHEB):
            real, imag = children[child][s]
            cosine, sine = child_ref[child, s, 0], child_ref[child, s, 1]
            line.append((cosine * real + sine * imag, cosine * imag - sine * real))
        scaled.append(line)
    halves = []
    for part in range(2):
        plus = [scaled[0][s][part] + scaled[1][CHEB - 1 - s][part] for s in range(CHEB)]
        minus = [scaled[0][s][part] - scaled[1][CHEB - 1 - s][part] for s in range(CHEB)]
        halves.append((plus, minus))
    common = common_ref[column]
    mid = CHEB // 2
    for t in range(mid + 1):
        sums = []
        for part in range(2):
            plus, minus = halves[part]
            even = plus[0] * float(EVEN_HALF[t, 0])
            for s in range(1, CHEB):
                even = even + plus[s] * float(EVEN_HALF[t, s])
            if t == mid:
                sums.append((even,))
                continue
            odd = minus[0] * float(ODD_HALF[t, 0])
            for s in range(1, CHEB):
                odd = odd + minus[s] * float(ODD_HALF[t, s])
            sums.append((even + odd, even - odd))
        for which, row in enumerate((t,) if t == mid else (t, CHEB - 1 - t)):
            real, imag = sums[0][which] * common, sums[1][which] * common
            cosine, sine = parent_ref[row, 0], parent_ref[row, 1]
            store(row, cosine * real - sine * imag, cosine * imag + sine * real)


def row_of(level, split, column, part):
    return part + 2 * (split * CHEB + column if level % 2 == 0 else column * CHEB + split)


def join_chips(me, blocks, order, held, sems, work, last_phases, factors):
    copies = []
    for index, step in enumerate(order):
        spot = pl.ds(pl.multiple_of(((me ^ step) // 2) * ROWS, 8), ROWS)
        copies.append(pltpu.make_async_copy(blocks[index], held.at[spot, :], sems.at[index]))
        copies[-1].start()
    for copy in copies:
        copy.wait()

    def received(row):
        return held[pl.ds(row, OCT, stride=ROWS), :]

    for part in range(4):
        last_phases[part] = received(WEIGHT_ROWS + part * LEVELS + LEVELS - 1)
    for level in range(LEVELS - 1):
        level_factors(level, [received(WEIGHT_ROWS + part * LEVELS + level) for part in range(4)], *factors)
        bit = OCT >> (level + 1)

        def column_step(column, _, level=level, bit=bit):
            upper = (lax.broadcasted_iota(jnp.int32, (OCT, LANES), 0) & bit) != 0
            children = [[], []]
            for s in range(CHEB):
                pairs = [[], []]
                for part in range(2):
                    row = row_of(level, s, column, part)
                    value = received(row) if level == 0 else work[row]
                    down = pltpu.roll(value, bit, 0)
                    up = down if 2 * bit == OCT else pltpu.roll(value, OCT - bit, 0)
                    pairs[0].append(jnp.where(upper, down, value))
                    pairs[1].append(jnp.where(upper, value, up))
                children[0].append(tuple(pairs[0]))
                children[1].append(tuple(pairs[1]))

            def store(row, real, imag):
                work[row_of(level, row, column, 0)] = real
                work[row_of(level, row, column, 1)] = imag

            level_column(column, children, *factors, store)
            return 0

        lax.fori_loop(0, CHEB, column_step, 0, unroll=3)


def even_kernel(me_ref, *refs):
    work, last_phases, held, parent_ref, child_ref, common_ref, sems = refs[OCT:]
    factors = (parent_ref, child_ref, common_ref)
    join_chips(me_ref[0], refs, EVEN_ORDER, held, sems, work, last_phases, factors)


def odd_kernel(me_ref, even_work, even_phases, *refs):
    out_hbm, work, last_phases, held, out_ref, parent_ref, child_ref, common_ref, sems, out_sems = refs[OCT:]
    me = me_ref[0]
    own = me % 2
    early = [
        pltpu.make_async_copy(even_work, work.at[own], out_sems.at[0]),
        pltpu.make_async_copy(even_phases, last_phases.at[own], out_sems.at[1]),
    ]
    for copy in early:
        copy.start()
    factors = [ref.at[0] for ref in (parent_ref, child_ref, common_ref)]
    join_chips(me, refs, ODD_ORDER, held, sems, work.at[1 - own], last_phases.at[1 - own], factors)
    for copy in early:
        copy.wait()

    level = LEVELS - 1
    for parity in range(2):
        level_factors(
            level,
            [last_phases[parity, part] for part in range(4)],
            parent_ref.at[parity],
            child_ref.at[parity],
            common_ref.at[parity],
        )
    chunk = out_ref.shape[0] // CHEB

    def leave(column):
        rows = pl.ds(pl.multiple_of(column * chunk, 8), chunk)
        return pltpu.make_async_copy(out_ref.at[rows, :], out_hbm.at[rows, :], out_sems.at[column])

    def column_step(column, _):
        children = [
            [tuple(work[child, row_of(level, s, column, part)] for part in range(2)) for s in range(CHEB)]
            for child in range(2)
        ]
        for parity in range(2):

            def store(row, real, imag, parity=parity):
                start = row_of(level, row, column, 0) * SLOTS + 2 * parity
                out_ref[pl.ds(start, OCT, stride=4), :] = real
                out_ref[pl.ds(start + 1, OCT, stride=4), :] = imag

            level_column(
                column, children, parent_ref.at[parity], child_ref.at[parity], common_ref.at[parity], store
            )
        leave(column).start()
        return 0

    lax.fori_loop(0, CHEB, column_step, 0, unroll=3)
    for column in range(CHEB):
        leave(column).wait()


def factor_scratch(count):
    return [
        pltpu.VMEM(count + (CHEB, 2, OCT, LANES), jnp.float32),
        pltpu.VMEM(count + (2, CHEB, 2, OCT, LANES), jnp.float32),
        pltpu.VMEM(count + (CHEB, OCT, LANES), jnp.float32),
    ]


def combine_even(me, blocks):
    vmem = pl.BlockSpec(memory_space=pltpu.VMEM)
    return pl.pallas_call(
        even_kernel,
        out_shape=[
            jax.ShapeDtypeStruct((WEIGHT_ROWS, OCT, LANES), jnp.float32),
            jax.ShapeDtypeStruct((4, OCT, LANES), jnp.float32),
        ],
        in_specs=[pl.BlockSpec(memory_space=pltpu.SMEM)] + [pl.BlockSpec(memory_space=pl.ANY)] * OCT,
        out_specs=[vmem, vmem],
        scratch_shapes=[
            pltpu.VMEM((OCT * ROWS, LANES), jnp.float32),
            *factor_scratch(()),
            pltpu.SemaphoreType.DMA((OCT,)),
        ],
        compiler_params=pltpu.CompilerParams(vmem_limit_bytes=16 * 2**20),
        cost_estimate=pl.CostEstimate(flops=40 * 2**20, bytes_accessed=12 * 2**20, transcendentals=0),
        name="combine_even",
    )(me, *blocks)


def combine_odd(me, even, blocks):
    hbm = pl.BlockSpec(memory_space=pltpu.HBM)
    anywhere = pl.BlockSpec(memory_space=pl.ANY)
    return pl.pallas_call(
        odd_kernel,
        out_shape=jax.ShapeDtypeStruct((WEIGHT_ROWS * SLOTS, LANES), jnp.float32),
        in_specs=[pl.BlockSpec(memory_space=pltpu.SMEM)] + [anywhere] * (2 + OCT),
        out_specs=hbm,
        scratch_shapes=[
            pltpu.VMEM((2, WEIGHT_ROWS, OCT, LANES), jnp.float32),
            pltpu.VMEM((2, 4, OCT, LANES), jnp.float32),
            pltpu.VMEM((OCT * ROWS, LANES), jnp.float32),
            pltpu.VMEM((WEIGHT_ROWS * SLOTS, LANES), jnp.float32),
            *factor_scratch((2,)),
            pltpu.SemaphoreType.DMA((OCT,)),
            pltpu.SemaphoreType.DMA((CHEB,)),
        ],
        compiler_params=pltpu.CompilerParams(vmem_limit_bytes=16 * 2**20),
        cost_estimate=pl.CostEstimate(flops=80 * 2**20, bytes_accessed=20 * 2**20, transcendentals=0),
        name="combine_odd",
    )(me, *even, *blocks)


def on_device(source_weights, wave_vectors, source_centers, phase_coef, phase_kind):
    devices = lax.axis_size("box")
    me = lax.axis_index("box").astype(jnp.int32)[None]
    direct = devices == SLOTS
    if not direct:
        me = jnp.zeros_like(me)
    weights = source_weights.reshape(2, POINTS, SLOTS, LANES).transpose(1, 2, 0, 3)
    weights, *sources = [
        pltpu.with_memory_space_constraint(operand, pltpu.HBM)
        for operand in (weights, phase_coef, wave_vectors, source_centers, phase_kind[None, :])
    ]
    blocks, phases = {}, None
    for steps in PACKS:
        if blocks:
            last = next(reversed(blocks))
            phases, blocks[last] = lax.optimization_barrier((phases, blocks[last]))
        packed, phases = pack(steps, me, weights, phases, sources)
        blocks.update(packed)
    blocks = {step: block.reshape(ROWS, LANES) for step, block in blocks.items()}
    if direct:
        for step in SENDS:
            if step in WAITS:
                earlier = WAITS[step]
                blocks[step], blocks[earlier] = lax.optimization_barrier((blocks[step], blocks[earlier]))
            blocks[step] = lax.ppermute(blocks[step], "box", [(s, s ^ step) for s in range(SLOTS)])
    else:
        whole = jnp.concatenate([blocks[step] for step in range(SLOTS)], axis=1)
        whole = lax.all_to_all(whole, "box", split_axis=1, concat_axis=1, tiled=True)
        blocks = [whole[:, s * LANES : (s + 1) * LANES] for s in range(SLOTS)]
    even = combine_even(me, [blocks[step] for step in EVEN_ORDER])
    rows = combine_odd(me, even, [blocks[step] for step in ODD_ORDER])
    return rows.reshape(POINTS, SLOTS, 2, LANES).transpose(2, 0, 1, 3).reshape(2, POINTS, SLOTS * LANES)


def solution(mesh):
    in_specs = (
        P(None, None, ("groups", "box")),
        P(None, None, ("groups", "box")),
        P(None, None, ("groups", "box")),
        P(),
        P(("groups", "box")),
    )
    out_specs = P(None, None, ("groups", "box"))
    return jax.shard_map(on_device, mesh=mesh, in_specs=in_specs, out_specs=out_specs, check_vma=False)
```

```python
import functools
import math

import numpy as np

import jax
import jax.numpy as jnp
from jax import lax
from jax.experimental import pallas as pl
from jax.experimental.pallas import tpu as pltpu
from jax.sharding import PartitionSpec as P

CHEB = 9
POINTS = CHEB * CHEB
KINDS = 4
LEVELS = 4
SLOTS = 1 << LEVELS
LANES = 128
WEIGHT_ROWS = 2 * POINTS
PHASE_ROWS = 4 * LEVELS
ROWS = WEIGHT_ROWS + PHASE_ROWS
OCT = SLOTS // 2
PACKS = ((12, 4, 6, 10), (2, 14, 9, 15, 3, 11, 8, 7, 13, 5, 1, 0))
SENDS = (8, 12, 4, 6, 2, 14, 15, 3, 11, 7, 13, 5, 1, 10, 9)
WAITS = {9: 4, 1: 11}
EVEN_ORDER = (8, 4, 2, 12, 10, 6, 14, 0)
ODD_ORDER = (1, 3, 5, 11, 9, 15, 13, 7)

NODES = np.cos(math.pi * (2.0 * np.arange(CHEB) + 1.0) / (2.0 * CHEB))
NODES[CHEB // 2] = 0.0


def interpolation_halves():
    targets = (NODES - 1.0) / 2.0
    matrix = np.ones((CHEB, CHEB))
    for t in range(CHEB):
        for m in range(CHEB):
            if m != t:
                matrix[t] *= (targets - NODES[m]) / (NODES[t] - NODES[m])
    return (matrix + matrix[::-1]) / 2.0, (matrix - matrix[::-1]) / 2.0


EVEN_HALF, ODD_HALF = interpolation_halves()

SIN_COEFS = (3.1415926401839673, -5.167710090328242, 2.5500776596583643, -0.5982921590176602, 0.0776594073245765)
COS_COEFS = (0.999999953466542, -4.934792858659144, 4.05841191384421, -1.3318801591805476, 0.219696794464285)


def cos_sin_turns(turns):
    rest = turns - jnp.round(turns)
    square = rest * rest
    sine = jnp.float32(SIN_COEFS[-1])
    cosine = jnp.float32(COS_COEFS[-1])
    for s, c in zip(SIN_COEFS[-2::-1], COS_COEFS[-2::-1]):
        sine = sine * square + s
        cosine = cosine * square + c
    sine = sine * rest
    twice = sine + sine
    return 1.0 - twice * sine, twice * cosine


def phase_rows(wave, center, kind, coef_ref):
    a = b = e = jnp.zeros(kind.shape, jnp.float32)
    for index in range(KINDS):
        chosen = kind == index
        a = jnp.where(chosen, coef_ref[index, 0], a)
        b = jnp.where(chosen, coef_ref[index, 1], b)
        e = jnp.where(chosen, coef_ref[index, 2], e)
    k1, k2 = wave
    x1, x2 = center
    level = lax.broadcasted_iota(jnp.int32, k1.shape, 0)
    half = jnp.full(k1.shape, 2.0**-LEVELS, jnp.float32)
    for index in range(1, LEVELS):
        half = jnp.where(level == index, 2.0 ** (index - LEVELS), half)
    scaled = b * k1
    root = a * jnp.sqrt(scaled * scaled + k2 * k2 + 1.0)
    bent = root * e
    constant = x1 * k1 + x2 * k2 + root + bent * x1 * x1
    constant = constant - jnp.round(constant)
    return constant, half * (k1 + 2.0 * bent * x1), half * half * bent, half * k2


def phase_kernel(coef_hbm, wave_hbm, center_hbm, kind_hbm, phases_ref, coef_ref, wave_ref, center_ref, kind_ref, sems):
    copies = [
        pltpu.make_async_copy(source, target, sems.at[index])
        for index, (source, target) in enumerate(
            ((coef_hbm, coef_ref), (wave_hbm, wave_ref), (center_hbm, center_ref), (kind_hbm, kind_ref))
        )
    ]
    for copy in copies:
        copy.start()
    for copy in copies:
        copy.wait()
    rows = phase_rows(
        (wave_ref[:, 0, :], wave_ref[:, 1, :]), (center_ref[:, 0, :], center_ref[:, 1, :]), kind_ref[...], coef_ref
    )
    for index, values in enumerate(rows):
        for level in range(LEVELS):
            row = index * LEVELS + level
            phases_ref[row // 2, row % 2, :] = values[level]


def pack_kernel(steps, first, me_ref, weights_hbm, *refs):
    if first:
        small, refs = refs[:4], refs[4:]
        outs, refs = refs[: len(steps)], refs[len(steps) :]
        phases_ref, block_sems, scratch = refs[0], refs[1], refs[2:]
    else:
        phases_ref, outs, block_sems = refs[0], refs[1 : 1 + len(steps)], refs[1 + len(steps)]
    slots = [me_ref[0] ^ step for step in steps]
    copies = [
        pltpu.make_async_copy(weights_hbm.at[:, slot], out.at[pl.ds(0, POINTS)], block_sems.at[index])
        for index, (slot, out) in enumerate(zip(slots, outs))
    ]
    for copy in copies:
        copy.start()
    if first:
        phase_kernel(*small, phases_ref, *scratch)
    for slot, out in zip(slots, outs):
        out[POINTS:] = phases_ref[:, :, pl.ds(pl.multiple_of(slot * LANES, LANES), LANES)]
    for copy in copies:
        copy.wait()


def pack(steps, me, weights, phases, sources):
    first = phases is None
    vmem = pl.BlockSpec(memory_space=pltpu.VMEM)
    hbm = pl.BlockSpec(memory_space=pltpu.HBM)
    out_shape = [jax.ShapeDtypeStruct((ROWS // 2, 2, LANES), jnp.float32) for _ in steps]
    scratch = [pltpu.SemaphoreType.DMA((len(steps),))]
    if first:
        boxes = sources[-1].shape[-1]
        out_shape.append(jax.ShapeDtypeStruct((PHASE_ROWS // 2, 2, boxes), jnp.float32))
        scratch += [pltpu.SMEM(sources[0].shape, jnp.float32)]
        scratch += [pltpu.VMEM(source.shape, source.dtype) for source in sources[1:]]
        scratch += [pltpu.SemaphoreType.DMA((len(sources),))]
    operands = sources if first else [phases]
    *arrays, last = pl.pallas_call(
        functools.partial(pack_kernel, steps, first),
        out_shape=out_shape,
        in_specs=[pl.BlockSpec(memory_space=pltpu.SMEM), hbm] + ([hbm] * len(sources) if first else [vmem]),
        out_specs=[vmem] * len(out_shape),
        scratch_shapes=scratch,
        compiler_params=pltpu.CompilerParams(vmem_limit_bytes=16 * 2**20),
        cost_estimate=pl.CostEstimate(flops=2**20, bytes_accessed=2**20, transcendentals=0),
        name="pack",
    )(me, weights, *operands)
    if first:
        phases = last
    else:
        arrays.append(last)
    return dict(zip(steps, arrays)), phases


def turn_both_ways(base, step):
    cc, ss = base[0] * step[0], base[1] * step[1]
    sc, cs = base[1] * step[0], base[0] * step[1]
    return (cc - ss, sc + cs), (cc + ss, sc - cs)


def level_factors(level, phases, parent_ref, child_ref, common_ref):
    constant, linear, quadratic, other = phases
    mid = CHEB // 2

    def put(ref, index, pair):
        ref[index + (0,)], ref[index + (1,)] = pair

    def norm(turns):
        cosine, sine = cos_sin_turns(turns)
        return cosine * cosine + sine * sine

    common_ref[mid] = jnp.ones_like(constant)
    for t in range(mid):
        node = float(NODES[t])
        if level % 2 == 0:
            common_ref[t] = common_ref[CHEB - 1 - t] = norm(node * other)
        else:
            common_ref[t] = norm(node * (linear + node * quadratic))
            common_ref[CHEB - 1 - t] = norm(node * (node * quadratic - linear))
    if level % 2 == 0:
        for t in range(CHEB):
            node = float(NODES[t])
            put(parent_ref, (t,), cos_sin_turns(constant + node * (linear + node * quadratic)))
            for child in range(2):
                shifted = (node + 2.0 * child - 1.0) / 2.0
                pair = cos_sin_turns(constant + shifted * (linear + shifted * quadratic))
                put(child_ref, (child, t), pair)
        return
    center = cos_sin_turns(constant)
    centers = [cos_sin_turns(constant + (child - 0.5) * other) for child in range(2)]
    put(parent_ref, (mid,), center)
    for child in range(2):
        put(child_ref, (child, mid), centers[child])
    for t in range(mid):
        half_step = cos_sin_turns((0.5 * float(NODES[t])) * other)
        for child in range(2):
            forth, back = turn_both_ways(centers[child], half_step)
            put(child_ref, (child, t), forth)
            put(child_ref, (child, CHEB - 1 - t), back)
        twice = half_step[1] + half_step[1]
        full_step = (1.0 - twice * half_step[1], twice * half_step[0])
        forth, back = turn_both_ways(center, full_step)
        put(parent_ref, (t,), forth)
        put(parent_ref, (CHEB - 1 - t,), back)


def level_column(column, children, parent_ref, child_ref, common_ref, store):
    scaled = []
    for child in range(2):
        line = []
        for s in range(CHEB):
            real, imag = children[child][s]
            cosine, sine = child_ref[child, s, 0], child_ref[child, s, 1]
            line.append((cosine * real + sine * imag, cosine * imag - sine * real))
        scaled.append(line)
    halves = []
    for part in range(2):
        plus = [scaled[0][s][part] + scaled[1][CHEB - 1 - s][part] for s in range(CHEB)]
        minus = [scaled[0][s][part] - scaled[1][CHEB - 1 - s][part] for s in range(CHEB)]
        halves.append((plus, minus))
    common = common_ref[column]
    mid = CHEB // 2
    for t in range(mid + 1):
        sums = []
        for part in range(2):
            plus, minus = halves[part]
            even = plus[0] * float(EVEN_HALF[t, 0])
            for s in range(1, CHEB):
                even = even + plus[s] * float(EVEN_HALF[t, s])
            if t == mid:
                sums.append((even,))
                continue
            odd = minus[0] * float(ODD_HALF[t, 0])
            for s in range(1, CHEB):
                odd = odd + minus[s] * float(ODD_HALF[t, s])
            sums.append((even + odd, even - odd))
        for which, row in enumerate((t,) if t == mid else (t, CHEB - 1 - t)):
            real, imag = sums[0][which] * common, sums[1][which] * common
            cosine, sine = parent_ref[row, 0], parent_ref[row, 1]
            store(row, cosine * real - sine * imag, cosine * imag + sine * real)


def row_of(level, split, column, part):
    return part + 2 * (split * CHEB + column if level % 2 == 0 else column * CHEB + split)


def join_chips(me, blocks, order, held, sems, work, last_phases, factors):
    copies = []
    for index, step in enumerate(order):
        spot = pl.ds(((me ^ step) // 2) * (ROWS // 2), ROWS // 2)
        copies.append(pltpu.make_async_copy(blocks[index], held.at[spot], sems.at[index]))
        copies[-1].start()
    for copy in copies:
        copy.wait()
    rows = held.reshape(OCT * ROWS, LANES)

    def received(row):
        return rows[pl.ds(row, OCT, stride=ROWS), :]

    for part in range(4):
        last_phases[part] = received(WEIGHT_ROWS + part * LEVELS + LEVELS - 1)
    for level in range(LEVELS - 1):
        level_factors(level, [received(WEIGHT_ROWS + part * LEVELS + level) for part in range(4)], *factors)
        bit = OCT >> (level + 1)

        def column_step(column, _, level=level, bit=bit):
            upper = (lax.broadcasted_iota(jnp.int32, (OCT, LANES), 0) & bit) != 0
            children = [[], []]
            for s in range(CHEB):
                pairs = [[], []]
                for part in range(2):
                    row = row_of(level, s, column, part)
                    value = received(row) if level == 0 else work[row]
                    down = pltpu.roll(value, bit, 0)
                    up = down if 2 * bit == OCT else pltpu.roll(value, OCT - bit, 0)
                    pairs[0].append(jnp.where(upper, down, value))
                    pairs[1].append(jnp.where(upper, value, up))
                children[0].append(tuple(pairs[0]))
                children[1].append(tuple(pairs[1]))

            def store(row, real, imag):
                work[row_of(level, row, column, 0)] = real
                work[row_of(level, row, column, 1)] = imag

            level_column(column, children, *factors, store)
            return 0

        lax.fori_loop(0, CHEB, column_step, 0, unroll=3)


def even_kernel(me_ref, *refs):
    work, last_phases, held, parent_ref, child_ref, common_ref, sems = refs[OCT:]
    factors = (parent_ref, child_ref, common_ref)
    join_chips(me_ref[0], refs, EVEN_ORDER, held, sems, work, last_phases, factors)


def odd_kernel(me_ref, even_work, even_phases, *refs):
    out_hbm, work, last_phases, held, out_ref, parent_ref, child_ref, common_ref, sems, out_sems = refs[OCT:]
    me = me_ref[0]
    own = me % 2
    early = [
        pltpu.make_async_copy(even_work, work.at[own], out_sems.at[0]),
        pltpu.make_async_copy(even_phases, last_phases.at[own], out_sems.at[1]),
    ]
    for copy in early:
        copy.start()
    factors = [ref.at[0] for ref in (parent_ref, child_ref, common_ref)]
    join_chips(me, refs, ODD_ORDER, held, sems, work.at[1 - own], last_phases.at[1 - own], factors)
    for copy in early:
        copy.wait()

    level = LEVELS - 1
    for parity in range(2):
        level_factors(
            level,
            [last_phases[parity, part] for part in range(4)],
            parent_ref.at[parity],
            child_ref.at[parity],
            common_ref.at[parity],
        )
    chunk = out_ref.shape[0] // CHEB

    def leave(column):
        rows = pl.ds(pl.multiple_of(column * chunk, 8), chunk)
        return pltpu.make_async_copy(out_ref.at[rows, :], out_hbm.at[rows, :], out_sems.at[column])

    def column_step(column, _):
        children = [
            [tuple(work[child, row_of(level, s, column, part)] for part in range(2)) for s in range(CHEB)]
            for child in range(2)
        ]
        for parity in range(2):

            def store(row, real, imag, parity=parity):
                start = row_of(level, row, column, 0) * SLOTS + 2 * parity
                out_ref[pl.ds(start, OCT, stride=4), :] = real
                out_ref[pl.ds(start + 1, OCT, stride=4), :] = imag

            level_column(
                column, children, parent_ref.at[parity], child_ref.at[parity], common_ref.at[parity], store
            )
        leave(column).start()
        return 0

    lax.fori_loop(0, CHEB, column_step, 0, unroll=3)
    for column in range(CHEB):
        leave(column).wait()


def factor_scratch(count):
    return [
        pltpu.VMEM(count + (CHEB, 2, OCT, LANES), jnp.float32),
        pltpu.VMEM(count + (2, CHEB, 2, OCT, LANES), jnp.float32),
        pltpu.VMEM(count + (CHEB, OCT, LANES), jnp.float32),
    ]


def combine_even(me, blocks):
    vmem = pl.BlockSpec(memory_space=pltpu.VMEM)
    return pl.pallas_call(
        even_kernel,
        out_shape=[
            jax.ShapeDtypeStruct((WEIGHT_ROWS, OCT, LANES), jnp.float32),
            jax.ShapeDtypeStruct((4, OCT, LANES), jnp.float32),
        ],
        in_specs=[pl.BlockSpec(memory_space=pltpu.SMEM)] + [pl.BlockSpec(memory_space=pl.ANY)] * OCT,
        out_specs=[vmem, vmem],
        scratch_shapes=[
            pltpu.VMEM((OCT * ROWS // 2, 2, LANES), jnp.float32),
            *factor_scratch(()),
            pltpu.SemaphoreType.DMA((OCT,)),
        ],
        compiler_params=pltpu.CompilerParams(vmem_limit_bytes=16 * 2**20),
        cost_estimate=pl.CostEstimate(flops=40 * 2**20, bytes_accessed=12 * 2**20, transcendentals=0),
        name="combine_even",
    )(me, *blocks)


def combine_odd(me, even, blocks):
    hbm = pl.BlockSpec(memory_space=pltpu.HBM)
    anywhere = pl.BlockSpec(memory_space=pl.ANY)
    return pl.pallas_call(
        odd_kernel,
        out_shape=jax.ShapeDtypeStruct((WEIGHT_ROWS * SLOTS, LANES), jnp.float32),
        in_specs=[pl.BlockSpec(memory_space=pltpu.SMEM)] + [anywhere] * (2 + OCT),
        out_specs=hbm,
        scratch_shapes=[
            pltpu.VMEM((2, WEIGHT_ROWS, OCT, LANES), jnp.float32),
            pltpu.VMEM((2, 4, OCT, LANES), jnp.float32),
            pltpu.VMEM((OCT * ROWS // 2, 2, LANES), jnp.float32),
            pltpu.VMEM((WEIGHT_ROWS * SLOTS, LANES), jnp.float32),
            *factor_scratch((2,)),
            pltpu.SemaphoreType.DMA((OCT,)),
            pltpu.SemaphoreType.DMA((CHEB,)),
        ],
        compiler_params=pltpu.CompilerParams(vmem_limit_bytes=16 * 2**20),
        cost_estimate=pl.CostEstimate(flops=80 * 2**20, bytes_accessed=20 * 2**20, transcendentals=0),
        name="combine_odd",
    )(me, *even, *blocks)


def on_device(source_weights, wave_vectors, source_centers, phase_coef, phase_kind):
    devices = lax.axis_size("box")
    me = lax.axis_index("box").astype(jnp.int32)[None]
    direct = devices == SLOTS
    if not direct:
        me = jnp.zeros_like(me)
    weights = source_weights.reshape(2, POINTS, SLOTS, LANES).transpose(1, 2, 0, 3)
    weights, *sources = [
        pltpu.with_memory_space_constraint(operand, pltpu.HBM)
        for operand in (weights, phase_coef, wave_vectors, source_centers, phase_kind[None, :])
    ]
    blocks, phases = {}, None
    for steps in PACKS:
        if blocks:
            last = next(reversed(blocks))
            phases, blocks[last] = lax.optimization_barrier((phases, blocks[last]))
        packed, phases = pack(steps, me, weights, phases, sources)
        blocks.update(packed)
    if direct:
        for step in SENDS:
            if step in WAITS:
                earlier = WAITS[step]
                blocks[step], blocks[earlier] = lax.optimization_barrier((blocks[step], blocks[earlier]))
            blocks[step] = lax.ppermute(blocks[step], "box", [(s, s ^ step) for s in range(SLOTS)])
    else:
        whole = jnp.concatenate([blocks[step] for step in range(SLOTS)], axis=2)
        whole = lax.all_to_all(whole, "box", split_axis=2, concat_axis=2, tiled=True)
        blocks = [whole[:, :, s * LANES : (s + 1) * LANES] for s in range(SLOTS)]
    even = combine_even(me, [blocks[step] for step in EVEN_ORDER])
    rows = combine_odd(me, even, [blocks[step] for step in ODD_ORDER])
    return rows.reshape(POINTS, SLOTS, 2, LANES).transpose(2, 0, 1, 3).reshape(2, POINTS, SLOTS * LANES)


def solution(mesh):
    in_specs = (
        P(None, None, ("groups", "box")),
        P(None, None, ("groups", "box")),
        P(None, None, ("groups", "box")),
        P(),
        P(("groups", "box")),
    )
    out_specs = P(None, None, ("groups", "box"))
    return jax.shard_map(on_device, mesh=mesh, in_specs=in_specs, out_specs=out_specs, check_vma=False)
```

```python
import functools
import math

import numpy as np

import jax
import jax.numpy as jnp
from jax import lax
from jax.experimental import pallas as pl
from jax.experimental.pallas import tpu as pltpu
from jax.sharding import PartitionSpec as P

CHEB = 9
POINTS = CHEB * CHEB
KINDS = 4
LEVELS = 4
SLOTS = 1 << LEVELS
LANES = 128
WEIGHT_ROWS = 2 * POINTS
PHASE_ROWS = 4 * LEVELS
ROWS = WEIGHT_ROWS + PHASE_ROWS
OCT = SLOTS // 2
PACKS = ((14, 8, 1), (6, 12, 2, 4, 10, 15, 7), (9, 11, 13), (5, 3, 0))
SENDS = (14, 8, 6, 12, 2, 4, 10, 15, 7, 9, 11, 13, 5, 3, 1)
WAITS = {2: 14, 1: 9}
SEEN = (15,)
EVEN_ORDER = (14, 8, 6, 12, 2, 4, 10, 0)
ODD_ORDER = (9, 7, 3, 15, 1, 13, 11, 5)

NODES = np.cos(math.pi * (2.0 * np.arange(CHEB) + 1.0) / (2.0 * CHEB))
NODES[CHEB // 2] = 0.0


def interpolation_halves():
    targets = (NODES - 1.0) / 2.0
    matrix = np.ones((CHEB, CHEB))
    for t in range(CHEB):
        for m in range(CHEB):
            if m != t:
                matrix[t] *= (targets - NODES[m]) / (NODES[t] - NODES[m])
    return (matrix + matrix[::-1]) / 2.0, (matrix - matrix[::-1]) / 2.0


EVEN_HALF, ODD_HALF = interpolation_halves()

SIN_COEFS = (3.1415926401839673, -5.167710090328242, 2.5500776596583643, -0.5982921590176602, 0.0776594073245765)
COS_COEFS = (0.999999953466542, -4.934792858659144, 4.05841191384421, -1.3318801591805476, 0.219696794464285)


def cos_sin_turns(turns):
    rest = turns - jnp.round(turns)
    square = rest * rest
    sine = jnp.float32(SIN_COEFS[-1])
    cosine = jnp.float32(COS_COEFS[-1])
    for s, c in zip(SIN_COEFS[-2::-1], COS_COEFS[-2::-1]):
        sine = sine * square + s
        cosine = cosine * square + c
    sine = sine * rest
    twice = sine + sine
    return 1.0 - twice * sine, twice * cosine


def phase_rows(wave, center, kind, coef_ref):
    a = b = e = jnp.zeros(kind.shape, jnp.float32)
    for index in range(KINDS):
        chosen = kind == index
        a = jnp.where(chosen, coef_ref[index, 0], a)
        b = jnp.where(chosen, coef_ref[index, 1], b)
        e = jnp.where(chosen, coef_ref[index, 2], e)
    k1, k2 = wave
    x1, x2 = center
    level = lax.broadcasted_iota(jnp.int32, k1.shape, 0)
    half = jnp.full(k1.shape, 2.0**-LEVELS, jnp.float32)
    for index in range(1, LEVELS):
        half = jnp.where(level == index, 2.0 ** (index - LEVELS), half)
    scaled = b * k1
    root = a * jnp.sqrt(scaled * scaled + k2 * k2 + 1.0)
    bent = root * e
    constant = x1 * k1 + x2 * k2 + root + bent * x1 * x1
    constant = constant - jnp.round(constant)
    return constant, half * (k1 + 2.0 * bent * x1), half * half * bent, half * k2


def phase_kernel(coef_hbm, wave_hbm, center_hbm, kind_hbm, phases_ref, coef_ref, wave_ref, center_ref, kind_ref, sems):
    copies = [
        pltpu.make_async_copy(source, target, sems.at[index])
        for index, (source, target) in enumerate(
            ((coef_hbm, coef_ref), (wave_hbm, wave_ref), (center_hbm, center_ref), (kind_hbm, kind_ref))
        )
    ]
    for copy in copies:
        copy.start()
    for copy in copies:
        copy.wait()
    rows = phase_rows(
        (wave_ref[:, 0, :], wave_ref[:, 1, :]), (center_ref[:, 0, :], center_ref[:, 1, :]), kind_ref[...], coef_ref
    )
    for index, values in enumerate(rows):
        for level in range(LEVELS):
            row = index * LEVELS + level
            phases_ref[row // 2, row % 2, :] = values[level]


def pack_kernel(steps, first, me_ref, weights_hbm, *refs):
    if first:
        small, refs = refs[:4], refs[4:]
        outs, refs = refs[: len(steps)], refs[len(steps) :]
        phases_ref, block_sems, scratch = refs[0], refs[1], refs[2:]
    else:
        phases_ref, outs, block_sems = refs[0], refs[1 : 1 + len(steps)], refs[1 + len(steps)]
    slots = [me_ref[0] ^ step for step in steps]
    copies = [
        pltpu.make_async_copy(weights_hbm.at[:, slot], out.at[pl.ds(0, POINTS)], block_sems.at[index])
        for index, (slot, out) in enumerate(zip(slots, outs))
    ]
    for copy in copies:
        copy.start()
    if first:
        phase_kernel(*small, phases_ref, *scratch)
    for slot, out in zip(slots, outs):
        out[POINTS:] = phases_ref[:, :, pl.ds(pl.multiple_of(slot * LANES, LANES), LANES)]
    for copy in copies:
        copy.wait()


def pack(steps, me, weights, phases, sources):
    first = phases is None
    vmem = pl.BlockSpec(memory_space=pltpu.VMEM)
    hbm = pl.BlockSpec(memory_space=pltpu.HBM)
    out_shape = [jax.ShapeDtypeStruct((ROWS // 2, 2, LANES), jnp.float32) for _ in steps]
    scratch = [pltpu.SemaphoreType.DMA((len(steps),))]
    if first:
        boxes = sources[-1].shape[-1]
        out_shape.append(jax.ShapeDtypeStruct((PHASE_ROWS // 2, 2, boxes), jnp.float32))
        scratch += [pltpu.SMEM(sources[0].shape, jnp.float32)]
        scratch += [pltpu.VMEM(source.shape, source.dtype) for source in sources[1:]]
        scratch += [pltpu.SemaphoreType.DMA((len(sources),))]
    operands = sources if first else [phases]
    *arrays, last = pl.pallas_call(
        functools.partial(pack_kernel, steps, first),
        out_shape=out_shape,
        in_specs=[pl.BlockSpec(memory_space=pltpu.SMEM), hbm] + ([hbm] * len(sources) if first else [vmem]),
        out_specs=[vmem] * len(out_shape),
        scratch_shapes=scratch,
        compiler_params=pltpu.CompilerParams(vmem_limit_bytes=16 * 2**20),
        cost_estimate=pl.CostEstimate(flops=2**20, bytes_accessed=2**20, transcendentals=0),
        name="pack",
    )(me, weights, *operands)
    if first:
        phases = last
    else:
        arrays.append(last)
    return dict(zip(steps, arrays)), phases


def turn_both_ways(base, step):
    cc, ss = base[0] * step[0], base[1] * step[1]
    sc, cs = base[1] * step[0], base[0] * step[1]
    return (cc - ss, sc + cs), (cc + ss, sc - cs)


def level_factors(level, phases, parent_ref, child_ref, common_ref):
    constant, linear, quadratic, other = phases
    mid = CHEB // 2

    def put(ref, index, pair):
        ref[index + (0,)], ref[index + (1,)] = pair

    def norm(turns):
        cosine, sine = cos_sin_turns(turns)
        return cosine * cosine + sine * sine

    common_ref[mid] = jnp.ones_like(constant)
    for t in range(mid):
        node = float(NODES[t])
        if level % 2 == 0:
            common_ref[t] = common_ref[CHEB - 1 - t] = norm(node * other)
        else:
            common_ref[t] = norm(node * (linear + node * quadratic))
            common_ref[CHEB - 1 - t] = norm(node * (node * quadratic - linear))
    if level % 2 == 0:
        for t in range(CHEB):
            node = float(NODES[t])
            put(parent_ref, (t,), cos_sin_turns(constant + node * (linear + node * quadratic)))
            for child in range(2):
                shifted = (node + 2.0 * child - 1.0) / 2.0
                pair = cos_sin_turns(constant + shifted * (linear + shifted * quadratic))
                put(child_ref, (child, t), pair)
        return
    center = cos_sin_turns(constant)
    centers = [cos_sin_turns(constant + (child - 0.5) * other) for child in range(2)]
    put(parent_ref, (mid,), center)
    for child in range(2):
        put(child_ref, (child, mid), centers[child])
    for t in range(mid):
        half_step = cos_sin_turns((0.5 * float(NODES[t])) * other)
        for child in range(2):
            forth, back = turn_both_ways(centers[child], half_step)
            put(child_ref, (child, t), forth)
            put(child_ref, (child, CHEB - 1 - t), back)
        twice = half_step[1] + half_step[1]
        full_step = (1.0 - twice * half_step[1], twice * half_step[0])
        forth, back = turn_both_ways(center, full_step)
        put(parent_ref, (t,), forth)
        put(parent_ref, (CHEB - 1 - t,), back)


def level_column(column, children, parent_ref, child_ref, common_ref, store):
    scaled = []
    for child in range(2):
        line = []
        for s in range(CHEB):
            real, imag = children[child][s]
            cosine, sine = child_ref[child, s, 0], child_ref[child, s, 1]
            line.append((cosine * real + sine * imag, cosine * imag - sine * real))
        scaled.append(line)
    halves = []
    for part in range(2):
        plus = [scaled[0][s][part] + scaled[1][CHEB - 1 - s][part] for s in range(CHEB)]
        minus = [scaled[0][s][part] - scaled[1][CHEB - 1 - s][part] for s in range(CHEB)]
        halves.append((plus, minus))
    common = common_ref[column]
    mid = CHEB // 2
    for t in range(mid + 1):
        sums = []
        for part in range(2):
            plus, minus = halves[part]
            even = plus[0] * float(EVEN_HALF[t, 0])
            for s in range(1, CHEB):
                even = even + plus[s] * float(EVEN_HALF[t, s])
            if t == mid:
                sums.append((even,))
                continue
            odd = minus[0] * float(ODD_HALF[t, 0])
            for s in range(1, CHEB):
                odd = odd + minus[s] * float(ODD_HALF[t, s])
            sums.append((even + odd, even - odd))
        for which, row in enumerate((t,) if t == mid else (t, CHEB - 1 - t)):
            real, imag = sums[0][which] * common, sums[1][which] * common
            cosine, sine = parent_ref[row, 0], parent_ref[row, 1]
            store(row, cosine * real - sine * imag, cosine * imag + sine * real)


def row_of(level, split, column, part):
    return part + 2 * (split * CHEB + column if level % 2 == 0 else column * CHEB + split)


def join_chips(me, blocks, order, held, sems, work, last_phases, factors):
    copies = []
    for index, step in enumerate(order):
        spot = pl.ds(((me ^ step) // 2) * (ROWS // 2), ROWS // 2)
        copies.append(pltpu.make_async_copy(blocks[index], held.at[spot], sems.at[index]))
        copies[-1].start()
    for copy in copies:
        copy.wait()
    rows = held.reshape(OCT * ROWS, LANES)

    def received(row):
        return rows[pl.ds(row, OCT, stride=ROWS), :]

    for part in range(4):
        last_phases[part] = received(WEIGHT_ROWS + part * LEVELS + LEVELS - 1)
    for level in range(LEVELS - 1):
        level_factors(level, [received(WEIGHT_ROWS + part * LEVELS + level) for part in range(4)], *factors)
        bit = OCT >> (level + 1)

        def column_step(column, _, level=level, bit=bit):
            upper = (lax.broadcasted_iota(jnp.int32, (OCT, LANES), 0) & bit) != 0
            children = [[], []]
            for s in range(CHEB):
                pairs = [[], []]
                for part in range(2):
                    row = row_of(level, s, column, part)
                    value = received(row) if level == 0 else work[row]
                    down = pltpu.roll(value, bit, 0)
                    up = down if 2 * bit == OCT else pltpu.roll(value, OCT - bit, 0)
                    pairs[0].append(jnp.where(upper, down, value))
                    pairs[1].append(jnp.where(upper, value, up))
                children[0].append(tuple(pairs[0]))
                children[1].append(tuple(pairs[1]))

            def store(row, real, imag):
                work[row_of(level, row, column, 0)] = real
                work[row_of(level, row, column, 1)] = imag

            level_column(column, children, *factors, store)
            return 0

        lax.fori_loop(0, CHEB, column_step, 0, unroll=3)


def even_kernel(me_ref, *refs):
    work, last_phases, held, parent_ref, child_ref, common_ref, sems = refs[OCT:]
    factors = (parent_ref, child_ref, common_ref)
    join_chips(me_ref[0], refs, EVEN_ORDER, held, sems, work, last_phases, factors)


def odd_kernel(me_ref, even_work, even_phases, *refs):
    out_hbm, work, last_phases, held, out_ref, parent_ref, child_ref, common_ref, sems, out_sems = refs[OCT:]
    me = me_ref[0]
    own = me % 2
    early = [
        pltpu.make_async_copy(even_work, work.at[own], out_sems.at[0]),
        pltpu.make_async_copy(even_phases, last_phases.at[own], out_sems.at[1]),
    ]
    for copy in early:
        copy.start()
    factors = [ref.at[0] for ref in (parent_ref, child_ref, common_ref)]
    join_chips(me, refs, ODD_ORDER, held, sems, work.at[1 - own], last_phases.at[1 - own], factors)
    for copy in early:
        copy.wait()

    level = LEVELS - 1
    for parity in range(2):
        level_factors(
            level,
            [last_phases[parity, part] for part in range(4)],
            parent_ref.at[parity],
            child_ref.at[parity],
            common_ref.at[parity],
        )
    chunk = out_ref.shape[0] // CHEB

    def leave(column):
        rows = pl.ds(pl.multiple_of(column * chunk, 8), chunk)
        return pltpu.make_async_copy(out_ref.at[rows, :], out_hbm.at[rows, :], out_sems.at[column])

    def column_step(column, _):
        children = [
            [tuple(work[child, row_of(level, s, column, part)] for part in range(2)) for s in range(CHEB)]
            for child in range(2)
        ]
        for parity in range(2):

            def store(row, real, imag, parity=parity):
                start = row_of(level, row, column, 0) * SLOTS + 2 * parity
                out_ref[pl.ds(start, OCT, stride=4), :] = real
                out_ref[pl.ds(start + 1, OCT, stride=4), :] = imag

            level_column(
                column, children, parent_ref.at[parity], child_ref.at[parity], common_ref.at[parity], store
            )
        leave(column).start()
        return 0

    lax.fori_loop(0, CHEB, column_step, 0, unroll=3)
    for column in range(CHEB):
        leave(column).wait()


def factor_scratch(count):
    return [
        pltpu.VMEM(count + (CHEB, 2, OCT, LANES), jnp.float32),
        pltpu.VMEM(count + (2, CHEB, 2, OCT, LANES), jnp.float32),
        pltpu.VMEM(count + (CHEB, OCT, LANES), jnp.float32),
    ]


def combine_even(me, blocks):
    vmem = pl.BlockSpec(memory_space=pltpu.VMEM)
    return pl.pallas_call(
        even_kernel,
        out_shape=[
            jax.ShapeDtypeStruct((WEIGHT_ROWS, OCT, LANES), jnp.float32),
            jax.ShapeDtypeStruct((4, OCT, LANES), jnp.float32),
        ],
        in_specs=[pl.BlockSpec(memory_space=pltpu.SMEM)] + [pl.BlockSpec(memory_space=pl.ANY)] * OCT,
        out_specs=[vmem, vmem],
        scratch_shapes=[
            pltpu.VMEM((OCT * ROWS // 2, 2, LANES), jnp.float32),
            *factor_scratch(()),
            pltpu.SemaphoreType.DMA((OCT,)),
        ],
        compiler_params=pltpu.CompilerParams(vmem_limit_bytes=16 * 2**20),
        cost_estimate=pl.CostEstimate(flops=40 * 2**20, bytes_accessed=12 * 2**20, transcendentals=0),
        name="combine_even",
    )(me, *blocks)


def combine_odd(me, even, blocks):
    hbm = pl.BlockSpec(memory_space=pltpu.HBM)
    anywhere = pl.BlockSpec(memory_space=pl.ANY)
    return pl.pallas_call(
        odd_kernel,
        out_shape=jax.ShapeDtypeStruct((WEIGHT_ROWS * SLOTS, LANES), jnp.float32),
        in_specs=[pl.BlockSpec(memory_space=pltpu.SMEM)] + [anywhere] * (2 + OCT),
        out_specs=hbm,
        scratch_shapes=[
            pltpu.VMEM((2, WEIGHT_ROWS, OCT, LANES), jnp.float32),
            pltpu.VMEM((2, 4, OCT, LANES), jnp.float32),
            pltpu.VMEM((OCT * ROWS // 2, 2, LANES), jnp.float32),
            pltpu.VMEM((WEIGHT_ROWS * SLOTS, LANES), jnp.float32),
            *factor_scratch((2,)),
            pltpu.SemaphoreType.DMA((OCT,)),
            pltpu.SemaphoreType.DMA((CHEB,)),
        ],
        compiler_params=pltpu.CompilerParams(vmem_limit_bytes=16 * 2**20),
        cost_estimate=pl.CostEstimate(flops=80 * 2**20, bytes_accessed=20 * 2**20, transcendentals=0),
        name="combine_odd",
    )(me, *even, *blocks)


def on_device(source_weights, wave_vectors, source_centers, phase_coef, phase_kind):
    devices = lax.axis_size("box")
    me = lax.axis_index("box").astype(jnp.int32)[None]
    direct = devices == SLOTS
    if not direct:
        me = jnp.zeros_like(me)
    weights = source_weights.reshape(2, POINTS, SLOTS, LANES).transpose(1, 2, 0, 3)
    weights, *sources = [
        pltpu.with_memory_space_constraint(operand, pltpu.HBM)
        for operand in (weights, phase_coef, wave_vectors, source_centers, phase_kind[None, :])
    ]
    blocks, phases = {}, None
    for steps in PACKS:
        if blocks:
            last = next(reversed(blocks))
            phases, blocks[last] = lax.optimization_barrier((phases, blocks[last]))
        packed, phases = pack(steps, me, weights, phases, sources)
        blocks.update(packed)
    if direct:
        for step in SENDS:
            if step in WAITS:
                earlier = WAITS[step]
                blocks[step], blocks[earlier] = lax.optimization_barrier((blocks[step], blocks[earlier]))
            blocks[step] = lax.ppermute(blocks[step], "box", [(s, s ^ step) for s in range(SLOTS)])
        own = me
        for step in SEEN:
            own, blocks[step] = lax.optimization_barrier((own, blocks[step]))
    else:
        own = me
        whole = jnp.concatenate([blocks[step] for step in range(SLOTS)], axis=2)
        whole = lax.all_to_all(whole, "box", split_axis=2, concat_axis=2, tiled=True)
        blocks = [whole[:, :, s * LANES : (s + 1) * LANES] for s in range(SLOTS)]
    even = combine_even(own, [blocks[step] for step in EVEN_ORDER])
    rows = combine_odd(me, even, [blocks[step] for step in ODD_ORDER])
    return rows.reshape(POINTS, SLOTS, 2, LANES).transpose(2, 0, 1, 3).reshape(2, POINTS, SLOTS * LANES)


def solution(mesh):
    in_specs = (
        P(None, None, ("groups", "box")),
        P(None, None, ("groups", "box")),
        P(None, None, ("groups", "box")),
        P(),
        P(("groups", "box")),
    )
    out_specs = P(None, None, ("groups", "box"))
    return jax.shard_map(on_device, mesh=mesh, in_specs=in_specs, out_specs=out_specs, check_vma=False)
```

```python
import functools
import math

import numpy as np

import jax
import jax.numpy as jnp
from jax import lax
from jax.experimental import pallas as pl
from jax.experimental.pallas import tpu as pltpu
from jax.sharding import PartitionSpec as P

CHEB = 9
POINTS = CHEB * CHEB
KINDS = 4
LEVELS = 4
SLOTS = 1 << LEVELS
LANES = 128
WEIGHT_ROWS = 2 * POINTS
PHASE_ROWS = 4 * LEVELS
ROWS = WEIGHT_ROWS + PHASE_ROWS
PAIRS = ROWS // 2
ACROSS_Y = 2
OCT = SLOTS // 2
PACKS = (((8, 10), (4, 6), (2,), (1, 3)), ((12,), (5,), (7,), (14,), (9, 11), (15,), (13,), (0,)))
ONWARD = {"even": (2, 8, 4), "odd": (9, 1)}
SENDS = (8, 4, 1, 12, 5, 7, 14, 9, 15, 13, "even", "odd")
WAITS = {14: 1, 15: 5, 12: 8, 7: 5, 5: 8}
EVEN_ORDER = (8, 12, 14, 4, "even", 0)
ODD_ORDER = (1, 13, 15, 7, 5, "odd", 9)

NODES = np.cos(math.pi * (2.0 * np.arange(CHEB) + 1.0) / (2.0 * CHEB))
NODES[CHEB // 2] = 0.0


def interpolation_halves():
    targets = (NODES - 1.0) / 2.0
    matrix = np.ones((CHEB, CHEB))
    for t in range(CHEB):
        for m in range(CHEB):
            if m != t:
                matrix[t] *= (targets - NODES[m]) / (NODES[t] - NODES[m])
    return (matrix + matrix[::-1]) / 2.0, (matrix - matrix[::-1]) / 2.0


EVEN_HALF, ODD_HALF = interpolation_halves()

SIN_COEFS = (3.1415926401839673, -5.167710090328242, 2.5500776596583643, -0.5982921590176602, 0.0776594073245765)
COS_COEFS = (0.999999953466542, -4.934792858659144, 4.05841191384421, -1.3318801591805476, 0.219696794464285)


def cos_sin_turns(turns):
    rest = turns - jnp.round(turns)
    square = rest * rest
    sine = jnp.float32(SIN_COEFS[-1])
    cosine = jnp.float32(COS_COEFS[-1])
    for s, c in zip(SIN_COEFS[-2::-1], COS_COEFS[-2::-1]):
        sine = sine * square + s
        cosine = cosine * square + c
    sine = sine * rest
    twice = sine + sine
    return 1.0 - twice * sine, twice * cosine


def phase_rows(wave, center, kind, coef_ref):
    a = b = e = jnp.zeros(kind.shape, jnp.float32)
    for index in range(KINDS):
        chosen = kind == index
        a = jnp.where(chosen, coef_ref[index, 0], a)
        b = jnp.where(chosen, coef_ref[index, 1], b)
        e = jnp.where(chosen, coef_ref[index, 2], e)
    k1, k2 = wave
    x1, x2 = center
    level = lax.broadcasted_iota(jnp.int32, k1.shape, 0)
    half = jnp.full(k1.shape, 2.0**-LEVELS, jnp.float32)
    for index in range(1, LEVELS):
        half = jnp.where(level == index, 2.0 ** (index - LEVELS), half)
    scaled = b * k1
    root = a * jnp.sqrt(scaled * scaled + k2 * k2 + 1.0)
    bent = root * e
    constant = x1 * k1 + x2 * k2 + root + bent * x1 * x1
    constant = constant - jnp.round(constant)
    return constant, half * (k1 + 2.0 * bent * x1), half * half * bent, half * k2


def phase_kernel(coef_hbm, wave_hbm, center_hbm, kind_hbm, phases_ref, coef_ref, wave_ref, center_ref, kind_ref, sems):
    copies = [
        pltpu.make_async_copy(source, target, sems.at[index])
        for index, (source, target) in enumerate(
            ((coef_hbm, coef_ref), (wave_hbm, wave_ref), (center_hbm, center_ref), (kind_hbm, kind_ref))
        )
    ]
    for copy in copies:
        copy.start()
    for copy in copies:
        copy.wait()
    rows = phase_rows(
        (wave_ref[:, 0, :], wave_ref[:, 1, :]), (center_ref[:, 0, :], center_ref[:, 1, :]), kind_ref[...], coef_ref
    )
    for index, values in enumerate(rows):
        for level in range(LEVELS):
            row = index * LEVELS + level
            phases_ref[row // 2, row % 2, :] = values[level]


def pack_kernel(messages, first, me_ref, weights_hbm, *refs):
    count = len(messages)
    if first:
        small, refs = refs[:4], refs[4:]
        arrays, phases_ref, block_sems, scratch = refs[:count], refs[count], refs[count + 1], refs[count + 2 :]
    else:
        phases_ref, arrays, block_sems = refs[0], refs[1 : 1 + count], refs[1 + count]
    slots = [me_ref[0] ^ step for message in messages for step in message]
    outs = [
        array.at[pl.ds(index * PAIRS, PAIRS)]
        for message, array in zip(messages, arrays)
        for index in range(len(message))
    ]
    copies = [
        pltpu.make_async_copy(weights_hbm.at[:, slot], out.at[pl.ds(0, POINTS)], block_sems.at[index])
        for index, (slot, out) in enumerate(zip(slots, outs))
    ]
    for copy in copies:
        copy.start()
    if first:
        phase_kernel(*small, phases_ref, *scratch)
    for slot, out in zip(slots, outs):
        out[POINTS:] = phases_ref[:, :, pl.ds(pl.multiple_of(slot * LANES, LANES), LANES)]
    for copy in copies:
        copy.wait()


def pack(messages, me, weights, phases, sources):
    first = phases is None
    vmem = pl.BlockSpec(memory_space=pltpu.VMEM)
    hbm = pl.BlockSpec(memory_space=pltpu.HBM)
    out_shape = [jax.ShapeDtypeStruct((len(m) * PAIRS, 2, LANES), jnp.float32) for m in messages]
    scratch = [pltpu.SemaphoreType.DMA((sum(map(len, messages)),))]
    if first:
        boxes = sources[-1].shape[-1]
        out_shape.append(jax.ShapeDtypeStruct((PHASE_ROWS // 2, 2, boxes), jnp.float32))
        scratch += [pltpu.SMEM(sources[0].shape, jnp.float32)]
        scratch += [pltpu.VMEM(source.shape, source.dtype) for source in sources[1:]]
        scratch += [pltpu.SemaphoreType.DMA((len(sources),))]
    operands = sources if first else [phases]
    *arrays, last = pl.pallas_call(
        functools.partial(pack_kernel, messages, first),
        out_shape=out_shape,
        in_specs=[pl.BlockSpec(memory_space=pltpu.SMEM), hbm] + ([hbm] * len(sources) if first else [vmem]),
        out_specs=[vmem] * len(out_shape),
        scratch_shapes=scratch,
        compiler_params=pltpu.CompilerParams(vmem_limit_bytes=16 * 2**20),
        cost_estimate=pl.CostEstimate(flops=2**20, bytes_accessed=2**20, transcendentals=0),
        name="pack",
    )(me, weights, *operands)
    if first:
        phases = last
    else:
        arrays.append(last)
    return {m[0]: array for m, array in zip(messages, arrays)}, phases


def turn_both_ways(base, step):
    cc, ss = base[0] * step[0], base[1] * step[1]
    sc, cs = base[1] * step[0], base[0] * step[1]
    return (cc - ss, sc + cs), (cc + ss, sc - cs)


def level_factors(level, phases, parent_ref, child_ref, common_ref):
    constant, linear, quadratic, other = phases
    mid = CHEB // 2

    def put(ref, index, pair):
        ref[index + (0,)], ref[index + (1,)] = pair

    def norm(turns):
        cosine, sine = cos_sin_turns(turns)
        return cosine * cosine + sine * sine

    common_ref[mid] = jnp.ones_like(constant)
    for t in range(mid):
        node = float(NODES[t])
        if level % 2 == 0:
            common_ref[t] = common_ref[CHEB - 1 - t] = norm(node * other)
        else:
            common_ref[t] = norm(node * (linear + node * quadratic))
            common_ref[CHEB - 1 - t] = norm(node * (node * quadratic - linear))
    if level % 2 == 0:
        for t in range(CHEB):
            node = float(NODES[t])
            put(parent_ref, (t,), cos_sin_turns(constant + node * (linear + node * quadratic)))
            for child in range(2):
                shifted = (node + 2.0 * child - 1.0) / 2.0
                pair = cos_sin_turns(constant + shifted * (linear + shifted * quadratic))
                put(child_ref, (child, t), pair)
        return
    center = cos_sin_turns(constant)
    centers = [cos_sin_turns(constant + (child - 0.5) * other) for child in range(2)]
    put(parent_ref, (mid,), center)
    for child in range(2):
        put(child_ref, (child, mid), centers[child])
    for t in range(mid):
        half_step = cos_sin_turns((0.5 * float(NODES[t])) * other)
        for child in range(2):
            forth, back = turn_both_ways(centers[child], half_step)
            put(child_ref, (child, t), forth)
            put(child_ref, (child, CHEB - 1 - t), back)
        twice = half_step[1] + half_step[1]
        full_step = (1.0 - twice * half_step[1], twice * half_step[0])
        forth, back = turn_both_ways(center, full_step)
        put(parent_ref, (t,), forth)
        put(parent_ref, (CHEB - 1 - t,), back)


def level_column(column, children, parent_ref, child_ref, common_ref, store):
    scaled = []
    for child in range(2):
        line = []
        for s in range(CHEB):
            real, imag = children[child][s]
            cosine, sine = child_ref[child, s, 0], child_ref[child, s, 1]
            line.append((cosine * real + sine * imag, cosine * imag - sine * real))
        scaled.append(line)
    halves = []
    for part in range(2):
        plus = [scaled[0][s][part] + scaled[1][CHEB - 1 - s][part] for s in range(CHEB)]
        minus = [scaled[0][s][part] - scaled[1][CHEB - 1 - s][part] for s in range(CHEB)]
        halves.append((plus, minus))
    common = common_ref[column]
    mid = CHEB // 2
    for t in range(mid + 1):
        sums = []
        for part in range(2):
            plus, minus = halves[part]
            even = plus[0] * float(EVEN_HALF[t, 0])
            for s in range(1, CHEB):
                even = even + plus[s] * float(EVEN_HALF[t, s])
            if t == mid:
                sums.append((even,))
                continue
            odd = minus[0] * float(ODD_HALF[t, 0])
            for s in range(1, CHEB):
                odd = odd + minus[s] * float(ODD_HALF[t, s])
            sums.append((even + odd, even - odd))
        for which, row in enumerate((t,) if t == mid else (t, CHEB - 1 - t)):
            real, imag = sums[0][which] * common, sums[1][which] * common
            cosine, sine = parent_ref[row, 0], parent_ref[row, 1]
            store(row, cosine * real - sine * imag, cosine * imag + sine * real)


def row_of(level, split, column, part):
    return part + 2 * (split * CHEB + column if level % 2 == 0 else column * CHEB + split)


def join_chips(me, arrays, pieces, held, sems, work, last_phases, factors):
    copies = []
    for step, (index, part) in pieces.items():
        spot = pl.ds(((me ^ step) // 2) * PAIRS, PAIRS)
        source = arrays[index].at[pl.ds(part * PAIRS, PAIRS)]
        copies.append(pltpu.make_async_copy(source, held.at[spot], sems.at[step // 2]))
        copies[-1].start()
    for copy in copies:
        copy.wait()
    rows = held.reshape(OCT * ROWS, LANES)

    def received(row):
        return rows[pl.ds(row, OCT, stride=ROWS), :]

    for part in range(4):
        last_phases[part] = received(WEIGHT_ROWS + part * LEVELS + LEVELS - 1)
    for level in range(LEVELS - 1):
        level_factors(level, [received(WEIGHT_ROWS + part * LEVELS + level) for part in range(4)], *factors)
        bit = OCT >> (level + 1)

        def column_step(column, _, level=level, bit=bit):
            upper = (lax.broadcasted_iota(jnp.int32, (OCT, LANES), 0) & bit) != 0
            children = [[], []]
            for s in range(CHEB):
                pairs = [[], []]
                for part in range(2):
                    row = row_of(level, s, column, part)
                    value = received(row) if level == 0 else work[row]
                    down = pltpu.roll(value, bit, 0)
                    up = down if 2 * bit == OCT else pltpu.roll(value, OCT - bit, 0)
                    pairs[0].append(jnp.where(upper, down, value))
                    pairs[1].append(jnp.where(upper, value, up))
                children[0].append(tuple(pairs[0]))
                children[1].append(tuple(pairs[1]))

            def store(row, real, imag):
                work[row_of(level, row, column, 0)] = real
                work[row_of(level, row, column, 1)] = imag

            level_column(column, children, *factors, store)
            return 0

        lax.fori_loop(0, CHEB, column_step, 0, unroll=3)


def even_kernel(pieces, count, me_ref, *refs):
    work, last_phases, held, parent_ref, child_ref, common_ref, sems = refs[count:]
    factors = (parent_ref, child_ref, common_ref)
    join_chips(me_ref[0], refs, pieces, held, sems, work, last_phases, factors)


def odd_kernel(pieces, count, me_ref, even_work, even_phases, *refs):
    out_hbm, work, last_phases, held, out_ref, parent_ref, child_ref, common_ref, sems, out_sems = refs[count:]
    me = me_ref[0]
    own = me % 2
    early = [
        pltpu.make_async_copy(even_work, work.at[own], out_sems.at[0]),
        pltpu.make_async_copy(even_phases, last_phases.at[own], out_sems.at[1]),
    ]
    for copy in early:
        copy.start()
    factors = [ref.at[0] for ref in (parent_ref, child_ref, common_ref)]
    join_chips(me, refs, pieces, held, sems, work.at[1 - own], last_phases.at[1 - own], factors)
    for copy in early:
        copy.wait()

    level = LEVELS - 1
    for parity in range(2):
        level_factors(
            level,
            [last_phases[parity, part] for part in range(4)],
            parent_ref.at[parity],
            child_ref.at[parity],
            common_ref.at[parity],
        )
    chunk = out_ref.shape[0] // CHEB

    def leave(column):
        rows = pl.ds(pl.multiple_of(column * chunk, 8), chunk)
        return pltpu.make_async_copy(out_ref.at[rows, :], out_hbm.at[rows, :], out_sems.at[column])

    def column_step(column, _):
        children = [
            [tuple(work[child, row_of(level, s, column, part)] for part in range(2)) for s in range(CHEB)]
            for child in range(2)
        ]
        for parity in range(2):

            def store(row, real, imag, parity=parity):
                start = row_of(level, row, column, 0) * SLOTS + 2 * parity
                out_ref[pl.ds(start, OCT, stride=4), :] = real
                out_ref[pl.ds(start + 1, OCT, stride=4), :] = imag

            level_column(
                column, children, parent_ref.at[parity], child_ref.at[parity], common_ref.at[parity], store
            )
        leave(column).start()
        return 0

    lax.fori_loop(0, CHEB, column_step, 0, unroll=3)
    for column in range(CHEB):
        leave(column).wait()


def factor_scratch(count):
    return [
        pltpu.VMEM(count + (CHEB, 2, OCT, LANES), jnp.float32),
        pltpu.VMEM(count + (2, CHEB, 2, OCT, LANES), jnp.float32),
        pltpu.VMEM(count + (CHEB, OCT, LANES), jnp.float32),
    ]


def combine_even(me, arrays, pieces):
    vmem = pl.BlockSpec(memory_space=pltpu.VMEM)
    return pl.pallas_call(
        functools.partial(even_kernel, pieces, len(arrays)),
        out_shape=[
            jax.ShapeDtypeStruct((WEIGHT_ROWS, OCT, LANES), jnp.float32),
            jax.ShapeDtypeStruct((4, OCT, LANES), jnp.float32),
        ],
        in_specs=[pl.BlockSpec(memory_space=pltpu.SMEM)] + [pl.BlockSpec(memory_space=pl.ANY)] * len(arrays),
        out_specs=[vmem, vmem],
        scratch_shapes=[
            pltpu.VMEM((OCT * PAIRS, 2, LANES), jnp.float32),
            *factor_scratch(()),
            pltpu.SemaphoreType.DMA((OCT,)),
        ],
        compiler_params=pltpu.CompilerParams(vmem_limit_bytes=16 * 2**20),
        cost_estimate=pl.CostEstimate(flops=40 * 2**20, bytes_accessed=12 * 2**20, transcendentals=0),
        name="combine_even",
    )(me, *arrays)


def combine_odd(me, even, arrays, pieces):
    hbm = pl.BlockSpec(memory_space=pltpu.HBM)
    anywhere = pl.BlockSpec(memory_space=pl.ANY)
    return pl.pallas_call(
        functools.partial(odd_kernel, pieces, len(arrays)),
        out_shape=jax.ShapeDtypeStruct((WEIGHT_ROWS * SLOTS, LANES), jnp.float32),
        in_specs=[pl.BlockSpec(memory_space=pltpu.SMEM)] + [anywhere] * (2 + len(arrays)),
        out_specs=hbm,
        scratch_shapes=[
            pltpu.VMEM((2, WEIGHT_ROWS, OCT, LANES), jnp.float32),
            pltpu.VMEM((2, 4, OCT, LANES), jnp.float32),
            pltpu.VMEM((OCT * PAIRS, 2, LANES), jnp.float32),
            pltpu.VMEM((WEIGHT_ROWS * SLOTS, LANES), jnp.float32),
            *factor_scratch((2,)),
            pltpu.SemaphoreType.DMA((OCT,)),
            pltpu.SemaphoreType.DMA((CHEB,)),
        ],
        compiler_params=pltpu.CompilerParams(vmem_limit_bytes=16 * 2**20),
        cost_estimate=pl.CostEstimate(flops=80 * 2**20, bytes_accessed=20 * 2**20, transcendentals=0),
        name="combine_odd",
    )(me, *even, *arrays)


def on_device(source_weights, wave_vectors, source_centers, phase_coef, phase_kind):
    devices = lax.axis_size("box")
    me = lax.axis_index("box").astype(jnp.int32)[None]
    direct = devices == SLOTS
    if not direct:
        me = jnp.zeros_like(me)
    weights = source_weights.reshape(2, POINTS, SLOTS, LANES).transpose(1, 2, 0, 3)
    weights, *sources = [
        pltpu.with_memory_space_constraint(operand, pltpu.HBM)
        for operand in (weights, phase_coef, wave_vectors, source_centers, phase_kind[None, :])
    ]
    blocks, phases = {}, None
    for messages in PACKS:
        if blocks:
            last = next(reversed(blocks))
            phases, blocks[last] = lax.optimization_barrier((phases, blocks[last]))
        packed, phases = pack(messages, me, weights, phases, sources)
        blocks.update(packed)
    inside = {m[0]: m for messages in PACKS for m in messages}
    if direct:
        pairs = {step for step, message in inside.items() if len(message) > 1}
        for name in SENDS:
            step = name
            if name in ONWARD:
                step = ACROSS_Y
                parts = [blocks[part][PAIRS:] if part in pairs else blocks[part] for part in ONWARD[name]]
                blocks[name] = jnp.concatenate(parts)
                inside[name] = tuple(part ^ ACROSS_Y if part in pairs else part for part in ONWARD[name])
            if name in WAITS:
                earlier = WAITS[name]
                blocks[name], blocks[earlier] = lax.optimization_barrier((blocks[name], blocks[earlier]))
            blocks[name] = lax.ppermute(blocks[name], "box", [(s, s ^ step) for s in range(SLOTS)])
            inside[step] = inside[step] if name in ONWARD else inside[step][:1]
        orders = EVEN_ORDER, ODD_ORDER
    else:
        parts = {step: blocks[m[0]][i * PAIRS : (i + 1) * PAIRS] for m in inside.values() for i, step in enumerate(m)}
        whole = jnp.concatenate([parts[step] for step in range(SLOTS)], axis=2)
        whole = lax.all_to_all(whole, "box", split_axis=2, concat_axis=2, tiled=True)
        blocks = {s: whole[:, :, s * LANES : (s + 1) * LANES] for s in range(SLOTS)}
        inside = {s: (s,) for s in range(SLOTS)}
        orders = range(0, SLOTS, 2), range(1, SLOTS, 2)
    arrays = [[blocks[name] for name in order] for order in orders]
    pieces = [
        {step: (index, part) for index, name in enumerate(order) for part, step in enumerate(inside[name])}
        for order in orders
    ]
    even = combine_even(me, arrays[0], pieces[0])
    rows = combine_odd(me, even, arrays[1], pieces[1])
    return rows.reshape(POINTS, SLOTS, 2, LANES).transpose(2, 0, 1, 3).reshape(2, POINTS, SLOTS * LANES)


def solution(mesh):
    in_specs = (
        P(None, None, ("groups", "box")),
        P(None, None, ("groups", "box")),
        P(None, None, ("groups", "box")),
        P(),
        P(("groups", "box")),
    )
    out_specs = P(None, None, ("groups", "box"))
    return jax.shard_map(on_device, mesh=mesh, in_specs=in_specs, out_specs=out_specs, check_vma=False)
```

```python
import functools
import math

import numpy as np

import jax
import jax.numpy as jnp
from jax import lax
from jax.experimental import pallas as pl
from jax.experimental.pallas import tpu as pltpu
from jax.sharding import PartitionSpec as P

CHEB = 9
POINTS = CHEB * CHEB
KINDS = 4
LEVELS = 4
SLOTS = 1 << LEVELS
LANES = 128
WEIGHT_ROWS = 2 * POINTS
PHASE_ROWS = 4 * LEVELS
ROWS = WEIGHT_ROWS + PHASE_ROWS
OCT = SLOTS // 2
PACKS = ((12, 4, 6, 10), (2, 14, 9, 15, 3, 11, 8), (7, 13, 5, 1, 0))
SENDS = (12, 4, 8, 6, 2, 14, 15, 3, 10, 11, 7, 13, 5, 1, 9)
WAITS = {9: 4, 1: 11}
EVEN_ORDER = (10, 6, 12, 14, 4, 2, 8, 0)
ODD_ORDER = (3, 11, 15, 9, 13, 1, 7, 5)

NODES = np.cos(math.pi * (2.0 * np.arange(CHEB) + 1.0) / (2.0 * CHEB))
NODES[CHEB // 2] = 0.0


def interpolation_halves():
    targets = (NODES - 1.0) / 2.0
    matrix = np.ones((CHEB, CHEB))
    for t in range(CHEB):
        for m in range(CHEB):
            if m != t:
                matrix[t] *= (targets - NODES[m]) / (NODES[t] - NODES[m])
    return (matrix + matrix[::-1]) / 2.0, (matrix - matrix[::-1]) / 2.0


EVEN_HALF, ODD_HALF = interpolation_halves()

SIN_COEFS = (3.1415926401839673, -5.167710090328242, 2.5500776596583643, -0.5982921590176602, 0.0776594073245765)
COS_COEFS = (0.999999953466542, -4.934792858659144, 4.05841191384421, -1.3318801591805476, 0.219696794464285)


def cos_sin_turns(turns):
    rest = turns - jnp.round(turns)
    square = rest * rest
    sine = jnp.float32(SIN_COEFS[-1])
    cosine = jnp.float32(COS_COEFS[-1])
    for s, c in zip(SIN_COEFS[-2::-1], COS_COEFS[-2::-1]):
        sine = sine * square + s
        cosine = cosine * square + c
    sine = sine * rest
    twice = sine + sine
    return 1.0 - twice * sine, twice * cosine


def phase_rows(wave, center, kind, coef_ref):
    a = b = e = jnp.zeros(kind.shape, jnp.float32)
    for index in range(KINDS):
        chosen = kind == index
        a = jnp.where(chosen, coef_ref[index, 0], a)
        b = jnp.where(chosen, coef_ref[index, 1], b)
        e = jnp.where(chosen, coef_ref[index, 2], e)
    k1, k2 = wave
    x1, x2 = center
    level = lax.broadcasted_iota(jnp.int32, k1.shape, 0)
    half = jnp.full(k1.shape, 2.0**-LEVELS, jnp.float32)
    for index in range(1, LEVELS):
        half = jnp.where(level == index, 2.0 ** (index - LEVELS), half)
    scaled = b * k1
    root = a * jnp.sqrt(scaled * scaled + k2 * k2 + 1.0)
    bent = root * e
    constant = x1 * k1 + x2 * k2 + root + bent * x1 * x1
    constant = constant - jnp.round(constant)
    return constant, half * (k1 + 2.0 * bent * x1), half * half * bent, half * k2


def phase_kernel(coef_hbm, wave_hbm, center_hbm, kind_hbm, phases_ref, coef_ref, wave_ref, center_ref, kind_ref, sems):
    copies = [
        pltpu.make_async_copy(source, target, sems.at[index])
        for index, (source, target) in enumerate(
            ((coef_hbm, coef_ref), (wave_hbm, wave_ref), (center_hbm, center_ref), (kind_hbm, kind_ref))
        )
    ]
    for copy in copies:
        copy.start()
    for copy in copies:
        copy.wait()
    rows = phase_rows(
        (wave_ref[:, 0, :], wave_ref[:, 1, :]), (center_ref[:, 0, :], center_ref[:, 1, :]), kind_ref[...], coef_ref
    )
    for index, values in enumerate(rows):
        for level in range(LEVELS):
            row = index * LEVELS + level
            phases_ref[row // 2, row % 2, :] = values[level]


def pack_kernel(steps, first, me_ref, weights_hbm, *refs):
    if first:
        small, refs = refs[:4], refs[4:]
        outs, refs = refs[: len(steps)], refs[len(steps) :]
        phases_ref, block_sems, scratch = refs[0], refs[1], refs[2:]
    else:
        phases_ref, outs, block_sems = refs[0], refs[1 : 1 + len(steps)], refs[1 + len(steps)]
    slots = [me_ref[0] ^ step for step in steps]
    copies = [
        pltpu.make_async_copy(weights_hbm.at[:, slot], out.at[pl.ds(0, POINTS)], block_sems.at[index])
        for index, (slot, out) in enumerate(zip(slots, outs))
    ]
    for copy in copies:
        copy.start()
    if first:
        phase_kernel(*small, phases_ref, *scratch)
    for slot, out in zip(slots, outs):
        out[POINTS:] = phases_ref[:, :, pl.ds(pl.multiple_of(slot * LANES, LANES), LANES)]
    for copy in copies:
        copy.wait()


def pack(steps, me, weights, phases, sources):
    first = phases is None
    vmem = pl.BlockSpec(memory_space=pltpu.VMEM)
    hbm = pl.BlockSpec(memory_space=pltpu.HBM)
    out_shape = [jax.ShapeDtypeStruct((ROWS // 2, 2, LANES), jnp.float32) for _ in steps]
    scratch = [pltpu.SemaphoreType.DMA((len(steps),))]
    if first:
        boxes = sources[-1].shape[-1]
        out_shape.append(jax.ShapeDtypeStruct((PHASE_ROWS // 2, 2, boxes), jnp.float32))
        scratch += [pltpu.SMEM(sources[0].shape, jnp.float32)]
        scratch += [pltpu.VMEM(source.shape, source.dtype) for source in sources[1:]]
        scratch += [pltpu.SemaphoreType.DMA((len(sources),))]
    operands = sources if first else [phases]
    *arrays, last = pl.pallas_call(
        functools.partial(pack_kernel, steps, first),
        out_shape=out_shape,
        in_specs=[pl.BlockSpec(memory_space=pltpu.SMEM), hbm] + ([hbm] * len(sources) if first else [vmem]),
        out_specs=[vmem] * len(out_shape),
        scratch_shapes=scratch,
        compiler_params=pltpu.CompilerParams(vmem_limit_bytes=16 * 2**20),
        cost_estimate=pl.CostEstimate(flops=2**20, bytes_accessed=2**20, transcendentals=0),
        name="pack",
    )(me, weights, *operands)
    if first:
        phases = last
    else:
        arrays.append(last)
    return dict(zip(steps, arrays)), phases


def turn_both_ways(base, step):
    cc, ss = base[0] * step[0], base[1] * step[1]
    sc, cs = base[1] * step[0], base[0] * step[1]
    return (cc - ss, sc + cs), (cc + ss, sc - cs)


def level_factors(level, phases, parent_ref, child_ref, common_ref):
    constant, linear, quadratic, other = phases
    mid = CHEB // 2

    def put(ref, index, pair):
        ref[index + (0,)], ref[index + (1,)] = pair

    def norm(turns):
        cosine, sine = cos_sin_turns(turns)
        return cosine * cosine + sine * sine

    common_ref[mid] = jnp.ones_like(constant)
    for t in range(mid):
        node = float(NODES[t])
        if level % 2 == 0:
            common_ref[t] = common_ref[CHEB - 1 - t] = norm(node * other)
        else:
            common_ref[t] = norm(node * (linear + node * quadratic))
            common_ref[CHEB - 1 - t] = norm(node * (node * quadratic - linear))
    if level % 2 == 0:
        for t in range(CHEB):
            node = float(NODES[t])
            put(parent_ref, (t,), cos_sin_turns(constant + node * (linear + node * quadratic)))
            for child in range(2):
                shifted = (node + 2.0 * child - 1.0) / 2.0
                pair = cos_sin_turns(constant + shifted * (linear + shifted * quadratic))
                put(child_ref, (child, t), pair)
        return
    center = cos_sin_turns(constant)
    centers = [cos_sin_turns(constant + (child - 0.5) * other) for child in range(2)]
    put(parent_ref, (mid,), center)
    for child in range(2):
        put(child_ref, (child, mid), centers[child])
    for t in range(mid):
        half_step = cos_sin_turns((0.5 * float(NODES[t])) * other)
        for child in range(2):
            forth, back = turn_both_ways(centers[child], half_step)
            put(child_ref, (child, t), forth)
            put(child_ref, (child, CHEB - 1 - t), back)
        twice = half_step[1] + half_step[1]
        full_step = (1.0 - twice * half_step[1], twice * half_step[0])
        forth, back = turn_both_ways(center, full_step)
        put(parent_ref, (t,), forth)
        put(parent_ref, (CHEB - 1 - t,), back)


def level_column(column, children, parent_ref, child_ref, common_ref, store):
    scaled = []
    for child in range(2):
        line = []
        for s in range(CHEB):
            real, imag = children[child][s]
            cosine, sine = child_ref[child, s, 0], child_ref[child, s, 1]
            line.append((cosine * real + sine * imag, cosine * imag - sine * real))
        scaled.append(line)
    halves = []
    for part in range(2):
        plus = [scaled[0][s][part] + scaled[1][CHEB - 1 - s][part] for s in range(CHEB)]
        minus = [scaled[0][s][part] - scaled[1][CHEB - 1 - s][part] for s in range(CHEB)]
        halves.append((plus, minus))
    common = common_ref[column]
    mid = CHEB // 2
    for t in range(mid + 1):
        sums = []
        for part in range(2):
            plus, minus = halves[part]
            even = plus[0] * float(EVEN_HALF[t, 0])
            for s in range(1, CHEB):
                even = even + plus[s] * float(EVEN_HALF[t, s])
            if t == mid:
                sums.append((even,))
                continue
            odd = minus[0] * float(ODD_HALF[t, 0])
            for s in range(1, CHEB):
                odd = odd + minus[s] * float(ODD_HALF[t, s])
            sums.append((even + odd, even - odd))
        for which, row in enumerate((t,) if t == mid else (t, CHEB - 1 - t)):
            real, imag = sums[0][which] * common, sums[1][which] * common
            cosine, sine = parent_ref[row, 0], parent_ref[row, 1]
            store(row, cosine * real - sine * imag, cosine * imag + sine * real)


def row_of(level, split, column, part):
    return part + 2 * (split * CHEB + column if level % 2 == 0 else column * CHEB + split)


def join_chips(me, blocks, order, held, sems, work, last_phases, factors):
    copies = []
    for index, step in enumerate(order):
        spot = pl.ds(((me ^ step) // 2) * (ROWS // 2), ROWS // 2)
        copies.append(pltpu.make_async_copy(blocks[index], held.at[spot], sems.at[index]))
        copies[-1].start()
    for copy in copies:
        copy.wait()
    rows = held.reshape(OCT * ROWS, LANES)

    def received(row):
        return rows[pl.ds(row, OCT, stride=ROWS), :]

    for part in range(4):
        last_phases[part] = received(WEIGHT_ROWS + part * LEVELS + LEVELS - 1)
    for level in range(LEVELS - 1):
        level_factors(level, [received(WEIGHT_ROWS + part * LEVELS + level) for part in range(4)], *factors)
        bit = OCT >> (level + 1)

        def column_step(column, _, level=level, bit=bit):
            upper = (lax.broadcasted_iota(jnp.int32, (OCT, LANES), 0) & bit) != 0
            children = [[], []]
            for s in range(CHEB):
                pairs = [[], []]
                for part in range(2):
                    row = row_of(level, s, column, part)
                    value = received(row) if level == 0 else work[row]
                    down = pltpu.roll(value, bit, 0)
                    up = down if 2 * bit == OCT else pltpu.roll(value, OCT - bit, 0)
                    pairs[0].append(jnp.where(upper, down, value))
                    pairs[1].append(jnp.where(upper, value, up))
                children[0].append(tuple(pairs[0]))
                children[1].append(tuple(pairs[1]))

            def store(row, real, imag):
                work[row_of(level, row, column, 0)] = real
                work[row_of(level, row, column, 1)] = imag

            level_column(column, children, *factors, store)
            return 0

        lax.fori_loop(0, CHEB, column_step, 0, unroll=3)


def even_kernel(me_ref, *refs):
    work, last_phases, held, parent_ref, child_ref, common_ref, sems = refs[OCT:]
    factors = (parent_ref, child_ref, common_ref)
    join_chips(me_ref[0], refs, EVEN_ORDER, held, sems, work, last_phases, factors)


def odd_kernel(me_ref, even_work, even_phases, *refs):
    out_hbm, work, last_phases, held, out_ref, parent_ref, child_ref, common_ref, sems, out_sems = refs[OCT:]
    me = me_ref[0]
    own = me % 2
    early = [
        pltpu.make_async_copy(even_work, work.at[own], out_sems.at[0]),
        pltpu.make_async_copy(even_phases, last_phases.at[own], out_sems.at[1]),
    ]
    for copy in early:
        copy.start()
    factors = [ref.at[0] for ref in (parent_ref, child_ref, common_ref)]
    join_chips(me, refs, ODD_ORDER, held, sems, work.at[1 - own], last_phases.at[1 - own], factors)
    for copy in early:
        copy.wait()

    level = LEVELS - 1
    for parity in range(2):
        level_factors(
            level,
            [last_phases[parity, part] for part in range(4)],
            parent_ref.at[parity],
            child_ref.at[parity],
            common_ref.at[parity],
        )
    chunk = out_ref.shape[0] // CHEB

    def leave(column):
        rows = pl.ds(pl.multiple_of(column * chunk, 8), chunk)
        return pltpu.make_async_copy(out_ref.at[rows, :], out_hbm.at[rows, :], out_sems.at[column])

    def column_step(column, _):
        children = [
            [tuple(work[child, row_of(level, s, column, part)] for part in range(2)) for s in range(CHEB)]
            for child in range(2)
        ]
        for parity in range(2):

            def store(row, real, imag, parity=parity):
                start = row_of(level, row, column, 0) * SLOTS + 2 * parity
                out_ref[pl.ds(start, OCT, stride=4), :] = real
                out_ref[pl.ds(start + 1, OCT, stride=4), :] = imag

            level_column(
                column, children, parent_ref.at[parity], child_ref.at[parity], common_ref.at[parity], store
            )
        leave(column).start()
        return 0

    lax.fori_loop(0, CHEB, column_step, 0, unroll=3)
    for column in range(CHEB):
        leave(column).wait()


def factor_scratch(count):
    return [
        pltpu.VMEM(count + (CHEB, 2, OCT, LANES), jnp.float32),
        pltpu.VMEM(count + (2, CHEB, 2, OCT, LANES), jnp.float32),
        pltpu.VMEM(count + (CHEB, OCT, LANES), jnp.float32),
    ]


def combine_even(me, blocks):
    vmem = pl.BlockSpec(memory_space=pltpu.VMEM)
    return pl.pallas_call(
        even_kernel,
        out_shape=[
            jax.ShapeDtypeStruct((WEIGHT_ROWS, OCT, LANES), jnp.float32),
            jax.ShapeDtypeStruct((4, OCT, LANES), jnp.float32),
        ],
        in_specs=[pl.BlockSpec(memory_space=pltpu.SMEM)] + [pl.BlockSpec(memory_space=pl.ANY)] * OCT,
        out_specs=[vmem, vmem],
        scratch_shapes=[
            pltpu.VMEM((OCT * ROWS // 2, 2, LANES), jnp.float32),
            *factor_scratch(()),
            pltpu.SemaphoreType.DMA((OCT,)),
        ],
        compiler_params=pltpu.CompilerParams(vmem_limit_bytes=16 * 2**20),
        cost_estimate=pl.CostEstimate(flops=40 * 2**20, bytes_accessed=12 * 2**20, transcendentals=0),
        name="combine_even",
    )(me, *blocks)


def combine_odd(me, even, blocks):
    hbm = pl.BlockSpec(memory_space=pltpu.HBM)
    anywhere = pl.BlockSpec(memory_space=pl.ANY)
    return pl.pallas_call(
        odd_kernel,
        out_shape=jax.ShapeDtypeStruct((WEIGHT_ROWS * SLOTS, LANES), jnp.float32),
        in_specs=[pl.BlockSpec(memory_space=pltpu.SMEM)] + [anywhere] * (2 + OCT),
        out_specs=hbm,
        scratch_shapes=[
            pltpu.VMEM((2, WEIGHT_ROWS, OCT, LANES), jnp.float32),
            pltpu.VMEM((2, 4, OCT, LANES), jnp.float32),
            pltpu.VMEM((OCT * ROWS // 2, 2, LANES), jnp.float32),
            pltpu.VMEM((WEIGHT_ROWS * SLOTS, LANES), jnp.float32),
            *factor_scratch((2,)),
            pltpu.SemaphoreType.DMA((OCT,)),
            pltpu.SemaphoreType.DMA((CHEB,)),
        ],
        compiler_params=pltpu.CompilerParams(vmem_limit_bytes=16 * 2**20),
        cost_estimate=pl.CostEstimate(flops=80 * 2**20, bytes_accessed=20 * 2**20, transcendentals=0),
        name="combine_odd",
    )(me, *even, *blocks)


def on_device(source_weights, wave_vectors, source_centers, phase_coef, phase_kind):
    devices = lax.axis_size("box")
    me = lax.axis_index("box").astype(jnp.int32)[None]
    direct = devices == SLOTS
    if not direct:
        me = jnp.zeros_like(me)
    weights = source_weights.reshape(2, POINTS, SLOTS, LANES).transpose(1, 2, 0, 3)
    weights, *sources = [
        pltpu.with_memory_space_constraint(operand, pltpu.HBM)
        for operand in (weights, phase_coef, wave_vectors, source_centers, phase_kind[None, :])
    ]
    blocks, phases = {}, None
    for steps in PACKS:
        if blocks:
            last = next(reversed(blocks))
            phases, blocks[last] = lax.optimization_barrier((phases, blocks[last]))
        packed, phases = pack(steps, me, weights, phases, sources)
        blocks.update(packed)
    if direct:
        for step in SENDS:
            if step in WAITS:
                earlier = WAITS[step]
                blocks[step], blocks[earlier] = lax.optimization_barrier((blocks[step], blocks[earlier]))
            blocks[step] = lax.ppermute(blocks[step], "box", [(s, s ^ step) for s in range(SLOTS)])
    else:
        whole = jnp.concatenate([blocks[step] for step in range(SLOTS)], axis=2)
        whole = lax.all_to_all(whole, "box", split_axis=2, concat_axis=2, tiled=True)
        blocks = [whole[:, :, s * LANES : (s + 1) * LANES] for s in range(SLOTS)]
    even = combine_even(me, [blocks[step] for step in EVEN_ORDER])
    rows = combine_odd(me, even, [blocks[step] for step in ODD_ORDER])
    return rows.reshape(POINTS, SLOTS, 2, LANES).transpose(2, 0, 1, 3).reshape(2, POINTS, SLOTS * LANES)


def solution(mesh):
    in_specs = (
        P(None, None, ("groups", "box")),
        P(None, None, ("groups", "box")),
        P(None, None, ("groups", "box")),
        P(),
        P(("groups", "box")),
    )
    out_specs = P(None, None, ("groups", "box"))
    return jax.shard_map(on_device, mesh=mesh, in_specs=in_specs, out_specs=out_specs, check_vma=False)
```

```python
import functools
import math

import numpy as np

import jax
import jax.numpy as jnp
from jax import lax
from jax.experimental import pallas as pl
from jax.experimental.pallas import tpu as pltpu
from jax.sharding import PartitionSpec as P

CHEB = 9
POINTS = CHEB * CHEB
KINDS = 4
LEVELS = 4
SLOTS = 1 << LEVELS
LANES = 128
WEIGHT_ROWS = 2 * POINTS
PHASE_ROWS = 4 * LEVELS
ROWS = WEIGHT_ROWS + PHASE_ROWS
OCT = SLOTS // 2
PACKS = ((12, 4, 6, 10), (2, 14, 9, 15, 3, 11, 8), (7, 13, 5, 1, 0))
SENDS = (12, 4, 8, 6, 2, 14, 15, 3, 10, 11, 7, 13, 5, 1, 9)
WAITS = {9: 4, 1: 11}
EVEN_ORDER = (10, 6, 12, 14, 4, 2, 8, 0)
ODD_ORDER = (3, 11, 15, 9, 13, 1, 7, 5)

NODES = np.cos(math.pi * (2.0 * np.arange(CHEB) + 1.0) / (2.0 * CHEB))
NODES[CHEB // 2] = 0.0


def interpolation_halves():
    targets = (NODES - 1.0) / 2.0
    matrix = np.ones((CHEB, CHEB))
    for t in range(CHEB):
        for m in range(CHEB):
            if m != t:
                matrix[t] *= (targets - NODES[m]) / (NODES[t] - NODES[m])
    return (matrix + matrix[::-1]) / 2.0, (matrix - matrix[::-1]) / 2.0


EVEN_HALF, ODD_HALF = interpolation_halves()

SIN_COEFS = (3.1415926401839673, -5.167710090328242, 2.5500776596583643, -0.5982921590176602, 0.0776594073245765)
COS_COEFS = (0.999999953466542, -4.934792858659144, 4.05841191384421, -1.3318801591805476, 0.219696794464285)


def cos_sin_turns(turns):
    rest = turns - jnp.round(turns)
    square = rest * rest
    sine = jnp.float32(SIN_COEFS[-1])
    cosine = jnp.float32(COS_COEFS[-1])
    for s, c in zip(SIN_COEFS[-2::-1], COS_COEFS[-2::-1]):
        sine = sine * square + s
        cosine = cosine * square + c
    sine = sine * rest
    twice = sine + sine
    return 1.0 - twice * sine, twice * cosine


def phase_rows(wave, center, kind, coef_ref):
    a = b = e = jnp.zeros(kind.shape, jnp.float32)
    for index in range(KINDS):
        chosen = kind == index
        a = jnp.where(chosen, coef_ref[index, 0], a)
        b = jnp.where(chosen, coef_ref[index, 1], b)
        e = jnp.where(chosen, coef_ref[index, 2], e)
    k1, k2 = wave
    x1, x2 = center
    level = lax.broadcasted_iota(jnp.int32, k1.shape, 0)
    half = jnp.full(k1.shape, 2.0**-LEVELS, jnp.float32)
    for index in range(1, LEVELS):
        half = jnp.where(level == index, 2.0 ** (index - LEVELS), half)
    scaled = b * k1
    root = a * jnp.sqrt(scaled * scaled + k2 * k2 + 1.0)
    bent = root * e
    constant = x1 * k1 + x2 * k2 + root + bent * x1 * x1
    constant = constant - jnp.round(constant)
    return constant, half * (k1 + 2.0 * bent * x1), half * half * bent, half * k2


def phase_kernel(coef_hbm, wave_hbm, center_hbm, kind_hbm, phases_ref, coef_ref, wave_ref, center_ref, kind_ref, sems):
    copies = [
        pltpu.make_async_copy(source, target, sems.at[index])
        for index, (source, target) in enumerate(
            ((coef_hbm, coef_ref), (wave_hbm, wave_ref), (center_hbm, center_ref), (kind_hbm, kind_ref))
        )
    ]
    for copy in copies:
        copy.start()
    for copy in copies:
        copy.wait()
    rows = phase_rows(
        (wave_ref[:, 0, :], wave_ref[:, 1, :]), (center_ref[:, 0, :], center_ref[:, 1, :]), kind_ref[...], coef_ref
    )
    for index, values in enumerate(rows):
        for level in range(LEVELS):
            row = index * LEVELS + level
            phases_ref[row // 2, row % 2, :] = values[level]


def pack_kernel(steps, first, me_ref, weights_hbm, *refs):
    if first:
        small, refs = refs[:4], refs[4:]
        outs, refs = refs[: len(steps)], refs[len(steps) :]
        phases_ref, block_sems, scratch = refs[0], refs[1], refs[2:]
    else:
        phases_ref, outs, block_sems = refs[0], refs[1 : 1 + len(steps)], refs[1 + len(steps)]
    slots = [me_ref[0] ^ step for step in steps]
    copies = [
        pltpu.make_async_copy(weights_hbm.at[:, slot], out.at[pl.ds(0, POINTS)], block_sems.at[index])
        for index, (slot, out) in enumerate(zip(slots, outs))
    ]
    for copy in copies:
        copy.start()
    if first:
        phase_kernel(*small, phases_ref, *scratch)
    for slot, out in zip(slots, outs):
        out[POINTS:] = phases_ref[:, :, pl.ds(pl.multiple_of(slot * LANES, LANES), LANES)]
    for copy in copies:
        copy.wait()


def pack(steps, me, weights, phases, sources):
    first = phases is None
    vmem = pl.BlockSpec(memory_space=pltpu.VMEM)
    hbm = pl.BlockSpec(memory_space=pltpu.HBM)
    out_shape = [jax.ShapeDtypeStruct((ROWS // 2, 2, LANES), jnp.float32) for _ in steps]
    scratch = [pltpu.SemaphoreType.DMA((len(steps),))]
    if first:
        boxes = sources[-1].shape[-1]
        out_shape.append(jax.ShapeDtypeStruct((PHASE_ROWS // 2, 2, boxes), jnp.float32))
        scratch += [pltpu.SMEM(sources[0].shape, jnp.float32)]
        scratch += [pltpu.VMEM(source.shape, source.dtype) for source in sources[1:]]
        scratch += [pltpu.SemaphoreType.DMA((len(sources),))]
    operands = sources if first else [phases]
    *arrays, last = pl.pallas_call(
        functools.partial(pack_kernel, steps, first),
        out_shape=out_shape,
        in_specs=[pl.BlockSpec(memory_space=pltpu.SMEM), hbm] + ([hbm] * len(sources) if first else [vmem]),
        out_specs=[vmem] * len(out_shape),
        scratch_shapes=scratch,
        compiler_params=pltpu.CompilerParams(vmem_limit_bytes=16 * 2**20),
        cost_estimate=pl.CostEstimate(flops=2**20, bytes_accessed=2**20, transcendentals=0),
        name="pack",
    )(me, weights, *operands)
    if first:
        phases = last
    else:
        arrays.append(last)
    return dict(zip(steps, arrays)), phases


def turn_both_ways(base, step):
    cc, ss = base[0] * step[0], base[1] * step[1]
    sc, cs = base[1] * step[0], base[0] * step[1]
    return (cc - ss, sc + cs), (cc + ss, sc - cs)


def level_factors(level, phases, parent_ref, child_ref, common_ref):
    constant, linear, quadratic, other = phases
    mid = CHEB // 2

    def put(ref, index, pair):
        ref[index + (0,)], ref[index + (1,)] = pair

    def norm(turns):
        cosine, sine = cos_sin_turns(turns)
        return cosine * cosine + sine * sine

    common_ref[mid] = jnp.ones_like(constant)
    for t in range(mid):
        node = float(NODES[t])
        if level % 2 == 0:
            common_ref[t] = common_ref[CHEB - 1 - t] = norm(node * other)
        else:
            common_ref[t] = norm(node * (linear + node * quadratic))
            common_ref[CHEB - 1 - t] = norm(node * (node * quadratic - linear))
    if level % 2 == 0:
        for t in range(CHEB):
            node = float(NODES[t])
            put(parent_ref, (t,), cos_sin_turns(constant + node * (linear + node * quadratic)))
            for child in range(2):
                shifted = (node + 2.0 * child - 1.0) / 2.0
                pair = cos_sin_turns(constant + shifted * (linear + shifted * quadratic))
                put(child_ref, (child, t), pair)
        return
    center = cos_sin_turns(constant)
    centers = [cos_sin_turns(constant + (child - 0.5) * other) for child in range(2)]
    put(parent_ref, (mid,), center)
    for child in range(2):
        put(child_ref, (child, mid), centers[child])
    for t in range(mid):
        half_step = cos_sin_turns((0.5 * float(NODES[t])) * other)
        for child in range(2):
            forth, back = turn_both_ways(centers[child], half_step)
            put(child_ref, (child, t), forth)
            put(child_ref, (child, CHEB - 1 - t), back)
        twice = half_step[1] + half_step[1]
        full_step = (1.0 - twice * half_step[1], twice * half_step[0])
        forth, back = turn_both_ways(center, full_step)
        put(parent_ref, (t,), forth)
        put(parent_ref, (CHEB - 1 - t,), back)


def level_column(column, children, parent_ref, child_ref, common_ref, store):
    scaled = []
    for child in range(2):
        line = []
        for s in range(CHEB):
            real, imag = children[child][s]
            cosine, sine = child_ref[child, s, 0], child_ref[child, s, 1]
            line.append((cosine * real + sine * imag, cosine * imag - sine * real))
        scaled.append(line)
    halves = []
    for part in range(2):
        plus = [scaled[0][s][part] + scaled[1][CHEB - 1 - s][part] for s in range(CHEB)]
        minus = [scaled[0][s][part] - scaled[1][CHEB - 1 - s][part] for s in range(CHEB)]
        halves.append((plus, minus))
    common = common_ref[column]
    mid = CHEB // 2
    for t in range(mid + 1):
        sums = []
        for part in range(2):
            plus, minus = halves[part]
            even = plus[0] * float(EVEN_HALF[t, 0])
            for s in range(1, CHEB):
                even = even + plus[s] * float(EVEN_HALF[t, s])
            if t == mid:
                sums.append((even,))
                continue
            odd = minus[0] * float(ODD_HALF[t, 0])
            for s in range(1, CHEB):
                odd = odd + minus[s] * float(ODD_HALF[t, s])
            sums.append((even + odd, even - odd))
        for which, row in enumerate((t,) if t == mid else (t, CHEB - 1 - t)):
            real, imag = sums[0][which] * common, sums[1][which] * common
            cosine, sine = parent_ref[row, 0], parent_ref[row, 1]
            store(row, cosine * real - sine * imag, cosine * imag + sine * real)


def row_of(level, split, column, part):
    return part + 2 * (split * CHEB + column if level % 2 == 0 else column * CHEB + split)


def join_chips(me, blocks, order, held, sems, work, last_phases, factors, unroll, meanwhile=None):
    copies = []
    for kind, (first, size) in enumerate(((POINTS, ROWS // 2 - POINTS), (0, POINTS))):
        for index, step in enumerate(order):
            spot = ((me ^ step) // 2) * (ROWS // 2) + first
            source = blocks[index].at[pl.ds(first, size)]
            copies.append(pltpu.make_async_copy(source, held.at[pl.ds(spot, size)], sems.at[kind, index]))
            copies[-1].start()
    rows = held.reshape(OCT * ROWS, LANES)

    def received(row):
        return rows[pl.ds(row, OCT, stride=ROWS), :]

    for copy in copies[:OCT]:
        copy.wait()
    for part in range(4):
        last_phases[part] = received(WEIGHT_ROWS + part * LEVELS + LEVELS - 1)
    for level in range(LEVELS - 1):
        phases = [received(WEIGHT_ROWS + part * LEVELS + level) for part in range(4)]
        level_factors(level, phases, *factors[level])
    if meanwhile is not None:
        meanwhile()
    for copy in copies[OCT:]:
        copy.wait()
    for level in range(LEVELS - 1):
        bit = OCT >> (level + 1)

        def column_step(column, _, level=level, bit=bit):
            upper = (lax.broadcasted_iota(jnp.int32, (OCT, LANES), 0) & bit) != 0
            children = [[], []]
            for s in range(CHEB):
                pairs = [[], []]
                for part in range(2):
                    row = row_of(level, s, column, part)
                    value = received(row) if level == 0 else work[row]
                    down = pltpu.roll(value, bit, 0)
                    up = down if 2 * bit == OCT else pltpu.roll(value, OCT - bit, 0)
                    pairs[0].append(jnp.where(upper, down, value))
                    pairs[1].append(jnp.where(upper, value, up))
                children[0].append(tuple(pairs[0]))
                children[1].append(tuple(pairs[1]))

            def store(row, real, imag):
                work[row_of(level, row, column, 0)] = real
                work[row_of(level, row, column, 1)] = imag

            level_column(column, children, *factors[level], store)
            return 0

        lax.fori_loop(0, CHEB, column_step, 0, unroll=unroll)


def even_kernel(me_ref, *refs):
    work, last_phases, held, *factor_refs, sems = refs[OCT:]
    factors = [[ref.at[level] for ref in factor_refs] for level in range(LEVELS - 1)]
    join_chips(me_ref[0], refs, EVEN_ORDER, held, sems, work, last_phases, factors, CHEB)


def odd_kernel(me_ref, even_work, even_phases, *refs):
    out_hbm, work, last_phases, held, out_ref, *factor_refs, sems, out_sems = refs[OCT:]
    me = me_ref[0]
    own = me % 2
    early = [
        pltpu.make_async_copy(even_phases, last_phases.at[own], out_sems.at[1]),
        pltpu.make_async_copy(even_work, work.at[own], out_sems.at[0]),
    ]
    for copy in early:
        copy.start()
    factors = [[ref.at[index] for ref in factor_refs] for index in range(LEVELS + 1)]
    level = LEVELS - 1

    def last_factors():
        early[0].wait()
        for parity in range(2):
            level_factors(level, [last_phases[parity, part] for part in range(4)], *factors[level + parity])

    join_chips(
        me, refs, ODD_ORDER, held, sems, work.at[1 - own], last_phases.at[1 - own], factors, 3, last_factors
    )
    early[1].wait()

    chunk = out_ref.shape[0] // CHEB

    def leave(column):
        rows = pl.ds(pl.multiple_of(column * chunk, 8), chunk)
        return pltpu.make_async_copy(out_ref.at[rows, :], out_hbm.at[rows, :], out_sems.at[column])

    def column_step(column, _):
        children = [
            [tuple(work[child, row_of(level, s, column, part)] for part in range(2)) for s in range(CHEB)]
            for child in range(2)
        ]
        for parity in range(2):

            def store(row, real, imag, parity=parity):
                start = row_of(level, row, column, 0) * SLOTS + 2 * parity
                out_ref[pl.ds(start, OCT, stride=4), :] = real
                out_ref[pl.ds(start + 1, OCT, stride=4), :] = imag

            level_column(column, children, *factors[level + parity], store)
        leave(column).start()
        return 0

    lax.fori_loop(0, CHEB, column_step, 0, unroll=3)
    for column in range(CHEB):
        leave(column).wait()


def factor_scratch(count):
    return [
        pltpu.VMEM(count + (CHEB, 2, OCT, LANES), jnp.float32),
        pltpu.VMEM(count + (2, CHEB, 2, OCT, LANES), jnp.float32),
        pltpu.VMEM(count + (CHEB, OCT, LANES), jnp.float32),
    ]


def combine_even(me, blocks):
    vmem = pl.BlockSpec(memory_space=pltpu.VMEM)
    return pl.pallas_call(
        even_kernel,
        out_shape=[
            jax.ShapeDtypeStruct((WEIGHT_ROWS, OCT, LANES), jnp.float32),
            jax.ShapeDtypeStruct((4, OCT, LANES), jnp.float32),
        ],
        in_specs=[pl.BlockSpec(memory_space=pltpu.SMEM)] + [pl.BlockSpec(memory_space=pl.ANY)] * OCT,
        out_specs=[vmem, vmem],
        scratch_shapes=[
            pltpu.VMEM((OCT * ROWS // 2, 2, LANES), jnp.float32),
            *factor_scratch((LEVELS - 1,)),
            pltpu.SemaphoreType.DMA((2, OCT)),
        ],
        compiler_params=pltpu.CompilerParams(vmem_limit_bytes=16 * 2**20),
        cost_estimate=pl.CostEstimate(flops=40 * 2**20, bytes_accessed=12 * 2**20, transcendentals=0),
        name="combine_even",
    )(me, *blocks)


def combine_odd(me, even, blocks):
    hbm = pl.BlockSpec(memory_space=pltpu.HBM)
    anywhere = pl.BlockSpec(memory_space=pl.ANY)
    return pl.pallas_call(
        odd_kernel,
        out_shape=jax.ShapeDtypeStruct((WEIGHT_ROWS * SLOTS, LANES), jnp.float32),
        in_specs=[pl.BlockSpec(memory_space=pltpu.SMEM)] + [anywhere] * (2 + OCT),
        out_specs=hbm,
        scratch_shapes=[
            pltpu.VMEM((2, WEIGHT_ROWS, OCT, LANES), jnp.float32),
            pltpu.VMEM((2, 4, OCT, LANES), jnp.float32),
            pltpu.VMEM((OCT * ROWS // 2, 2, LANES), jnp.float32),
            pltpu.VMEM((WEIGHT_ROWS * SLOTS, LANES), jnp.float32),
            *factor_scratch((LEVELS + 1,)),
            pltpu.SemaphoreType.DMA((2, OCT)),
            pltpu.SemaphoreType.DMA((CHEB,)),
        ],
        compiler_params=pltpu.CompilerParams(vmem_limit_bytes=16 * 2**20),
        cost_estimate=pl.CostEstimate(flops=80 * 2**20, bytes_accessed=20 * 2**20, transcendentals=0),
        name="combine_odd",
    )(me, *even, *blocks)


def on_device(source_weights, wave_vectors, source_centers, phase_coef, phase_kind):
    devices = lax.axis_size("box")
    me = lax.axis_index("box").astype(jnp.int32)[None]
    direct = devices == SLOTS
    if not direct:
        me = jnp.zeros_like(me)
    weights = source_weights.reshape(2, POINTS, SLOTS, LANES).transpose(1, 2, 0, 3)
    weights, *sources = [
        pltpu.with_memory_space_constraint(operand, pltpu.HBM)
        for operand in (weights, phase_coef, wave_vectors, source_centers, phase_kind[None, :])
    ]
    blocks, phases = {}, None
    for steps in PACKS:
        if blocks:
            last = next(reversed(blocks))
            phases, blocks[last] = lax.optimization_barrier((phases, blocks[last]))
        packed, phases = pack(steps, me, weights, phases, sources)
        blocks.update(packed)
    if direct:
        for step in SENDS:
            if step in WAITS:
                earlier = WAITS[step]
                blocks[step], blocks[earlier] = lax.optimization_barrier((blocks[step], blocks[earlier]))
            blocks[step] = lax.ppermute(blocks[step], "box", [(s, s ^ step) for s in range(SLOTS)])
    else:
        whole = jnp.concatenate([blocks[step] for step in range(SLOTS)], axis=2)
        whole = lax.all_to_all(whole, "box", split_axis=2, concat_axis=2, tiled=True)
        blocks = [whole[:, :, s * LANES : (s + 1) * LANES] for s in range(SLOTS)]
    even = combine_even(me, [blocks[step] for step in EVEN_ORDER])
    rows = combine_odd(me, even, [blocks[step] for step in ODD_ORDER])
    return rows.reshape(POINTS, SLOTS, 2, LANES).transpose(2, 0, 1, 3).reshape(2, POINTS, SLOTS * LANES)


def solution(mesh):
    in_specs = (
        P(None, None, ("groups", "box")),
        P(None, None, ("groups", "box")),
        P(None, None, ("groups", "box")),
        P(),
        P(("groups", "box")),
    )
    out_specs = P(None, None, ("groups", "box"))
    return jax.shard_map(on_device, mesh=mesh, in_specs=in_specs, out_specs=out_specs, check_vma=False)
```

```python
import functools
import math

import numpy as np

import jax
import jax.numpy as jnp
from jax import lax
from jax.experimental import pallas as pl
from jax.experimental.pallas import tpu as pltpu
from jax.sharding import PartitionSpec as P

CHEB = 9
POINTS = CHEB * CHEB
KINDS = 4
LEVELS = 4
SLOTS = 1 << LEVELS
LANES = 128
WEIGHT_ROWS = 2 * POINTS
PHASE_ROWS = 4 * LEVELS
ROWS = WEIGHT_ROWS + PHASE_ROWS
OCT = SLOTS // 2
PACKS = ((12, 4, 6, 10), (2, 14, 9, 15, 3, 11, 8), (7, 13, 5, 1, 0))
SENDS = (12, 4, 8, 6, 2, 14, 15, 3, 10, 11, 7, 13, 5, 1, 9)
WAITS = {9: 4, 1: 11}
EVEN_ORDER = (10, 6, 12, 14, 4, 2, 8, 0)
ODD_ORDER = (3, 11, 15, 9, 13, 1, 7, 5)

NODES = np.cos(math.pi * (2.0 * np.arange(CHEB) + 1.0) / (2.0 * CHEB))
NODES[CHEB // 2] = 0.0


def interpolation_halves():
    targets = (NODES - 1.0) / 2.0
    matrix = np.ones((CHEB, CHEB))
    for t in range(CHEB):
        for m in range(CHEB):
            if m != t:
                matrix[t] *= (targets - NODES[m]) / (NODES[t] - NODES[m])
    return (matrix + matrix[::-1]) / 2.0, (matrix - matrix[::-1]) / 2.0


EVEN_HALF, ODD_HALF = interpolation_halves()
ONES = (CHEB // 2, CHEB - 2)
ROW_SCALE = EVEN_HALF[:, ONES[1]].copy()
COLUMN_SCALE = EVEN_HALF[ONES[0]] / ROW_SCALE[ONES[0]]
EVEN_HALF, ODD_HALF = (half / ROW_SCALE[:, None] / COLUMN_SCALE for half in (EVEN_HALF, ODD_HALF))

SIN_COEFS = (3.1415926401839673, -5.167710090328242, 2.5500776596583643, -0.5982921590176602, 0.0776594073245765)
COS_COEFS = (0.999999953466542, -4.934792858659144, 4.05841191384421, -1.3318801591805476, 0.219696794464285)


def cos_sin_turns(turns):
    rest = turns - jnp.round(turns)
    square = rest * rest
    sine = jnp.float32(SIN_COEFS[-1])
    cosine = jnp.float32(COS_COEFS[-1])
    for s, c in zip(SIN_COEFS[-2::-1], COS_COEFS[-2::-1]):
        sine = sine * square + s
        cosine = cosine * square + c
    sine = sine * rest
    twice = sine + sine
    return 1.0 - twice * sine, twice * cosine


def phase_rows(wave, center, kind, coef_ref):
    a = b = e = jnp.zeros(kind.shape, jnp.float32)
    for index in range(KINDS):
        chosen = kind == index
        a = jnp.where(chosen, coef_ref[index, 0], a)
        b = jnp.where(chosen, coef_ref[index, 1], b)
        e = jnp.where(chosen, coef_ref[index, 2], e)
    k1, k2 = wave
    x1, x2 = center
    level = lax.broadcasted_iota(jnp.int32, k1.shape, 0)
    half = jnp.full(k1.shape, 2.0**-LEVELS, jnp.float32)
    for index in range(1, LEVELS):
        half = jnp.where(level == index, 2.0 ** (index - LEVELS), half)
    scaled = b * k1
    root = a * jnp.sqrt(scaled * scaled + k2 * k2 + 1.0)
    bent = root * e
    constant = x1 * k1 + x2 * k2 + root + bent * x1 * x1
    constant = constant - jnp.round(constant)
    return constant, half * (k1 + 2.0 * bent * x1), half * half * bent, half * k2


def pack_kernel(steps, me_ref, weights_hbm, coef_hbm, wave_hbm, center_hbm, kind_hbm, *refs):
    outs, (coef_ref, wave_ref, center_ref, kind_ref, small_sems, block_sems) = refs[: len(steps)], refs[len(steps) :]
    small, large = [pltpu.make_async_copy(coef_hbm, coef_ref, small_sems.at[3, 0])], []
    for index, (step, out) in enumerate(zip(steps, outs)):
        slot = me_ref[0] ^ step
        there = pl.ds(pl.multiple_of(slot * LANES, LANES), LANES)
        here = pl.ds(index * LANES, LANES)
        small += [
            pltpu.make_async_copy(wave_hbm.at[:, :, there], wave_ref.at[:, :, here], small_sems.at[0, index]),
            pltpu.make_async_copy(center_hbm.at[:, :, there], center_ref.at[:, :, here], small_sems.at[1, index]),
            pltpu.make_async_copy(kind_hbm.at[:, there], kind_ref.at[:, here], small_sems.at[2, index]),
        ]
        large.append(pltpu.make_async_copy(weights_hbm.at[:, slot], out.at[pl.ds(0, POINTS)], block_sems.at[index]))
    for copy in small + large:
        copy.start()
    for copy in small:
        copy.wait()
    rows = phase_rows(
        (wave_ref[:, 0, :], wave_ref[:, 1, :]), (center_ref[:, 0, :], center_ref[:, 1, :]), kind_ref[...], coef_ref
    )
    for part, values in enumerate(rows):
        for level in range(LEVELS):
            row = part * LEVELS + level
            for index, out in enumerate(outs):
                out[POINTS + row // 2, row % 2, :] = values[level, index * LANES : (index + 1) * LANES]
    for copy in large:
        copy.wait()


def pack(steps, me, weights, sources):
    hbm = pl.BlockSpec(memory_space=pltpu.HBM)
    count = len(steps)
    arrays = pl.pallas_call(
        functools.partial(pack_kernel, steps),
        out_shape=[jax.ShapeDtypeStruct((ROWS // 2, 2, LANES), jnp.float32)] * count,
        in_specs=[pl.BlockSpec(memory_space=pltpu.SMEM)] + [hbm] * (1 + len(sources)),
        out_specs=[pl.BlockSpec(memory_space=pltpu.VMEM)] * count,
        scratch_shapes=[
            pltpu.SMEM(sources[0].shape, jnp.float32),
            pltpu.VMEM((LEVELS, 2, count * LANES), jnp.float32),
            pltpu.VMEM((LEVELS, 2, count * LANES), jnp.float32),
            pltpu.VMEM((1, count * LANES), jnp.int32),
            pltpu.SemaphoreType.DMA((4, count)),
            pltpu.SemaphoreType.DMA((count,)),
        ],
        compiler_params=pltpu.CompilerParams(vmem_limit_bytes=16 * 2**20),
        cost_estimate=pl.CostEstimate(flops=2**20, bytes_accessed=2**20, transcendentals=0),
        name="pack",
    )(me, weights, *sources)
    return dict(zip(steps, arrays))


def turn_both_ways(base, step):
    cc, ss = base[0] * step[0], base[1] * step[1]
    sc, cs = base[1] * step[0], base[0] * step[1]
    return (cc - ss, sc + cs), (cc + ss, sc - cs)


def level_factors(level, phases, parent_ref, child_ref, common_ref):
    constant, linear, quadratic, other = phases
    mid = CHEB // 2

    def put(ref, index, pair):
        scale = ROW_SCALE[index[0]]
        if len(index) > 1:
            scale = COLUMN_SCALE[index[1] if index[0] == 0 else CHEB - 1 - index[1]]
        ref[index + (0,)], ref[index + (1,)] = (float(scale) * value for value in pair)

    def norm(turns):
        cosine, sine = cos_sin_turns(turns)
        return cosine * cosine + sine * sine

    common_ref[mid] = jnp.ones_like(constant)
    for t in range(mid):
        node = float(NODES[t])
        if level % 2 == 0:
            common_ref[t] = common_ref[CHEB - 1 - t] = norm(node * other)
        else:
            common_ref[t] = norm(node * (linear + node * quadratic))
            common_ref[CHEB - 1 - t] = norm(node * (node * quadratic - linear))
    if level % 2 == 0:
        for t in range(CHEB):
            node = float(NODES[t])
            put(parent_ref, (t,), cos_sin_turns(constant + node * (linear + node * quadratic)))
            for child in range(2):
                shifted = (node + 2.0 * child - 1.0) / 2.0
                pair = cos_sin_turns(constant + shifted * (linear + shifted * quadratic))
                put(child_ref, (child, t), pair)
        return
    center = cos_sin_turns(constant)
    centers = [cos_sin_turns(constant + (child - 0.5) * other) for child in range(2)]
    put(parent_ref, (mid,), center)
    for child in range(2):
        put(child_ref, (child, mid), centers[child])
    for t in range(mid):
        half_step = cos_sin_turns((0.5 * float(NODES[t])) * other)
        for child in range(2):
            forth, back = turn_both_ways(centers[child], half_step)
            put(child_ref, (child, t), forth)
            put(child_ref, (child, CHEB - 1 - t), back)
        twice = half_step[1] + half_step[1]
        full_step = (1.0 - twice * half_step[1], twice * half_step[0])
        forth, back = turn_both_ways(center, full_step)
        put(parent_ref, (t,), forth)
        put(parent_ref, (CHEB - 1 - t,), back)


def level_column(column, children, parent_ref, child_ref, common_ref, store):
    scaled = []
    for child in range(2):
        line = []
        for s in range(CHEB):
            real, imag = children[child][s]
            cosine, sine = child_ref[child, s, 0], child_ref[child, s, 1]
            line.append((cosine * real + sine * imag, cosine * imag - sine * real))
        scaled.append(line)
    halves = []
    for part in range(2):
        plus = [scaled[0][s][part] + scaled[1][CHEB - 1 - s][part] for s in range(CHEB)]
        minus = [scaled[0][s][part] - scaled[1][CHEB - 1 - s][part] for s in range(CHEB)]
        halves.append((plus, minus))
    common = common_ref[column]
    mid = CHEB // 2
    for t in range(mid + 1):
        sums = []
        for part in range(2):
            plus, minus = halves[part]
            even = None
            for s in range(CHEB):
                term = plus[s] if t == ONES[0] or s == ONES[1] else plus[s] * float(EVEN_HALF[t, s])
                even = term if even is None else even + term
            if t == mid:
                sums.append((even,))
                continue
            odd = minus[0] * float(ODD_HALF[t, 0])
            for s in range(1, CHEB):
                odd = odd + minus[s] * float(ODD_HALF[t, s])
            sums.append((even + odd, even - odd))
        for which, row in enumerate((t,) if t == mid else (t, CHEB - 1 - t)):
            real, imag = sums[0][which] * common, sums[1][which] * common
            cosine, sine = parent_ref[row, 0], parent_ref[row, 1]
            store(row, cosine * real - sine * imag, cosine * imag + sine * real)


def row_of(level, split, column, part):
    return part + 2 * (split * CHEB + column if level % 2 == 0 else column * CHEB + split)


def join_chips(me, blocks, order, held, sems, work, last_phases, factors, unroll, meanwhile=None):
    copies = []
    for kind, (first, size) in enumerate(((POINTS, ROWS // 2 - POINTS), (0, POINTS))):
        for index, step in enumerate(order):
            spot = ((me ^ step) // 2) * (ROWS // 2) + first
            source = blocks[index].at[pl.ds(first, size)]
            copies.append(pltpu.make_async_copy(source, held.at[pl.ds(spot, size)], sems.at[kind, index]))
            copies[-1].start()
    rows = held.reshape(OCT * ROWS, LANES)

    def received(row):
        return rows[pl.ds(row, OCT, stride=ROWS), :]

    for copy in copies[:OCT]:
        copy.wait()
    for part in range(4):
        last_phases[part] = received(WEIGHT_ROWS + part * LEVELS + LEVELS - 1)
    for level in range(LEVELS - 1):
        phases = [received(WEIGHT_ROWS + part * LEVELS + level) for part in range(4)]
        level_factors(level, phases, *factors[level])
    if meanwhile is not None:
        meanwhile()
    for copy in copies[OCT:]:
        copy.wait()
    for level in range(LEVELS - 1):
        bit = OCT >> (level + 1)

        def column_step(column, _, level=level, bit=bit):
            upper = (lax.broadcasted_iota(jnp.int32, (OCT, LANES), 0) & bit) != 0
            children = [[], []]
            for s in range(CHEB):
                pairs = [[], []]
                for part in range(2):
                    row = row_of(level, s, column, part)
                    value = received(row) if level == 0 else work[row]
                    down = pltpu.roll(value, bit, 0)
                    up = down if 2 * bit == OCT else pltpu.roll(value, OCT - bit, 0)
                    pairs[0].append(jnp.where(upper, down, value))
                    pairs[1].append(jnp.where(upper, value, up))
                children[0].append(tuple(pairs[0]))
                children[1].append(tuple(pairs[1]))

            def store(row, real, imag):
                work[row_of(level, row, column, 0)] = real
                work[row_of(level, row, column, 1)] = imag

            level_column(column, children, *factors[level], store)
            return 0

        lax.fori_loop(0, CHEB, column_step, 0, unroll=unroll)


def even_kernel(me_ref, *refs):
    work, last_phases, held, *factor_refs, sems = refs[OCT:]
    factors = [[ref.at[level] for ref in factor_refs] for level in range(LEVELS - 1)]
    join_chips(me_ref[0], refs, EVEN_ORDER, held, sems, work, last_phases, factors, 3)


def odd_kernel(me_ref, even_work, even_phases, *refs):
    out_hbm, work, last_phases, held, out_ref, *factor_refs, sems, out_sems = refs[OCT:]
    me = me_ref[0]
    own = me % 2
    early = [
        pltpu.make_async_copy(even_phases, last_phases.at[own], out_sems.at[1]),
        pltpu.make_async_copy(even_work, work.at[own], out_sems.at[0]),
    ]
    for copy in early:
        copy.start()
    factors = [[ref.at[index] for ref in factor_refs] for index in range(LEVELS + 1)]
    level = LEVELS - 1

    def last_factors():
        early[0].wait()
        for parity in range(2):
            level_factors(level, [last_phases[parity, part] for part in range(4)], *factors[level + parity])

    join_chips(
        me, refs, ODD_ORDER, held, sems, work.at[1 - own], last_phases.at[1 - own], factors, 3, last_factors
    )
    early[1].wait()

    chunk = out_ref.shape[0] // CHEB

    def leave(column):
        rows = pl.ds(pl.multiple_of(column * chunk, 8), chunk)
        return pltpu.make_async_copy(out_ref.at[rows, :], out_hbm.at[rows, :], out_sems.at[column])

    def column_step(column, _):
        children = [
            [tuple(work[child, row_of(level, s, column, part)] for part in range(2)) for s in range(CHEB)]
            for child in range(2)
        ]
        for parity in range(2):

            def store(row, real, imag, parity=parity):
                start = row_of(level, row, column, 0) * SLOTS + 2 * parity
                out_ref[pl.ds(start, OCT, stride=4), :] = real
                out_ref[pl.ds(start + 1, OCT, stride=4), :] = imag

            level_column(column, children, *factors[level + parity], store)
        leave(column).start()
        return 0

    lax.fori_loop(0, CHEB, column_step, 0, unroll=3)
    for column in range(CHEB):
        leave(column).wait()


def factor_scratch(count):
    return [
        pltpu.VMEM(count + (CHEB, 2, OCT, LANES), jnp.float32),
        pltpu.VMEM(count + (2, CHEB, 2, OCT, LANES), jnp.float32),
        pltpu.VMEM(count + (CHEB, OCT, LANES), jnp.float32),
    ]


def combine_even(me, blocks):
    vmem = pl.BlockSpec(memory_space=pltpu.VMEM)
    return pl.pallas_call(
        even_kernel,
        out_shape=[
            jax.ShapeDtypeStruct((WEIGHT_ROWS, OCT, LANES), jnp.float32),
            jax.ShapeDtypeStruct((4, OCT, LANES), jnp.float32),
        ],
        in_specs=[pl.BlockSpec(memory_space=pltpu.SMEM)] + [pl.BlockSpec(memory_space=pl.ANY)] * OCT,
        out_specs=[vmem, vmem],
        scratch_shapes=[
            pltpu.VMEM((OCT * ROWS // 2, 2, LANES), jnp.float32),
            *factor_scratch((LEVELS - 1,)),
            pltpu.SemaphoreType.DMA((2, OCT)),
        ],
        compiler_params=pltpu.CompilerParams(vmem_limit_bytes=16 * 2**20),
        cost_estimate=pl.CostEstimate(flops=40 * 2**20, bytes_accessed=12 * 2**20, transcendentals=0),
        name="combine_even",
    )(me, *blocks)


def combine_odd(me, even, blocks):
    hbm = pl.BlockSpec(memory_space=pltpu.HBM)
    anywhere = pl.BlockSpec(memory_space=pl.ANY)
    return pl.pallas_call(
        odd_kernel,
        out_shape=jax.ShapeDtypeStruct((WEIGHT_ROWS * SLOTS, LANES), jnp.float32),
        in_specs=[pl.BlockSpec(memory_space=pltpu.SMEM)] + [anywhere] * (2 + OCT),
        out_specs=hbm,
        scratch_shapes=[
            pltpu.VMEM((2, WEIGHT_ROWS, OCT, LANES), jnp.float32),
            pltpu.VMEM((2, 4, OCT, LANES), jnp.float32),
            pltpu.VMEM((OCT * ROWS // 2, 2, LANES), jnp.float32),
            pltpu.VMEM((WEIGHT_ROWS * SLOTS, LANES), jnp.float32),
            *factor_scratch((LEVELS + 1,)),
            pltpu.SemaphoreType.DMA((2, OCT)),
            pltpu.SemaphoreType.DMA((CHEB,)),
        ],
        compiler_params=pltpu.CompilerParams(vmem_limit_bytes=16 * 2**20),
        cost_estimate=pl.CostEstimate(flops=80 * 2**20, bytes_accessed=20 * 2**20, transcendentals=0),
        name="combine_odd",
    )(me, *even, *blocks)


def on_device(source_weights, wave_vectors, source_centers, phase_coef, phase_kind):
    devices = lax.axis_size("box")
    me = lax.axis_index("box").astype(jnp.int32)[None]
    direct = devices == SLOTS
    if not direct:
        me = jnp.zeros_like(me)
    weights = source_weights.reshape(2, POINTS, SLOTS, LANES).transpose(1, 2, 0, 3)
    weights, *sources = [
        pltpu.with_memory_space_constraint(operand, pltpu.HBM)
        for operand in (weights, phase_coef, wave_vectors, source_centers, phase_kind[None, :])
    ]
    blocks, slot = {}, me
    for steps in PACKS:
        if blocks:
            last = next(reversed(blocks))
            slot, blocks[last] = lax.optimization_barrier((slot, blocks[last]))
        blocks.update(pack(steps, slot, weights, sources))
    if direct:
        for step in SENDS:
            if step in WAITS:
                earlier = WAITS[step]
                blocks[step], blocks[earlier] = lax.optimization_barrier((blocks[step], blocks[earlier]))
            blocks[step] = lax.ppermute(blocks[step], "box", [(s, s ^ step) for s in range(SLOTS)])
    else:
        whole = jnp.concatenate([blocks[step] for step in range(SLOTS)], axis=2)
        whole = lax.all_to_all(whole, "box", split_axis=2, concat_axis=2, tiled=True)
        blocks = [whole[:, :, s * LANES : (s + 1) * LANES] for s in range(SLOTS)]
    even = combine_even(me, [blocks[step] for step in EVEN_ORDER])
    rows = combine_odd(me, even, [blocks[step] for step in ODD_ORDER])
    return rows.reshape(POINTS, SLOTS, 2, LANES).transpose(2, 0, 1, 3).reshape(2, POINTS, SLOTS * LANES)


def solution(mesh):
    in_specs = (
        P(None, None, ("groups", "box")),
        P(None, None, ("groups", "box")),
        P(None, None, ("groups", "box")),
        P(),
        P(("groups", "box")),
    )
    out_specs = P(None, None, ("groups", "box"))
    return jax.shard_map(on_device, mesh=mesh, in_specs=in_specs, out_specs=out_specs, check_vma=False)
```

```python
import functools
import math

import numpy as np

import jax
import jax.numpy as jnp
from jax import lax
from jax.experimental import pallas as pl
from jax.experimental.pallas import tpu as pltpu
from jax.sharding import PartitionSpec as P

CHEB = 9
POINTS = CHEB * CHEB
KINDS = 4
LEVELS = 4
SLOTS = 1 << LEVELS
LANES = 128
WEIGHT_ROWS = 2 * POINTS
PHASE_ROWS = 4 * LEVELS
ROWS = WEIGHT_ROWS + PHASE_ROWS
PAIRS = ROWS // 2
ACROSS_Y = 2
OCT = SLOTS // 2
PACKS = (((8, 10),), ((9, 11), (13,), (15,), (4, 6), (7,), (2,), (14,), (5,), (12,), (1, 3), (0,)))
ONWARD = {"even": (2, 8, 4), "odd": (9, 1)}
SENDS = (8, 14, 12, 9, 13, 4, 7, 5, 15, 1, "even", "odd")
WAITS = {"odd": 4, 15: 4, "even": 5, 14: 8}
EVEN_ORDER = (14, 4, "even", 8, 12, 0)
ODD_ORDER = (13, 1, 5, 15, 9, "odd", 7)

NODES = np.cos(math.pi * (2.0 * np.arange(CHEB) + 1.0) / (2.0 * CHEB))
NODES[CHEB // 2] = 0.0


def interpolation_halves():
    targets = (NODES - 1.0) / 2.0
    matrix = np.ones((CHEB, CHEB))
    for t in range(CHEB):
        for m in range(CHEB):
            if m != t:
                matrix[t] *= (targets - NODES[m]) / (NODES[t] - NODES[m])
    return (matrix + matrix[::-1]) / 2.0, (matrix - matrix[::-1]) / 2.0


EVEN_HALF, ODD_HALF = interpolation_halves()

SIN_COEFS = (3.1415926401839673, -5.167710090328242, 2.5500776596583643, -0.5982921590176602, 0.0776594073245765)
COS_COEFS = (0.999999953466542, -4.934792858659144, 4.05841191384421, -1.3318801591805476, 0.219696794464285)


def cos_sin_turns(turns):
    rest = turns - jnp.round(turns)
    square = rest * rest
    sine = jnp.float32(SIN_COEFS[-1])
    cosine = jnp.float32(COS_COEFS[-1])
    for s, c in zip(SIN_COEFS[-2::-1], COS_COEFS[-2::-1]):
        sine = sine * square + s
        cosine = cosine * square + c
    sine = sine * rest
    twice = sine + sine
    return 1.0 - twice * sine, twice * cosine


def phase_rows(wave, center, kind, coef_ref):
    a = b = e = jnp.zeros(kind.shape, jnp.float32)
    for index in range(KINDS):
        chosen = kind == index
        a = jnp.where(chosen, coef_ref[index, 0], a)
        b = jnp.where(chosen, coef_ref[index, 1], b)
        e = jnp.where(chosen, coef_ref[index, 2], e)
    k1, k2 = wave
    x1, x2 = center
    level = lax.broadcasted_iota(jnp.int32, k1.shape, 0)
    half = jnp.full(k1.shape, 2.0**-LEVELS, jnp.float32)
    for index in range(1, LEVELS):
        half = jnp.where(level == index, 2.0 ** (index - LEVELS), half)
    scaled = b * k1
    root = a * jnp.sqrt(scaled * scaled + k2 * k2 + 1.0)
    bent = root * e
    constant = x1 * k1 + x2 * k2 + root + bent * x1 * x1
    constant = constant - jnp.round(constant)
    return constant, half * (k1 + 2.0 * bent * x1), half * half * bent, half * k2


def phase_kernel(coef_hbm, wave_hbm, center_hbm, kind_hbm, phases_ref, coef_ref, wave_ref, center_ref, kind_ref, sems):
    copies = [
        pltpu.make_async_copy(source, target, sems.at[index])
        for index, (source, target) in enumerate(
            ((coef_hbm, coef_ref), (wave_hbm, wave_ref), (center_hbm, center_ref), (kind_hbm, kind_ref))
        )
    ]
    for copy in copies:
        copy.start()
    for copy in copies:
        copy.wait()
    rows = phase_rows(
        (wave_ref[:, 0, :], wave_ref[:, 1, :]), (center_ref[:, 0, :], center_ref[:, 1, :]), kind_ref[...], coef_ref
    )
    for index, values in enumerate(rows):
        for level in range(LEVELS):
            row = index * LEVELS + level
            phases_ref[row // 2, row % 2, :] = values[level]


def pack_kernel(messages, first, me_ref, weights_hbm, *refs):
    count = len(messages)
    if first:
        small, refs = refs[:4], refs[4:]
        arrays, phases_ref, block_sems, scratch = refs[:count], refs[count], refs[count + 1], refs[count + 2 :]
    else:
        phases_ref, arrays, block_sems = refs[0], refs[1 : 1 + count], refs[1 + count]
    slots = [me_ref[0] ^ step for message in messages for step in message]
    outs = [
        array.at[pl.ds(index * PAIRS, PAIRS)]
        for message, array in zip(messages, arrays)
        for index in range(len(message))
    ]
    copies = [
        pltpu.make_async_copy(weights_hbm.at[:, slot], out.at[pl.ds(0, POINTS)], block_sems.at[index])
        for index, (slot, out) in enumerate(zip(slots, outs))
    ]
    for copy in copies:
        copy.start()
    if first:
        phase_kernel(*small, phases_ref, *scratch)
    for slot, out in zip(slots, outs):
        out[POINTS:] = phases_ref[:, :, pl.ds(pl.multiple_of(slot * LANES, LANES), LANES)]
    for copy in copies:
        copy.wait()


def pack(messages, me, weights, phases, sources):
    first = phases is None
    vmem = pl.BlockSpec(memory_space=pltpu.VMEM)
    hbm = pl.BlockSpec(memory_space=pltpu.HBM)
    out_shape = [jax.ShapeDtypeStruct((len(m) * PAIRS, 2, LANES), jnp.float32) for m in messages]
    scratch = [pltpu.SemaphoreType.DMA((sum(map(len, messages)),))]
    if first:
        boxes = sources[-1].shape[-1]
        out_shape.append(jax.ShapeDtypeStruct((PHASE_ROWS // 2, 2, boxes), jnp.float32))
        scratch += [pltpu.SMEM(sources[0].shape, jnp.float32)]
        scratch += [pltpu.VMEM(source.shape, source.dtype) for source in sources[1:]]
        scratch += [pltpu.SemaphoreType.DMA((len(sources),))]
    operands = sources if first else [phases]
    *arrays, last = pl.pallas_call(
        functools.partial(pack_kernel, messages, first),
        out_shape=out_shape,
        in_specs=[pl.BlockSpec(memory_space=pltpu.SMEM), hbm] + ([hbm] * len(sources) if first else [vmem]),
        out_specs=[vmem] * len(out_shape),
        scratch_shapes=scratch,
        compiler_params=pltpu.CompilerParams(vmem_limit_bytes=16 * 2**20),
        cost_estimate=pl.CostEstimate(flops=2**20, bytes_accessed=2**20, transcendentals=0),
        name="pack",
    )(me, weights, *operands)
    if first:
        phases = last
    else:
        arrays.append(last)
    return {m[0]: array for m, array in zip(messages, arrays)}, phases


def turn_both_ways(base, step):
    cc, ss = base[0] * step[0], base[1] * step[1]
    sc, cs = base[1] * step[0], base[0] * step[1]
    return (cc - ss, sc + cs), (cc + ss, sc - cs)


def level_factors(level, phases, parent_ref, child_ref, common_ref):
    constant, linear, quadratic, other = phases
    mid = CHEB // 2

    def put(ref, index, pair):
        ref[index + (0,)], ref[index + (1,)] = pair

    def norm(turns):
        cosine, sine = cos_sin_turns(turns)
        return cosine * cosine + sine * sine

    common_ref[mid] = jnp.ones_like(constant)
    for t in range(mid):
        node = float(NODES[t])
        if level % 2 == 0:
            common_ref[t] = common_ref[CHEB - 1 - t] = norm(node * other)
        else:
            common_ref[t] = norm(node * (linear + node * quadratic))
            common_ref[CHEB - 1 - t] = norm(node * (node * quadratic - linear))
    if level % 2 == 0:
        for t in range(CHEB):
            node = float(NODES[t])
            put(parent_ref, (t,), cos_sin_turns(constant + node * (linear + node * quadratic)))
            for child in range(2):
                shifted = (node + 2.0 * child - 1.0) / 2.0
                pair = cos_sin_turns(constant + shifted * (linear + shifted * quadratic))
                put(child_ref, (child, t), pair)
        return
    center = cos_sin_turns(constant)
    centers = [cos_sin_turns(constant + (child - 0.5) * other) for child in range(2)]
    put(parent_ref, (mid,), center)
    for child in range(2):
        put(child_ref, (child, mid), centers[child])
    for t in range(mid):
        half_step = cos_sin_turns((0.5 * float(NODES[t])) * other)
        for child in range(2):
            forth, back = turn_both_ways(centers[child], half_step)
            put(child_ref, (child, t), forth)
            put(child_ref, (child, CHEB - 1 - t), back)
        twice = half_step[1] + half_step[1]
        full_step = (1.0 - twice * half_step[1], twice * half_step[0])
        forth, back = turn_both_ways(center, full_step)
        put(parent_ref, (t,), forth)
        put(parent_ref, (CHEB - 1 - t,), back)


def level_column(column, children, parent_ref, child_ref, common_ref, store):
    scaled = []
    for child in range(2):
        line = []
        for s in range(CHEB):
            real, imag = children[child][s]
            cosine, sine = child_ref[child, s, 0], child_ref[child, s, 1]
            line.append((cosine * real + sine * imag, cosine * imag - sine * real))
        scaled.append(line)
    halves = []
    for part in range(2):
        plus = [scaled[0][s][part] + scaled[1][CHEB - 1 - s][part] for s in range(CHEB)]
        minus = [scaled[0][s][part] - scaled[1][CHEB - 1 - s][part] for s in range(CHEB)]
        halves.append((plus, minus))
    common = common_ref[column]
    mid = CHEB // 2
    for t in range(mid + 1):
        sums = []
        for part in range(2):
            plus, minus = halves[part]
            even = plus[0] * float(EVEN_HALF[t, 0])
            for s in range(1, CHEB):
                even = even + plus[s] * float(EVEN_HALF[t, s])
            if t == mid:
                sums.append((even,))
                continue
            odd = minus[0] * float(ODD_HALF[t, 0])
            for s in range(1, CHEB):
                odd = odd + minus[s] * float(ODD_HALF[t, s])
            sums.append((even + odd, even - odd))
        for which, row in enumerate((t,) if t == mid else (t, CHEB - 1 - t)):
            real, imag = sums[0][which] * common, sums[1][which] * common
            cosine, sine = parent_ref[row, 0], parent_ref[row, 1]
            store(row, cosine * real - sine * imag, cosine * imag + sine * real)


def row_of(level, split, column, part):
    return part + 2 * (split * CHEB + column if level % 2 == 0 else column * CHEB + split)


def join_chips(me, arrays, pieces, held, sems, work, last_phases, factors):
    copies = []
    for step, (index, part) in pieces.items():
        spot = pl.ds(((me ^ step) // 2) * PAIRS, PAIRS)
        source = arrays[index].at[pl.ds(part * PAIRS, PAIRS)]
        copies.append(pltpu.make_async_copy(source, held.at[spot], sems.at[step // 2]))
        copies[-1].start()
    for copy in copies:
        copy.wait()
    rows = held.reshape(OCT * ROWS, LANES)

    def received(row):
        return rows[pl.ds(row, OCT, stride=ROWS), :]

    for part in range(4):
        last_phases[part] = received(WEIGHT_ROWS + part * LEVELS + LEVELS - 1)
    for level in range(LEVELS - 1):
        level_factors(level, [received(WEIGHT_ROWS + part * LEVELS + level) for part in range(4)], *factors)
        bit = OCT >> (level + 1)

        def column_step(column, _, level=level, bit=bit):
            upper = (lax.broadcasted_iota(jnp.int32, (OCT, LANES), 0) & bit) != 0
            children = [[], []]
            for s in range(CHEB):
                pairs = [[], []]
                for part in range(2):
                    row = row_of(level, s, column, part)
                    value = received(row) if level == 0 else work[row]
                    down = pltpu.roll(value, bit, 0)
                    up = down if 2 * bit == OCT else pltpu.roll(value, OCT - bit, 0)
                    pairs[0].append(jnp.where(upper, down, value))
                    pairs[1].append(jnp.where(upper, value, up))
                children[0].append(tuple(pairs[0]))
                children[1].append(tuple(pairs[1]))

            def store(row, real, imag):
                work[row_of(level, row, column, 0)] = real
                work[row_of(level, row, column, 1)] = imag

            level_column(column, children, *factors, store)
            return 0

        lax.fori_loop(0, CHEB, column_step, 0, unroll=3)


def even_kernel(pieces, count, me_ref, *refs):
    work, last_phases, held, parent_ref, child_ref, common_ref, sems = refs[count:]
    factors = (parent_ref, child_ref, common_ref)
    join_chips(me_ref[0], refs, pieces, held, sems, work, last_phases, factors)


def odd_kernel(pieces, count, me_ref, even_work, even_phases, *refs):
    out_hbm, work, last_phases, held, out_ref, parent_ref, child_ref, common_ref, sems, out_sems = refs[count:]
    me = me_ref[0]
    own = me % 2
    early = [
        pltpu.make_async_copy(even_work, work.at[own], out_sems.at[0]),
        pltpu.make_async_copy(even_phases, last_phases.at[own], out_sems.at[1]),
    ]
    for copy in early:
        copy.start()
    factors = [ref.at[0] for ref in (parent_ref, child_ref, common_ref)]
    join_chips(me, refs, pieces, held, sems, work.at[1 - own], last_phases.at[1 - own], factors)
    for copy in early:
        copy.wait()

    level = LEVELS - 1
    for parity in range(2):
        level_factors(
            level,
            [last_phases[parity, part] for part in range(4)],
            parent_ref.at[parity],
            child_ref.at[parity],
            common_ref.at[parity],
        )
    chunk = out_ref.shape[0] // CHEB

    def leave(column):
        rows = pl.ds(pl.multiple_of(column * chunk, 8), chunk)
        return pltpu.make_async_copy(out_ref.at[rows, :], out_hbm.at[rows, :], out_sems.at[column])

    def column_step(column, _):
        children = [
            [tuple(work[child, row_of(level, s, column, part)] for part in range(2)) for s in range(CHEB)]
            for child in range(2)
        ]
        for parity in range(2):

            def store(row, real, imag, parity=parity):
                start = row_of(level, row, column, 0) * SLOTS + 2 * parity
                out_ref[pl.ds(start, OCT, stride=4), :] = real
                out_ref[pl.ds(start + 1, OCT, stride=4), :] = imag

            level_column(
                column, children, parent_ref.at[parity], child_ref.at[parity], common_ref.at[parity], store
            )
        leave(column).start()
        return 0

    lax.fori_loop(0, CHEB, column_step, 0, unroll=3)
    for column in range(CHEB):
        leave(column).wait()


def factor_scratch(count):
    return [
        pltpu.VMEM(count + (CHEB, 2, OCT, LANES), jnp.float32),
        pltpu.VMEM(count + (2, CHEB, 2, OCT, LANES), jnp.float32),
        pltpu.VMEM(count + (CHEB, OCT, LANES), jnp.float32),
    ]


def combine_even(me, arrays, pieces):
    vmem = pl.BlockSpec(memory_space=pltpu.VMEM)
    return pl.pallas_call(
        functools.partial(even_kernel, pieces, len(arrays)),
        out_shape=[
            jax.ShapeDtypeStruct((WEIGHT_ROWS, OCT, LANES), jnp.float32),
            jax.ShapeDtypeStruct((4, OCT, LANES), jnp.float32),
        ],
        in_specs=[pl.BlockSpec(memory_space=pltpu.SMEM)] + [pl.BlockSpec(memory_space=pl.ANY)] * len(arrays),
        out_specs=[vmem, vmem],
        scratch_shapes=[
            pltpu.VMEM((OCT * PAIRS, 2, LANES), jnp.float32),
            *factor_scratch(()),
            pltpu.SemaphoreType.DMA((OCT,)),
        ],
        compiler_params=pltpu.CompilerParams(vmem_limit_bytes=16 * 2**20),
        cost_estimate=pl.CostEstimate(flops=40 * 2**20, bytes_accessed=12 * 2**20, transcendentals=0),
        name="combine_even",
    )(me, *arrays)


def combine_odd(me, even, arrays, pieces):
    hbm = pl.BlockSpec(memory_space=pltpu.HBM)
    anywhere = pl.BlockSpec(memory_space=pl.ANY)
    return pl.pallas_call(
        functools.partial(odd_kernel, pieces, len(arrays)),
        out_shape=jax.ShapeDtypeStruct((WEIGHT_ROWS * SLOTS, LANES), jnp.float32),
        in_specs=[pl.BlockSpec(memory_space=pltpu.SMEM)] + [anywhere] * (2 + len(arrays)),
        out_specs=hbm,
        scratch_shapes=[
            pltpu.VMEM((2, WEIGHT_ROWS, OCT, LANES), jnp.float32),
            pltpu.VMEM((2, 4, OCT, LANES), jnp.float32),
            pltpu.VMEM((OCT * PAIRS, 2, LANES), jnp.float32),
            pltpu.VMEM((WEIGHT_ROWS * SLOTS, LANES), jnp.float32),
            *factor_scratch((2,)),
            pltpu.SemaphoreType.DMA((OCT,)),
            pltpu.SemaphoreType.DMA((CHEB,)),
        ],
        compiler_params=pltpu.CompilerParams(vmem_limit_bytes=16 * 2**20),
        cost_estimate=pl.CostEstimate(flops=80 * 2**20, bytes_accessed=20 * 2**20, transcendentals=0),
        name="combine_odd",
    )(me, *even, *arrays)


def on_device(source_weights, wave_vectors, source_centers, phase_coef, phase_kind):
    devices = lax.axis_size("box")
    me = lax.axis_index("box").astype(jnp.int32)[None]
    direct = devices == SLOTS
    if not direct:
        me = jnp.zeros_like(me)
    weights = source_weights.reshape(2, POINTS, SLOTS, LANES).transpose(1, 2, 0, 3)
    weights, *sources = [
        pltpu.with_memory_space_constraint(operand, pltpu.HBM)
        for operand in (weights, phase_coef, wave_vectors, source_centers, phase_kind[None, :])
    ]
    blocks, phases = {}, None
    for messages in PACKS:
        if blocks:
            last = next(reversed(blocks))
            phases, blocks[last] = lax.optimization_barrier((phases, blocks[last]))
        packed, phases = pack(messages, me, weights, phases, sources)
        blocks.update(packed)
    inside = {m[0]: m for messages in PACKS for m in messages}
    if direct:
        pairs = {step for step, message in inside.items() if len(message) > 1}
        for name in SENDS:
            step = name
            if name in ONWARD:
                step = ACROSS_Y
                parts = [blocks[part][PAIRS:] if part in pairs else blocks[part] for part in ONWARD[name]]
                blocks[name] = jnp.concatenate(parts)
                inside[name] = tuple(part ^ ACROSS_Y if part in pairs else part for part in ONWARD[name])
            if name in WAITS:
                earlier = WAITS[name]
                blocks[name], blocks[earlier] = lax.optimization_barrier((blocks[name], blocks[earlier]))
            blocks[name] = lax.ppermute(blocks[name], "box", [(s, s ^ step) for s in range(SLOTS)])
            inside[step] = inside[step] if name in ONWARD else inside[step][:1]
        orders = EVEN_ORDER, ODD_ORDER
    else:
        parts = {step: blocks[m[0]][i * PAIRS : (i + 1) * PAIRS] for m in inside.values() for i, step in enumerate(m)}
        whole = jnp.concatenate([parts[step] for step in range(SLOTS)], axis=2)
        whole = lax.all_to_all(whole, "box", split_axis=2, concat_axis=2, tiled=True)
        blocks = {s: whole[:, :, s * LANES : (s + 1) * LANES] for s in range(SLOTS)}
        inside = {s: (s,) for s in range(SLOTS)}
        orders = range(0, SLOTS, 2), range(1, SLOTS, 2)
    arrays = [[blocks[name] for name in order] for order in orders]
    pieces = [
        {step: (index, part) for index, name in enumerate(order) for part, step in enumerate(inside[name])}
        for order in orders
    ]
    even = combine_even(me, arrays[0], pieces[0])
    rows = combine_odd(me, even, arrays[1], pieces[1])
    return rows.reshape(POINTS, SLOTS, 2, LANES).transpose(2, 0, 1, 3).reshape(2, POINTS, SLOTS * LANES)


def solution(mesh):
    in_specs = (
        P(None, None, ("groups", "box")),
        P(None, None, ("groups", "box")),
        P(None, None, ("groups", "box")),
        P(),
        P(("groups", "box")),
    )
    out_specs = P(None, None, ("groups", "box"))
    return jax.shard_map(on_device, mesh=mesh, in_specs=in_specs, out_specs=out_specs, check_vma=False)
```
